32 devices in a mesh: phi: 16 (over z, y, core), layer: 2 (over x).
Axes of the slice: x: 2, y: 2, z: 4, core: 2. Of those that a mesh axis runs over, the one named last changes fastest.
Arguments:
- node_feats: bfloat16 [64, 1024], P(None, ('phi', 'layer')), may hold values from -6 to 6
- edge_feats: bfloat16 [64, 65536], P(None, ('phi', 'layer')), may hold values from -6 to 6
- edge_source: int32 [65536], P(('phi', 'layer')), may hold values from 0 to 111
- edge_target: int32 [65536], P(('phi', 'layer')), may hold values from 0 to 63
- edge_counts: int32 [16, 2], P('phi', 'layer'), may hold values from 256 to 2048, as said below
- rim_upper: int32 [16, 24], P('phi'), may hold values from 0 to 63, as said below
- rim_lower: int32 [16, 24], P('phi'), may hold values from 0 to 63, as said below
- edge_first: bfloat16 [64, 192], replicated, may hold values from -0.4375 to 0.4375
- edge_second: bfloat16 [64, 64], replicated, may hold values from -0.75 to 0.75
- node_first: bfloat16 [64, 128], replicated, may hold values from -0.1875 to 0.1875
- node_second: bfloat16 [64, 64], replicated, may hold values from -0.75 to 0.75
- biases: float32 [4, 64], replicated, may hold values from -3 to 3
- node_cot: float32 [64, 1024], P(None, ('phi', 'layer')), may hold values from -2 to 2
Outputs:
- node_out: bfloat16 [64, 1024], P(None, ('phi', 'layer'))
- edge_out: bfloat16 [64, 65536], P(None, ('phi', 'layer'))
- node_grad: float32 [64, 1024], P(None, ('phi', 'layer'))
- grad_edge_first: float32 [64, 192], replicated
- grad_edge_second: float32 [64, 64], replicated
- grad_node_first: float32 [64, 128], replicated
- grad_node_second: float32 [64, 64], replicated
- grad_biases: float32 [4, 64], replicated
The draws below stay inside these ranges and needn't reach their ends.
Inputs may be any that keep to these rules, and one draw needn't show every extreme that they name: `edge_source`: columns 0 to 63 are the slab's own hits, the next 24 come from the slab below in phi and the last 24 from the slab above, on a closed loop; slots past the count hold any index. `edge_target`: a hit of the edge's own slab. `edge_counts`: slots of a device at or past this count are padding; some device is full in every draw. `rim_upper`: distinct hits of the slab within each row. `rim_lower`: distinct hits of the slab within each row.
All inputs are finite; a program needn't handle non-finite values.
Results may differ from the reference program's by a relative error of at most 0.02.
Values may be sent and summed in bfloat16 or wider, within the bound.
No kernel may reach another device: no remote copies, remote signals or barrier semaphores. Data moves between devices by JAX's collectives and lax.ppermute only.
A program may use at most 64 MiB of HBM per device.

```python
import jax
import jax.numpy as jnp
from jax import lax

F = 64
HID = 64
E_DEV = 2048
ITERS = 2
SLAB = 64
RIM = 24
EXT = 112
NODES = 1024
EDGES = 65536
N_PHI = 16
N_LAYER = 2


def draw_order(single):
    return jax.random.permutation(single, SLAB).astype(jnp.int32)


def rim_choice(key):
    orders = jax.vmap(draw_order)(jax.random.split(key, N_PHI))
    highest = SLAB - 1
    leading = orders[:, 0:1]
    orders = jnp.where(orders == highest, leading, orders)
    orders = orders.at[:, 0].set(highest)
    second = orders[:, 1:2]
    orders = jnp.where(orders == 0, second, orders)
    orders = orders.at[:, 1].set(0)
    return orders[:, :RIM].astype(jnp.int32)


def draw_rim_upper(key, part):
    key = jax.random.fold_in(key, 21)
    return rim_choice(key)


def draw_rim_lower(key, part):
    key = jax.random.fold_in(key, 22)
    return rim_choice(key)


def draw_edge_counts(key, part):
    key = jax.random.fold_in(key, 11)
    split_one, split_two = jax.random.split(key)
    spread = E_DEV - E_DEV // 8
    drawn = jax.random.randint(split_one, (N_PHI * N_LAYER,), 0, spread + 1)
    counts = E_DEV // 8 + drawn * drawn // spread
    busiest = jax.random.randint(split_two, (), 0, N_PHI * N_LAYER)
    counts = counts.at[busiest].set(E_DEV)
    return counts.reshape(N_PHI, N_LAYER).astype(jnp.int32)


def with_ends(entries, own_key, low, largest):
    index_at = [jax.random.randint(jax.random.fold_in(own_key, axis), (), 0, length) for axis, length in enumerate(entries.shape)]
    main_axis = entries.shape.index(max(entries.shape))
    neighbour = index_at[:main_axis] + [(index_at[main_axis] + 1) % entries.shape[main_axis]] + index_at[main_axis + 1:]
    return entries.at[tuple(index_at)].set(low).at[tuple(neighbour)].set(largest)


def levels(stream_key, dims, pieces, least, high):
    level = 1.0
    for dim, parts in pieces:
        steps = jax.random.uniform(jax.random.fold_in(jax.random.fold_in(stream_key, 6), dim), (parts,), jnp.float32, least / len(pieces), high / len(pieces))
        level = level * jnp.repeat(jnp.exp(steps), dims[dim] // parts).reshape((-1,) + (1,) * (len(dims) - 1 - dim))
    return level


def scatter_about(rng, dims, scale, reach, shards=(), held_as=jnp.bfloat16):
    values = jax.random.normal(rng, dims, jnp.float32) * scale
    if len(shards) > 0:
        values = levels(rng, dims, shards, -0.22, 0.18) * values
    return jnp.clip(values, min=-reach, max=reach).astype(held_as)


def setup_inputs(seed: int = 0) -> dict:
    streams_of = jax.random.split(jax.random.key(seed), 14)
    node_feats = scatter_about(streams_of[0], (F, NODES), 1.0, 6.0, ((1, 32),))
    edge_feats = scatter_about(streams_of[1], (F, EDGES), 1.0, 6.0, ((1, 32),))
    edge_source = with_ends(jax.random.randint(streams_of[2], (EDGES,), 0, EXT), jax.random.fold_in(streams_of[2], 1), 0, EXT - 1).astype(jnp.int32)
    edge_target = with_ends(jax.random.randint(streams_of[3], (EDGES,), 0, SLAB), jax.random.fold_in(streams_of[3], 1), 0, SLAB - 1).astype(jnp.int32)
    edge_counts = draw_edge_counts(jax.random.fold_in(streams_of[13], 71), 0)
    rim_upper = draw_rim_upper(jax.random.fold_in(streams_of[13], 71), 0)
    rim_lower = draw_rim_lower(jax.random.fold_in(streams_of[13], 71), 0)
    edge_first = scatter_about(streams_of[7], (HID, 3 * F), (3 * F) ** -0.5, 0.4375)
    edge_second = scatter_about(streams_of[8], (F, HID), HID ** -0.5, 0.75)
    node_first = scatter_about(streams_of[9], (HID, 2 * F), (16 * F) ** -0.5, 0.1875)
    node_second = scatter_about(streams_of[10], (F, HID), HID ** -0.5, 0.75)
    biases = scatter_about(streams_of[11], (4, HID), 0.5, 3.0, (), jnp.float32)
    node_cot = scatter_about(streams_of[12], (F, NODES), (4 * NODES ** -0.5), 2.0, ((1, 32),), jnp.float32)
    return {"node_feats": node_feats, "edge_feats": edge_feats, "edge_source": edge_source, "edge_target": edge_target, "edge_counts": edge_counts, "rim_upper": rim_upper, "rim_lower": rim_lower, "edge_first": edge_first, "edge_second": edge_second, "node_first": node_first, "node_second": node_second, "biases": biases, "node_cot": node_cot}


def forward_dot(weight, data):
    return jnp.dot(weight, data, preferred_element_type=jnp.float32)


def back_dot(weight, data):
    return lax.dot_general(weight, data, (((0,), (0,)), ((), ())), preferred_element_type=jnp.float32)


def outer_dot(left, right):
    return lax.dot_general(left, right, (((1,), (1,)), ((), ())), preferred_element_type=jnp.float32)


def silu_slope(value):
    logistic = jax.nn.sigmoid(value)
    return logistic * (1.0 + value * (1.0 - logistic))


def pick_columns(table, index):
    return jnp.take(table, index, axis=1)


def place_rims(slab_grad, upper_back, lower_back, upper_index, lower_index):
    return slab_grad.at[:, upper_index].add(upper_back).at[:, lower_index].add(lower_back)


def reference(node_feats, edge_feats, edge_source, edge_target, edge_counts, rim_upper, rim_lower,
              edge_first, edge_second, node_first, node_second, biases, node_cot):
    latent = F
    slab_slots = N_LAYER * E_DEV
    edge_state = edge_feats.reshape(latent, N_PHI, slab_slots).transpose(1, 0, 2)
    source_all = edge_source.reshape(N_PHI, slab_slots)
    target_all = edge_target.reshape(N_PHI, slab_slots)
    position = jnp.arange(slab_slots, dtype=jnp.int32) % E_DEV
    limits = jnp.repeat(edge_counts, E_DEV, axis=1)
    edge_valid = (position[None, :] < limits).astype(jnp.float32)
    bias_edge = biases[0][:, None]
    bias_message = biases[1][:, None]
    bias_node = biases[2][:, None]
    bias_update = biases[3][:, None]

    def extend(node_state):
        slab_nodes = node_state.reshape(latent, N_PHI, SLAB).transpose(1, 0, 2)
        upper_rows = jax.vmap(pick_columns)(slab_nodes, rim_upper)
        lower_rows = jax.vmap(pick_columns)(slab_nodes, rim_lower)
        from_below = jnp.roll(upper_rows, 1, axis=0)
        from_above = jnp.roll(lower_rows, -1, axis=0)
        return slab_nodes, jnp.concatenate([slab_nodes, from_below, from_above], axis=2)

    def edge_inputs(extended, slab_nodes, edges_now, source_p, target_p):
        return jnp.concatenate([jnp.take(extended, source_p, axis=1), jnp.take(slab_nodes, target_p, axis=1),
                                edges_now], axis=0)

    def slab_forward(bundle):
        extended, slab_nodes, edges_now, source_p, target_p, valid_p = bundle
        inputs = edge_inputs(extended, slab_nodes, edges_now, source_p, target_p)
        hidden_pre = forward_dot(edge_first, inputs) + bias_edge
        hidden = jax.nn.silu(hidden_pre).astype(jnp.bfloat16)
        new_edges = (valid_p * (edges_now.astype(jnp.float32) + forward_dot(edge_second, hidden)
                                + bias_message)).astype(jnp.bfloat16)
        messages = jnp.zeros((latent, SLAB), jnp.float32).at[:, target_p].add(new_edges.astype(jnp.float32))
        return new_edges, messages

    node_state = node_feats
    stored = []
    for iteration in range(ITERS):
        slab_nodes, extended = extend(node_state)
        new_edges, messages = lax.map(slab_forward, (extended, slab_nodes, edge_state, source_all, target_all, edge_valid))
        message_cols = messages.transpose(1, 0, 2).reshape(latent, NODES).astype(jnp.bfloat16)
        node_in = jnp.concatenate([node_state, message_cols], axis=0)
        node_pre = forward_dot(node_first, node_in) + bias_node
        node_hidden = jax.nn.silu(node_pre).astype(jnp.bfloat16)
        new_nodes = (node_state.astype(jnp.float32) + forward_dot(node_second, node_hidden)
                     + bias_update).astype(jnp.bfloat16)
        stored.append((slab_nodes, extended, edge_state, node_in, node_pre, node_hidden))
        node_state = new_nodes
        edge_state = new_edges
    node_out = node_state
    edge_out = edge_state.transpose(1, 0, 2).reshape(latent, EDGES)

    def slab_backward(bundle):
        extended, slab_nodes, edges_now, source_p, target_p, valid_p, message_p, grad_edge_p = bundle
        inputs = edge_inputs(extended, slab_nodes, edges_now, source_p, target_p)
        hidden_pre = forward_dot(edge_first, inputs) + bias_edge
        hidden = jax.nn.silu(hidden_pre).astype(jnp.bfloat16)
        edge_grad = valid_p * (grad_edge_p + jnp.take(message_p, target_p, axis=1).astype(jnp.float32))
        edge_low = edge_grad.astype(jnp.bfloat16)
        second_term = outer_dot(edge_low, hidden)
        pre_grad = back_dot(edge_second, edge_low) * silu_slope(hidden_pre)
        pre_low = pre_grad.astype(jnp.bfloat16)
        first_term = outer_dot(pre_low, inputs)
        previous = edge_grad + back_dot(edge_first[:, 2 * latent:], pre_low)
        extended_grad = jnp.zeros((latent, EXT), jnp.float32).at[:, source_p].add(
            back_dot(edge_first[:, :latent], pre_low))
        slab_grad = extended_grad[:, :SLAB].at[:, target_p].add(back_dot(edge_first[:, latent:2 * latent], pre_low))
        return (previous, slab_grad, extended_grad[:, SLAB:SLAB + RIM], extended_grad[:, SLAB + RIM:],
                first_term, second_term, jnp.sum(pre_grad, axis=1), jnp.sum(edge_grad, axis=1))

    grad_nodes = node_cot
    grad_edges = jnp.zeros((N_PHI, latent, slab_slots), jnp.float32)
    sum_first_edge = jnp.zeros(edge_first.shape, jnp.float32)
    sum_second_edge = jnp.zeros(edge_second.shape, jnp.float32)
    sum_first_node = jnp.zeros(node_first.shape, jnp.float32)
    sum_second_node = jnp.zeros(node_second.shape, jnp.float32)
    edge_bias = jnp.zeros((HID,), jnp.float32)
    message_bias = jnp.zeros((F,), jnp.float32)
    node_bias = jnp.zeros((HID,), jnp.float32)
    update_bias = jnp.zeros((F,), jnp.float32)
    for iteration in reversed(range(ITERS)):
        slab_nodes, extended, edges_now, node_in, node_pre, node_hidden = stored[iteration]
        nodes_low = grad_nodes.astype(jnp.bfloat16)
        sum_second_node = sum_second_node + outer_dot(nodes_low, node_hidden)
        update_bias = update_bias + jnp.sum(grad_nodes, axis=1)
        node_pre_grad = back_dot(node_second, nodes_low) * silu_slope(node_pre)
        node_pre_low = node_pre_grad.astype(jnp.bfloat16)
        sum_first_node = sum_first_node + outer_dot(node_pre_low, node_in)
        node_bias = node_bias + jnp.sum(node_pre_grad, axis=1)
        node_in_grad = back_dot(node_first, node_pre_low)
        message_grad = node_in_grad[latent:].astype(jnp.bfloat16)
        message_slabs = message_grad.reshape(latent, N_PHI, SLAB).transpose(1, 0, 2)
        results = lax.map(slab_backward, (extended, slab_nodes, edges_now, source_all, target_all, edge_valid,
                                          message_slabs, grad_edges))
        previous, slab_grad, upper_grad, lower_grad, first_term, second_term, pre_sums, edge_sums = results
        upper_back = jnp.roll(upper_grad, -1, axis=0)
        lower_back = jnp.roll(lower_grad, 1, axis=0)
        slab_grad = jax.vmap(place_rims)(slab_grad, upper_back, lower_back, rim_upper, rim_lower)
        grad_nodes = grad_nodes + node_in_grad[:latent] + slab_grad.transpose(1, 0, 2).reshape(latent, NODES)
        grad_edges = previous
        sum_first_edge = sum_first_edge + jnp.sum(first_term, axis=0)
        sum_second_edge = sum_second_edge + jnp.sum(second_term, axis=0)
        edge_bias = edge_bias + jnp.sum(pre_sums, axis=0)
        message_bias = message_bias + jnp.sum(edge_sums, axis=0)
    grad_biases = jnp.stack([edge_bias, message_bias, node_bias, update_bias])
    return (node_out, edge_out, grad_nodes, sum_first_edge, sum_second_edge, sum_first_node, sum_second_node,
            grad_biases)
```

```python
import functools
import math

import jax
import jax.numpy as jnp
from jax import lax
from jax.experimental import pallas as pl
from jax.experimental.pallas import tpu as pltpu
from jax.sharding import PartitionSpec as P

BF = jnp.bfloat16
F32 = jnp.float32
CHUNK = 512
LANES = 128
HBM = pltpu.HBM
VM = pltpu.VMEM


def mm(left, right):
    return jnp.dot(left, right, preferred_element_type=F32)


def mm_nt(left, right):
    return lax.dot_general(left, right, (((1,), (1,)), ((), ())), preferred_element_type=F32)


def flip(weight):
    return weight.astype(F32).T.astype(BF)


def halves(value):
    high = value.astype(BF)
    return high, (value - high.astype(F32)).astype(BF)


def wide_mm(weight, value):
    high, low = halves(value)
    return mm(jnp.concatenate([weight, weight], axis=1), jnp.concatenate([high, low], axis=0))


def gather_mm(table, onehot):
    high, low = halves(table)
    return mm(jnp.concatenate([high, low], axis=1), jnp.concatenate([onehot, onehot], axis=0))


def sigmoid(value):
    return 0.5 + 0.5 * jnp.tanh(0.5 * value)


def add_to(total, value):
    return value if total is None else total + value


def chunks_of(count):
    return [slice(first, first + CHUNK) for first in range(0, count, CHUNK)]


def is_even():
    return lax.rem(lax.axis_index("phi"), 2) == 0


def pick(parts, natural):
    groups = len(parts)
    turn = lax.rem(lax.axis_index("layer") - natural + groups, groups)
    value = parts[0]
    for rank in range(1, groups):
        value = jnp.where(turn == rank, parts[rank], value)
    return value


def own_rows(slab_rows, width):
    layer = lax.axis_index("layer")
    value = slab_rows[:width]
    for rank in range(1, slab_rows.shape[0] // width):
        value = jnp.where(layer == rank, slab_rows[rank * width : (rank + 1) * width], value)
    return value


def rim_payloads(slab16, upper_ref, lower_ref, alpha_ref, beta_ref):
    upper = mm(slab16, upper_ref[...])
    lower = mm(slab16, lower_ref[...])
    even = is_even()
    alpha_ref[...] = jnp.where(even, upper, lower).astype(BF)
    beta_ref[...] = jnp.where(even, lower, upper).astype(BF)


def rim_columns(alpha, beta, room):
    even = is_even()
    below = jnp.where(even, beta, alpha)
    above = jnp.where(even, alpha, beta)
    pad = jnp.zeros((below.shape[0], room - 2 * below.shape[1]), F32)
    return jnp.concatenate([below, above, pad], axis=1).astype(BF)


def placed_rims(alpha, beta, upper_ref, lower_ref):
    even = is_even()
    from_upper = jnp.where(even, alpha, beta).astype(BF)
    from_lower = jnp.where(even, beta, alpha).astype(BF)
    return mm_nt(from_upper, upper_ref[...]) + mm_nt(from_lower, lower_ref[...])


def rim_gradients(ext_grad, slab, rim):
    even = is_even()
    below = ext_grad[:, slab : slab + rim]
    above = ext_grad[:, slab + rim : slab + 2 * rim]
    return jnp.where(even, above, below), jnp.where(even, below, above)


def slope_parts(pre):
    logistic = sigmoid(pre)
    value = pre * logistic
    return value, logistic + value * (1.0 - logistic)


def activate(base_ref, rim_table, onehot_ref, slab, hidden_ref, slope_ref):
    wide = onehot_ref.shape[0] - slab
    high, low = halves(rim_table)
    table = jnp.concatenate([high, low], axis=1)
    total = None
    for cols in chunks_of(base_ref.shape[1]):
        rims = onehot_ref[slab:wide, cols]
        pre = base_ref[:, cols] + mm(table, jnp.concatenate([rims, rims], axis=0))
        value, slope = slope_parts(pre)
        hidden = value.astype(BF)
        hidden_ref[:, cols] = hidden
        slope_ref[:, cols] = slope
        total = add_to(total, mm_nt(hidden, onehot_ref[wide:, cols]))
    return total


def slab_base(first_ref, slab16, bias, onehot_ref, edges_of, base_ref):
    latent, slab = slab16.shape
    wide = onehot_ref.shape[0] - slab
    source = halves(mm(first_ref[:, :latent], slab16))
    target = halves(mm(first_ref[:, latent : 2 * latent], slab16))
    own = first_ref[:, 2 * latent :]
    table = jnp.concatenate([*source, *target, own], axis=1)
    for cols in chunks_of(base_ref.shape[1]):
        near = onehot_ref[:slab, cols]
        hit = onehot_ref[wide:, cols]
        stack = jnp.concatenate([near, near, hit, hit, edges_of(cols)], axis=0)
        base_ref[:, cols] = mm(table, stack) + bias[:, 0:1]


def node_backward(grad, pre, first_back_ref, second_back_ref):
    latent = grad.shape[0]
    pre_grad = mm(second_back_ref[...], grad.astype(BF)) * slope_parts(pre)[1]
    back = mm(first_back_ref[...], pre_grad.astype(BF))
    return pre_grad, back[:latent], back[latent:].astype(BF)


def node_sums(grad, pre_grad, joined, hidden):
    return (
        mm_nt(pre_grad.astype(BF), joined),
        mm_nt(grad.astype(BF), hidden),
        jnp.sum(pre_grad, axis=1, keepdims=True),
        jnp.sum(grad, axis=1, keepdims=True),
    )


def table_grads(first_back_ref, sums, slab, wide):
    latent = sums.shape[0]
    ext_grad = mm(first_back_ref[:latent], sums[:, :wide].astype(BF))
    target = mm(first_back_ref[latent : 2 * latent], sums[:, wide : wide + slab].astype(BF))
    return ext_grad, ext_grad[:, :slab] + target


def first_total(sums, slab16, rims16, slab, wide):
    source = sums[:, :wide].astype(BF)
    target = sums[:, wide : wide + slab].astype(BF)
    ext16 = jnp.concatenate([slab16, rims16], axis=1)
    return jnp.concatenate(
        [mm_nt(source, ext16), mm_nt(target, slab16), sums[:, wide + slab :]], axis=1
    )


def prep_kernel(count_ref, source_hbm, target_hbm, feats_hbm, cot_hbm, upper_hbm, lower_hbm,
                out_ref, upper_ref, lower_ref,
                source, target, feats, cot, upper, lower, sems):
    pairs = ((source_hbm, source), (target_hbm, target), (feats_hbm, feats), (cot_hbm, cot),
             (upper_hbm, upper), (lower_hbm, lower))
    copies = [pltpu.make_async_copy(a, b, sems.at[place]) for place, (a, b) in enumerate(pairs)]
    for copy in copies:
        copy.start()
    for copy in copies:
        copy.wait()
    rows = source.shape[0]
    position = lax.broadcasted_iota(jnp.int32, (rows, LANES), 0) * LANES + lax.broadcasted_iota(
        jnp.int32, (rows, LANES), 1
    )
    valid = position < count_ref[0, 0]
    index = source[...]
    out_ref[:rows] = jnp.where(valid, index // LANES, -1).astype(F32).astype(BF)
    out_ref[rows : 2 * rows] = (index % LANES).astype(F32).astype(BF)
    out_ref[2 * rows : 3 * rows] = jnp.where(valid, target[...], -1).astype(F32).astype(BF)
    out_ref[3 * rows :] = jnp.concatenate([feats[...].astype(F32), cot[...]], axis=1).astype(BF)
    hits = lax.broadcasted_iota(jnp.int32, upper_ref.shape, 0)
    upper_ref[...] = (hits == upper[...]).astype(F32).astype(BF)
    lower_ref[...] = (hits == lower[...]).astype(F32).astype(BF)


def slab_kernel(groups, rows, *refs):
    packs = [ref[3 * rows :].astype(F32) for ref in refs[:groups]]
    upper_ref, lower_ref, slab_ref, cot_ref, alpha_ref, beta_ref = refs[groups:]
    latent = slab_ref.shape[0]
    both = jnp.concatenate([pick(packs, rank) for rank in range(groups)], axis=0).T
    slab16 = both[:latent].astype(BF)
    slab_ref[...] = slab16
    cot_ref[...] = both[latent:]
    rim_payloads(slab16, upper_ref, lower_ref, alpha_ref, beta_ref)


def onehot_kernel(groups, rows, rim, *refs):
    packs = [ref[: 3 * rows].astype(F32) for ref in refs[:groups]]
    parts = refs[groups : 2 * groups]
    (slab_ref, first_ref, second_ref, node_first_ref, node_second_ref, bias_ref,
     onehot_ref, edges_ref, base_ref, message_ref, count_ref,
     first_back, second_back, node_first_back, node_second_back, bias_out) = refs[2 * groups :]
    latent, slab = slab_ref.shape
    wide = onehot_ref.shape[0] - slab
    first_back[...] = flip(first_ref[...])
    second_back[...] = flip(second_ref[...])
    node_first_back[...] = flip(node_first_ref[...])
    node_second_back[...] = flip(node_second_ref[...])
    bias = bias_ref[...].T
    bias_out[...] = bias
    source_rows = lax.broadcasted_iota(jnp.int32, (wide, LANES), 0).astype(F32)
    target_rows = lax.broadcasted_iota(jnp.int32, (slab, LANES), 0).astype(F32)
    ones_row = source_rows == float(slab + 2 * rim)
    for rank in range(groups):
        pack = pick(packs, rank)
        source = jnp.where(pack[:rows] < 0.0, -1.0, pack[:rows] * LANES + pack[rows : 2 * rows])
        target = pack[2 * rows :]
        for row in range(rows):
            cols = slice((rank * rows + row) * LANES, (rank * rows + row + 1) * LANES)
            match = (source_rows == source[row : row + 1]) | ones_row
            onehot_ref[:wide, cols] = jnp.where(match, 1.0, 0.0).astype(BF)
            onehot_ref[wide:, cols] = jnp.where(target_rows == target[row : row + 1], 1.0, 0.0).astype(BF)
        for cols in chunks_of(parts[0].shape[1]):
            first = rank * rows * LANES + cols.start
            edges_ref[:, first : first + CHUNK] = pick([part[:, cols] for part in parts], rank)
    message = None
    count = None
    for cols in chunks_of(edges_ref.shape[1]):
        hit = onehot_ref[wide:, cols]
        message = add_to(message, mm_nt(edges_ref[:, cols], hit))
        count = add_to(count, mm_nt(jnp.ones((16, CHUNK), BF), hit))
    message_ref[...] = message
    count_ref[...] = count[:8]
    slab_base(first_ref, slab_ref[...], bias, onehot_ref, lambda cols: edges_ref[:, cols], base_ref)


def forward_kernel(base_ref, onehot_ref, slab_ref, alpha_in, beta_in, message_in, count_ref,
                   first_ref, second_ref, node_first_ref, node_second_ref, bias_ref, upper_ref, lower_ref,
                   hidden_ref, slope_ref, rims_ref, sums_ref, message_ref, joined_ref, node_pre_ref,
                   node_hidden_ref, state_ref, alpha_ref, beta_ref):
    latent, slab = slab_ref.shape
    wide = onehot_ref.shape[0] - slab
    rims16 = rim_columns(alpha_in[...].astype(F32), beta_in[...].astype(F32), wide - slab)
    rims_ref[...] = rims16
    sums = activate(
        base_ref, mm(first_ref[:, :latent], rims16), onehot_ref, slab, hidden_ref, slope_ref
    )
    sums_ref[...] = sums
    bias = bias_ref[...]
    message = message_in[...] + wide_mm(second_ref[...], sums) + bias[:, 1:2] * count_ref[0:1]
    message_ref[...] = message
    slab16 = slab_ref[...]
    joined = jnp.concatenate([slab16, message.astype(BF)], axis=0)
    joined_ref[...] = joined
    node_pre = mm(node_first_ref[...], joined) + bias[:, 2:3]
    node_pre_ref[...] = node_pre
    node_hidden = slope_parts(node_pre)[0].astype(BF)
    node_hidden_ref[...] = node_hidden
    state = (slab16.astype(F32) + mm(node_second_ref[...], node_hidden) + bias[:, 3:4]).astype(BF)
    state_ref[...] = state
    rim_payloads(state, upper_ref, lower_ref, alpha_ref, beta_ref)


def between_kernel(edges_ref, hidden_ref, onehot_ref, slab_ref, first_ref, second_ref, bias_ref,
                   new_ref, base_ref):
    bias = bias_ref[...]
    second = second_ref[...]
    for cols in chunks_of(edges_ref.shape[1]):
        new_ref[:, cols] = (
            edges_ref[:, cols].astype(F32) + mm(second, hidden_ref[:, cols]) + bias[:, 1:2]
        ).astype(BF)
    slab_base(first_ref, slab_ref[...], bias, onehot_ref, lambda cols: new_ref[:, cols], base_ref)


def edge_gradient(gm_total, extra_ref, slope_ref, onehot_ref, edges_ref, second_back, low_ref):
    slab = gm_total.shape[1]
    wide = onehot_ref.shape[0] - slab
    high, low = halves(wide_mm(second_back[...], gm_total))
    table = jnp.concatenate([high, low], axis=1)
    total = None
    for cols in chunks_of(edges_ref.shape[1]):
        hit = onehot_ref[wide:, cols]
        grad = mm(table, jnp.concatenate([hit, hit], axis=0))
        if extra_ref is not None:
            grad = grad + extra_ref[:, cols]
        pre_low = (grad * slope_ref[:, cols]).astype(BF)
        if low_ref is not None:
            low_ref[:, cols] = pre_low
        total = add_to(
            total, mm_nt(pre_low, jnp.concatenate([onehot_ref[:, cols], edges_ref[:, cols]], axis=0))
        )
    return total


def middle_kernel(base_ref, onehot_ref, edges_ref, slab_ref, alpha_in, beta_in, message_in, count_ref, cot_ref,
                  first_ref, second_ref, node_first_ref, bias_ref, first_back, second_back,
                  node_first_back, node_second_back,
                  hidden_ref, low_ref, rims_ref, sums_ref, joined_ref, node_pre_ref, node_grad_ref, gm_ref,
                  first_sums_ref, back_ref, alpha_ref, beta_ref, slope_ref):
    latent, slab = slab_ref.shape
    wide = onehot_ref.shape[0] - slab
    rims16 = rim_columns(alpha_in[...].astype(F32), beta_in[...].astype(F32), wide - slab)
    rims_ref[...] = rims16
    sums = activate(
        base_ref, mm(first_ref[:, :latent], rims16), onehot_ref, slab, hidden_ref, slope_ref
    )
    sums_ref[...] = sums
    bias = bias_ref[...]
    message = message_in[...] + wide_mm(second_ref[...], sums) + bias[:, 1:2] * count_ref[0:1]
    joined = jnp.concatenate([slab_ref[...], message.astype(BF)], axis=0)
    joined_ref[...] = joined
    node_pre = mm(node_first_ref[...], joined) + bias[:, 2:3]
    node_pre_ref[...] = node_pre
    cot = cot_ref[...]
    pre_grad, through, gm = node_backward(cot, node_pre, node_first_back, node_second_back)
    node_grad_ref[...] = pre_grad
    gm_ref[...] = gm
    first_sums = edge_gradient(
        gm.astype(F32), None, slope_ref, onehot_ref, edges_ref, second_back, low_ref
    )
    first_sums_ref[...] = first_sums
    ext_grad, slab_grad = table_grads(first_back, first_sums, slab, wide)
    back_ref[...] = cot + through + slab_grad
    alpha, beta = rim_gradients(ext_grad, slab, alpha_ref.shape[1])
    alpha_ref[...] = alpha.astype(BF)
    beta_ref[...] = beta.astype(BF)


def carry_kernel(rim, low_ref, hidden_zero_ref, hidden_ref, edges_ref, slab_ref, rims_ref, sums_ref, sums_zero_ref,
                 joined_ref, node_pre_ref, node_grad_ref, gm_ref, first_sums_ref, count_ref, cot_ref,
                 first_back, second_back,
                 extra_ref, total_ref):
    latent, slab = slab_ref.shape
    wide = slab + rims_ref.shape[1]
    self_back = first_back[2 * latent :]
    back = second_back[...]
    cross = None
    for cols in chunks_of(low_ref.shape[1]):
        low = low_ref[:, cols]
        extra_ref[:, cols] = mm(back, mm(self_back, low).astype(BF))
        cross = add_to(cross, mm_nt(low, hidden_zero_ref[:, cols]))
    sums = first_sums_ref[...]
    pre_sum = sums[:, slab + 2 * rim : slab + 2 * rim + 1]
    gm = gm_ref[...]
    edge_two = (
        mm_nt(gm, sums_ref[...].astype(BF))
        + mm_nt(gm, sums_zero_ref[...].astype(BF))
        + mm(self_back, cross.astype(BF))
    )
    gm_sum = 2.0 * jnp.sum(gm.astype(F32) * count_ref[0:1], axis=1, keepdims=True) + wide_mm(
        self_back, jnp.broadcast_to(pre_sum, (latent, LANES))
    )[:, :1]
    cot = cot_ref[...]
    node_pre = node_pre_ref[...]
    node_one, node_two, node_pre_sum, cot_sum = node_sums(
        cot, node_grad_ref[...], joined_ref[...], slope_parts(node_pre)[0].astype(BF)
    )
    edge_one = first_total(sums, slab_ref[...], rims_ref[...], slab, wide)
    used = edge_one.shape[1] + edge_two.shape[1] + node_one.shape[1] + node_two.shape[1]
    pad = jnp.zeros((latent, total_ref.shape[1] - used - 4), F32)
    total_ref[...] = jnp.concatenate(
        [edge_one, edge_two, node_one, node_two, pre_sum, gm_sum, node_pre_sum, cot_sum, pad], axis=1
    )


def output_kernel(count_ref, edges_ref, hidden_ref, joined_ref, node_pre_ref, second_ref, node_second_ref, bias_ref,
                  edge_out, node_out, new_ref):
    bias = bias_ref[...]
    latent = edges_ref.shape[0]
    second = second_ref[...]
    for cols in chunks_of(edges_ref.shape[1]):
        new_ref[:, cols] = (
            edges_ref[:, cols].astype(F32) + mm(second, hidden_ref[:, cols]) + bias[:, 1:2]
        ).astype(BF)
    slots = edge_out.shape[1]
    begin = lax.axis_index("layer") * slots
    for cols in chunks_of(slots):
        position = lax.broadcasted_iota(jnp.int32, (latent, CHUNK), 1) + cols.start
        mine = new_ref[:, pl.ds(pl.multiple_of(begin + cols.start, CHUNK), CHUNK)].astype(F32)
        edge_out[:, cols] = jnp.where(position < count_ref[0, 0], mine, 0.0).astype(BF)
    node_hidden = slope_parts(node_pre_ref[...])[0].astype(BF)
    state = joined_ref[:latent].astype(F32) + mm(node_second_ref[...], node_hidden) + bias[:, 3:4]
    node_out[...] = own_rows(state.T, node_out.shape[0]).astype(BF)


def last_kernel(back_in, alpha_grad, beta_grad, upper_ref, lower_ref, joined_ref, node_pre_ref, node_hidden_ref,
                gm_in, sums_ref, count_ref, extra_ref, slope_ref, onehot_ref, edges_ref, slab_ref, rims_ref,
                total_in, first_back, second_back, node_first_back, node_second_back,
                total_ref, back_ref):
    latent, slab = slab_ref.shape
    wide = onehot_ref.shape[0] - slab
    rim = alpha_grad.shape[1]
    grad = back_in[...] + placed_rims(
        alpha_grad[...].astype(F32), beta_grad[...].astype(F32), upper_ref, lower_ref
    )
    pre_grad, through, gm = node_backward(grad, node_pre_ref[...], node_first_back, node_second_back)
    gm_wide = gm.astype(F32) + gm_in[...].astype(F32)
    sums = edge_gradient(gm_wide, extra_ref, slope_ref, onehot_ref, edges_ref, second_back, None)
    ext_grad, slab_grad = table_grads(first_back, sums, slab, wide)
    back_ref[...] = grad + through + slab_grad
    alpha, beta = rim_gradients(ext_grad, slab, rim)
    node_one, node_two, node_pre_sum, grad_sum = node_sums(grad, pre_grad, joined_ref[...], node_hidden_ref[...])
    edge_one = first_total(sums, slab_ref[...], rims_ref[...], slab, wide)
    edge_two = mm_nt(gm, sums_ref[...].astype(BF))
    pre_sum = sums[:, slab + 2 * rim : slab + 2 * rim + 1]
    gm_sum = jnp.sum(gm.astype(F32) * count_ref[0:1], axis=1, keepdims=True)
    used = edge_one.shape[1] + edge_two.shape[1] + node_one.shape[1] + node_two.shape[1]
    pad = jnp.zeros((latent, total_ref.shape[1] - used - 4 - 2 * rim), F32)
    total_ref[...] = (
        total_in[...]
        + jnp.concatenate(
            [edge_one, edge_two, node_one, node_two, pre_sum, gm_sum, node_pre_sum, grad_sum, alpha, beta, pad],
            axis=1,
        )
    ).astype(BF)


def add_kernel(used, rim, bit, mine_ref, other_ref, out_ref):
    mine = mine_ref[...].astype(F32)
    other = other_ref[...].astype(F32)
    lane = lax.broadcasted_iota(jnp.int32, mine.shape, 1)
    held = other[:, used + rim : used + 2 * rim]
    if bit == 1:
        arrived = jnp.zeros_like(held)
        passing = held
    else:
        place = lax.axis_index("phi")
        home = (lax.rem(place // bit, 2) == 1) == (lax.rem(place, 2) == 0)
        arrived = mine[:, used : used + rim] + jnp.where(home, held, 0.0)
        passing = jnp.where(home, 0.0, held)
    pad = jnp.zeros((mine.shape[0], mine.shape[1] - used - 2 * rim), F32)
    out_ref[...] = jnp.concatenate(
        [(mine + other)[:, :used], arrived, passing, pad], axis=1
    ).astype(BF)


def finish_kernel(used, rim, mine_ref, other_ref, back_ref, alpha_in, upper_ref, lower_ref,
                  node_grad, edge_one, edge_two, node_one, node_two, bias_out):
    mine = mine_ref[...].astype(F32)
    other = other_ref[...].astype(F32)
    total = mine + other
    cut = 0
    for ref in (edge_one, edge_two, node_one, node_two):
        ref[...] = total[:, cut : cut + ref.shape[1]]
        cut += ref.shape[1]
    block = used - 4 - (used - 4) % LANES
    turned = total[:, block : block + LANES].T
    bias_out[...] = turned[used - 4 - block : used - block]
    alpha = alpha_in[...].astype(F32)[:, used : used + rim]
    beta = mine[:, used : used + rim] + other[:, used + rim : used + 2 * rim]
    grad = back_ref[...] + placed_rims(alpha, beta, upper_ref, lower_ref)
    node_grad[...] = own_rows(grad.T, node_grad.shape[0])


def call(kernel, outs, *args, scratch=(), smem=0, hbm=(), cost=1.0):
    args = [
        pltpu.with_memory_space_constraint(arg, HBM) if place in hbm else arg for place, arg in enumerate(args)
    ]
    held = [(arg.shape, arg.dtype) for arg in args] + list(outs)
    held += [(ref.shape, ref.dtype) for ref in scratch if jnp.issubdtype(ref.dtype, jnp.number)]
    room = sum(math.prod(shape) * jnp.dtype(kind).itemsize for shape, kind in held)
    spaces = [pltpu.SMEM if place < smem else HBM if place in hbm else VM for place in range(len(args))]
    specs = [pl.BlockSpec(memory_space=space) for space in spaces]
    return pl.pallas_call(
        kernel,
        out_shape=[jax.ShapeDtypeStruct(shape, kind) for shape, kind in outs],
        in_specs=specs,
        out_specs=[pl.BlockSpec(memory_space=VM) for _ in outs],
        scratch_shapes=list(scratch),
        compiler_params=pltpu.CompilerParams(vmem_limit_bytes=room + 10 * 1024 * 1024),
        cost_estimate=pl.CostEstimate(
            flops=int(cost * 1e9), bytes_accessed=int(cost * 3.6e6), transcendentals=0
        ),
    )(*args)


def swap(value, axis, pairing):
    count = lax.axis_size(axis)
    return lax.ppermute(value, axis, [(source, pairing(source) % count) for source in range(count)])


def by_alpha(value):
    return swap(value, "phi", lambda index: index ^ 1)


def by_beta(value):
    return swap(value, "phi", lambda index: index - 1 if index % 2 == 0 else index + 1)


def layer_parts(value):
    groups = lax.axis_size("layer")
    return [value] + [
        swap(value, "layer", lambda index, turn=turn: index + turn) for turn in range(1, groups)
    ]


def body(node_feats, edge_feats, edge_source, edge_target, edge_counts, rim_upper, rim_lower,
         edge_first, edge_second, node_first, node_second, biases, node_cot):
    groups = lax.axis_size("layer")
    ring = lax.axis_size("phi")
    latent, width = node_feats.shape
    hidden = edge_second.shape[1]
    slots = edge_feats.shape[1]
    slab = width * groups
    rim = rim_upper.shape[1]
    wide = (slab + 2 * rim) // LANES * LANES + LANES
    total_slots = slots * groups
    rows = slots // LANES
    rim_shape = ((latent, rim), BF)
    per_slot = lambda kind: ((latent, total_slots), kind)
    per_hit = lambda kind, depth=1: ((depth * latent, slab), kind)

    packed, upper, lower = call(
        prep_kernel, [((3 * rows + width, LANES), BF), ((slab, rim), BF), ((slab, rim), BF)],
        edge_counts, edge_source.reshape(rows, LANES), edge_target.reshape(rows, LANES),
        node_feats.T, node_cot.T, rim_upper, rim_lower,
        scratch=[VM((rows, LANES), jnp.int32), VM((rows, LANES), jnp.int32),
                 VM((width, latent), BF), VM((width, latent), F32), VM((1, rim), jnp.int32),
                 VM((1, rim), jnp.int32), pltpu.SemaphoreType.DMA((6,))],
        smem=1, hbm=range(1, 7),
    )
    packs = layer_parts(packed)
    parts = layer_parts(edge_feats)
    slab_zero, cot, alpha, beta = call(
        functools.partial(slab_kernel, groups, rows),
        [per_hit(BF), per_hit(F32), rim_shape, rim_shape], *packs, upper, lower, cost=0.3,
    )
    alpha = by_alpha(alpha)
    beta = by_beta(beta)
    (onehot, edges_zero, base, message, count, first_back, second_back, node_first_back, node_second_back,
     bias) = call(
        functools.partial(onehot_kernel, groups, rows, rim),
        [((wide + slab, total_slots), BF), per_slot(BF), per_slot(F32), per_hit(F32), ((8, slab), F32),
         (edge_first.shape[::-1], BF), (edge_second.shape[::-1], BF), (node_first.shape[::-1], BF),
         (node_second.shape[::-1], BF), (biases.shape[::-1], F32)],
        *packs, *parts, slab_zero, edge_first, edge_second, node_first, node_second, biases, cost=2.0,
    )
    (hidden_zero, slope, rims_zero, sums_zero, message, joined_zero, node_pre_zero, node_hidden_zero, slab_one,
     alpha, beta) = call(
        forward_kernel,
        [per_slot(BF), per_slot(F32), ((latent, wide - slab), BF), per_hit(F32), per_hit(F32), per_hit(BF, 2),
         per_hit(F32), per_hit(BF), per_hit(BF), rim_shape, rim_shape],
        base, onehot, slab_zero, alpha, beta, message, count, edge_first, edge_second, node_first, node_second,
        bias, upper, lower, cost=2.0,
    )
    alpha = by_alpha(alpha)
    beta = by_beta(beta)
    edges_one, base = call(
        between_kernel, [per_slot(BF), per_slot(F32)],
        edges_zero, hidden_zero, onehot, slab_one, edge_first, edge_second, bias, cost=2.0,
    )
    total_width = edge_first.shape[1] + hidden + node_first.shape[1] + node_second.shape[1] + 4
    lanes = -(-(total_width + 2 * rim) // LANES) * LANES
    (hidden_one, low, rims_one, sums_one, joined_one, node_pre_one, node_grad_one, gm, first_sums, back,
     alpha, beta) = call(
        middle_kernel,
        [per_slot(BF), per_slot(BF), ((latent, wide - slab), BF), per_hit(F32), per_hit(BF, 2), per_hit(F32),
         per_hit(F32), per_hit(BF), ((hidden, wide + slab + latent), F32), per_hit(F32), rim_shape, rim_shape],
        base, onehot, edges_one, slab_one, alpha, beta, message, count, cot, edge_first, edge_second, node_first,
        bias, first_back, second_back, node_first_back, node_second_back,
        scratch=[VM((hidden, total_slots), F32)], cost=3.0,
    )
    alpha = by_alpha(alpha)
    beta = by_beta(beta)
    extra, total = call(
        functools.partial(carry_kernel, rim), [per_slot(F32), ((latent, lanes), F32)],
        low, hidden_zero, hidden_one, edges_one, slab_one, rims_one, sums_one, sums_zero, joined_one, node_pre_one,
        node_grad_one, gm, first_sums, count, cot, first_back, second_back, cost=2.0,
    )
    edge_out, node_out = call(
        output_kernel, [((latent, slots), BF), ((width, latent), BF)],
        edge_counts, edges_one, hidden_one, joined_one, node_pre_one, edge_second, node_second, bias,
        scratch=[VM((latent, total_slots), BF)], smem=1, cost=2.0,
    )
    total, back = call(
        last_kernel, [((latent, lanes), BF), per_hit(F32)],
        back, alpha, beta, upper, lower, joined_zero, node_pre_zero, node_hidden_zero, gm, sums_zero, count, extra,
        slope, onehot, edges_zero, slab_zero, rims_zero, total, first_back, second_back, node_first_back,
        node_second_back, cost=2.0,
    )
    other = by_alpha(total)
    alpha_last = other
    bit = 1
    while 2 * bit < ring:
        total = call(
            functools.partial(add_kernel, total_width, rim, bit), [((latent, lanes), BF)], total, other, cost=0.1,
        )[0]
        bit *= 2
        other = swap(total, "phi", lambda index, bit=bit: index ^ bit)
    node_grad, edge_one, edge_two, node_one, node_two, bias_out = call(
        functools.partial(finish_kernel, total_width, rim),
        [((width, latent), F32), (edge_first.shape, F32), (edge_second.shape, F32),
         (node_first.shape, F32), (node_second.shape, F32), (biases.shape, F32)],
        total, other, back, alpha_last, upper, lower,
    )
    return node_out.T, edge_out, node_grad.T, edge_one, edge_two, node_one, node_two, bias_out


def solution(mesh):
    split = P(None, ("phi", "layer"))
    return jax.shard_map(
        body,
        mesh=mesh,
        in_specs=(split, split, P(("phi", "layer")), P(("phi", "layer")), P("phi", "layer"),
                  P("phi", None), P("phi", None), P(), P(), P(), P(), P(), split),
        out_specs=(split, split, split, P(), P(), P(), P(), P()),
        check_vma=False,
    )
```

```python
import functools
import math

import jax
import jax.numpy as jnp
from jax import lax
from jax.experimental import pallas as pl
from jax.experimental.pallas import tpu as pltpu
from jax.sharding import PartitionSpec as P

BF = jnp.bfloat16
F32 = jnp.float32
CHUNK = 512
LANES = 128
HBM = pltpu.HBM
VM = pltpu.VMEM


def mm(left, right):
    return jnp.dot(left, right, preferred_element_type=F32)


def mm_nt(left, right):
    return lax.dot_general(left, right, (((1,), (1,)), ((), ())), preferred_element_type=F32)


def flip(weight):
    return weight.astype(F32).T.astype(BF)


def halves(value):
    high = value.astype(BF)
    return high, (value - high.astype(F32)).astype(BF)


def wide_mm(weight, value):
    high, low = halves(value)
    return mm(jnp.concatenate([weight, weight], axis=1), jnp.concatenate([high, low], axis=0))


def sigmoid(value):
    return 0.5 + 0.5 * jnp.tanh(0.5 * value)


def add_to(total, value):
    return value if total is None else total + value


def chunks_of(count):
    return [slice(first, first + CHUNK) for first in range(0, count, CHUNK)]


def is_even():
    return lax.rem(lax.axis_index("phi"), 2) == 0


def pick(parts, natural):
    groups = len(parts)
    turn = lax.rem(lax.axis_index("layer") - natural + groups, groups)
    value = parts[0]
    for rank in range(1, groups):
        value = jnp.where(turn == rank, parts[rank], value)
    return value


def own_rows(slab_rows, width):
    layer = lax.axis_index("layer")
    value = slab_rows[:width]
    for rank in range(1, slab_rows.shape[0] // width):
        value = jnp.where(layer == rank, slab_rows[rank * width : (rank + 1) * width], value)
    return value


def split(value):
    high, low = halves(value)
    return jnp.concatenate([high, high, low], axis=1)


def split_mm(table, value):
    high, low = halves(value)
    return mm(table, jnp.concatenate([high, low, high], axis=0))


def pair_mm(table, value):
    return mm(table[:, value.shape[0] :], jnp.concatenate([value, value], axis=0))


def placed_rims(alpha, beta, upper_ref, lower_ref):
    even = is_even()
    from_upper = jnp.where(even, alpha, beta).astype(BF)
    from_lower = jnp.where(even, beta, alpha).astype(BF)
    return mm_nt(from_upper, upper_ref[...]) + mm_nt(from_lower, lower_ref[...])


def rim_gradients(ext_grad, slab, rim):
    even = is_even()
    below = ext_grad[:, slab : slab + rim]
    above = ext_grad[:, slab + rim : slab + 2 * rim]
    return jnp.where(even, above, below), jnp.where(even, below, above)


def slope_parts(pre):
    logistic = sigmoid(pre)
    value = pre * logistic
    return value, logistic + value * (1.0 - logistic)


def activate(base_ref, table, onehot_ref, slab, hidden_ref, slope_ref):
    wide = onehot_ref.shape[0] - slab
    total = None
    for cols in chunks_of(base_ref.shape[1]):
        rims = onehot_ref[slab:wide, cols]
        pre = base_ref[:, cols] + mm(table, jnp.concatenate([rims, rims], axis=0))
        value, slope = slope_parts(pre)
        hidden = value.astype(BF)
        hidden_ref[:, cols] = hidden
        slope_ref[:, cols] = slope
        total = add_to(total, mm_nt(hidden, onehot_ref[wide:, cols]))
    return total


def slab_base(source, target, own, bias, onehot_ref, edges_ref, base_ref):
    slab = source.shape[1]
    wide = onehot_ref.shape[0] - slab
    table = jnp.concatenate([*halves(source), *halves(target), own], axis=1)
    for cols in chunks_of(base_ref.shape[1]):
        near = onehot_ref[:slab, cols]
        hit = onehot_ref[wide:, cols]
        stack = jnp.concatenate([near, near, hit, hit, edges_ref[:, cols]], axis=0)
        base_ref[:, cols] = mm(table, stack) + bias[:, 0:1]


def node_base(state16, message, first_ref, bias):
    latent = state16.shape[0]
    return (
        mm(first_ref[:, :latent], state16)
        + wide_mm(first_ref[:, latent:], message)
        + bias[:, 2:3]
    )


def node_sums(grad, pre_grad, joined, hidden):
    return (
        mm_nt(pre_grad.astype(BF), joined),
        mm_nt(grad.astype(BF), hidden),
        jnp.sum(pre_grad, axis=1, keepdims=True),
        jnp.sum(grad, axis=1, keepdims=True),
    )


def prep_kernel(count_ref, source_hbm, target_hbm, feats_hbm, cot_hbm, upper_hbm, lower_hbm,
                out_ref, upper_ref, lower_ref, source, target, feats, cot, sems):
    pairs = ((source_hbm, source), (target_hbm, target), (feats_hbm, feats), (cot_hbm, cot),
             (upper_hbm, upper_ref), (lower_hbm, lower_ref))
    copies = [pltpu.make_async_copy(a, b, sems.at[place]) for place, (a, b) in enumerate(pairs)]
    for copy in copies:
        copy.start()
    for copy in copies:
        copy.wait()
    rows = source.shape[0]
    position = lax.broadcasted_iota(jnp.int32, (rows, LANES), 0) * LANES + lax.broadcasted_iota(
        jnp.int32, (rows, LANES), 1
    )
    valid = position < count_ref[0, 0]
    index = source[...]
    out_ref[:rows] = jnp.where(valid, index // LANES, -1).astype(F32).astype(BF)
    out_ref[rows : 2 * rows] = (index % LANES).astype(F32).astype(BF)
    out_ref[2 * rows : 3 * rows] = jnp.where(valid, target[...], -1).astype(F32).astype(BF)
    out_ref[3 * rows :] = jnp.concatenate([feats[...].astype(F32), cot[...]], axis=1).astype(BF)


def pick_kernel(packed_ref, upper, lower, upper_ref, lower_ref, alpha_pick, beta_pick):
    hits = lax.broadcasted_iota(jnp.int32, upper_ref.shape, 0)
    upper_ref[...] = (hits == upper[...]).astype(F32).astype(BF)
    lower_ref[...] = (hits == lower[...]).astype(F32).astype(BF)
    slab, room = alpha_pick.shape
    rim = upper.shape[1]
    first = jnp.concatenate([upper[...], jnp.full((1, room - rim), -1, jnp.int32)], axis=1)
    second = jnp.concatenate(
        [jnp.full((1, rim), -1, jnp.int32), lower[...], jnp.full((1, room - 2 * rim), -1, jnp.int32)], axis=1
    )
    even = is_even()
    hits = lax.broadcasted_iota(jnp.int32, (slab, room), 0)
    alpha_pick[...] = (hits == jnp.where(even, first, second)).astype(F32).astype(BF)
    beta_pick[...] = (hits == jnp.where(even, second, first)).astype(F32).astype(BF)


def slab_kernel(groups, rows, *refs):
    packs = [ref[3 * rows :].astype(F32) for ref in refs[:groups]]
    alpha_pick, beta_pick, slab_ref, cot_ref, alpha_ref, beta_ref = refs[groups:]
    latent = slab_ref.shape[0]
    both = jnp.concatenate([pick(packs, rank) for rank in range(groups)], axis=0).T
    slab16 = both[:latent].astype(BF)
    slab_ref[...] = slab16
    cot_ref[...] = both[latent:]
    alpha_ref[...] = mm(slab16, alpha_pick[...]).astype(BF)
    beta_ref[...] = mm(slab16, beta_pick[...]).astype(BF)


def onehot_kernel(groups, rows, rim, *refs):
    packs = [ref[: 3 * rows].astype(F32) for ref in refs[:groups]]
    (first_ref, second_ref, node_first_ref, node_second_ref, bias_ref, alpha_pick, beta_pick,
     onehot_ref, first_back, second_back, node_first_back, node_second_back, bias_out,
     to_node, to_node_back, to_table, to_table_back, to_hidden, alpha_place, beta_place) = refs[groups:]
    latent = first_ref.shape[0]
    slab, room = alpha_pick.shape
    wide = slab + room
    source_rows = lax.broadcasted_iota(jnp.int32, (wide, LANES), 0).astype(F32)
    target_rows = lax.broadcasted_iota(jnp.int32, (slab, LANES), 0).astype(F32)
    ones_row = source_rows == float(slab + 2 * rim)
    for rank in range(groups):
        pack = pick(packs, rank)
        source = jnp.where(pack[:rows] < 0.0, -1.0, pack[:rows] * LANES + pack[rows : 2 * rows])
        target = pack[2 * rows :]
        for row in range(rows):
            cols = slice((rank * rows + row) * LANES, (rank * rows + row + 1) * LANES)
            match = (source_rows == source[row : row + 1]) | ones_row
            onehot_ref[:wide, cols] = jnp.where(match, 1.0, 0.0).astype(BF)
            onehot_ref[wide:, cols] = jnp.where(target_rows == target[row : row + 1], 1.0, 0.0).astype(BF)
    first_back[...] = flip(first_ref[...])
    second_back[...] = flip(second_ref[...])
    node_first_back[...] = flip(node_first_ref[...])
    node_second_back[...] = flip(node_second_ref[...])
    bias_out[...] = bias_ref[...].T
    forward = mm(node_first_ref[:, latent:], second_ref[...])
    to_node[...] = split(forward)
    to_node_back[...] = split(forward.T)
    table = mm(first_ref[:, :latent], node_second_ref[...])
    to_table[...] = split(table)
    to_table_back[...] = split(table.T)
    to_hidden[...] = split(mm(first_ref[:, 2 * latent :], second_ref[...]).T)
    for choose, place in ((alpha_pick, alpha_place), (beta_pick, beta_place)):
        block = choose[...].astype(F32)
        none = jnp.zeros_like(block)
        place[...] = jnp.concatenate(
            [jnp.concatenate([block, none], axis=1), jnp.concatenate([none, block], axis=1)], axis=0
        ).astype(BF)


def start_kernel(groups, *refs):
    parts = refs[:groups]
    (onehot_ref, slab_ref, first_ref, node_first_ref, bias_ref,
     edges_ref, base_ref, message_ref, count_ref, node_base_ref, table_ref) = refs[groups:]
    latent, slab = slab_ref.shape
    wide = onehot_ref.shape[0] - slab
    slots = parts[0].shape[1]
    message = None
    count = None
    for rank in range(groups):
        for cols in chunks_of(slots):
            here = slice(rank * slots + cols.start, rank * slots + cols.stop)
            edges = pick([part[:, cols] for part in parts], rank)
            edges_ref[:, here] = edges
            hit = onehot_ref[wide:, here]
            message = add_to(message, mm_nt(edges, hit))
            count = add_to(count, mm_nt(jnp.ones((16, CHUNK), BF), hit))
    bias = bias_ref[...]
    count_ref[...] = count[:8]
    message = message + bias[:, 1:2] * count[0:1]
    message_ref[...] = message
    slab16 = slab_ref[...]
    source = mm(first_ref[:, :latent], slab16)
    target = mm(first_ref[:, latent : 2 * latent], slab16)
    slab_base(source, target, first_ref[:, 2 * latent :], bias, onehot_ref, edges_ref, base_ref)
    node_base_ref[...] = node_base(slab16, message, node_first_ref, bias)
    shift = wide_mm(first_ref[:, :latent], jnp.broadcast_to(bias[:, 3:4], (latent, LANES)))
    table_ref[...] = source + shift[:, :1]


def forward_kernel(base_ref, onehot_ref, slab_ref, beta_in, alpha_in, node_base_ref, table_in,
                   first_ref, node_second_ref, bias_ref, to_node, to_table, alpha_place, beta_place,
                   hidden_ref, slope_ref, rims_ref, sums_ref, node_pre_ref, node_hidden_ref, state_ref, table_ref,
                   alpha_ref, beta_ref):
    latent, slab = slab_ref.shape
    rims16 = alpha_in[...] + beta_in[...]
    rims_ref[...] = rims16
    table = jnp.concatenate(halves(mm(first_ref[:, :latent], rims16)), axis=1)
    sums = activate(base_ref, table, onehot_ref, slab, hidden_ref, slope_ref)
    sums_ref[...] = sums
    node_pre = node_base_ref[...] + split_mm(to_node[...], sums)
    node_pre_ref[...] = node_pre
    node_hidden = slope_parts(node_pre)[0].astype(BF)
    node_hidden_ref[...] = node_hidden
    table = table_in[...] + pair_mm(to_table[...], node_hidden)
    table_ref[...] = table
    both = jnp.concatenate(halves(table), axis=1)
    alpha_ref[...] = mm(both, alpha_place[...]).astype(BF)
    beta_ref[...] = mm(both, beta_place[...]).astype(BF)
    state = slab_ref[...].astype(F32) + mm(node_second_ref[...], node_hidden) + bias_ref[:, 3:4]
    state_ref[...] = state.astype(BF)


def between_kernel(edges_ref, hidden_ref, onehot_ref, slab_in, state_ref, table_ref, sums_ref, message_in, count_ref,
                   first_ref, second_ref, node_first_ref, bias_ref,
                   new_ref, base_ref, message_ref, joined_ref, node_base_ref):
    latent = edges_ref.shape[0]
    bias = bias_ref[...]
    second = second_ref[...]
    for cols in chunks_of(edges_ref.shape[1]):
        new_ref[:, cols] = (
            edges_ref[:, cols].astype(F32) + mm(second, hidden_ref[:, cols]) + bias[:, 1:2]
        ).astype(BF)
    state16 = state_ref[...]
    target = mm(first_ref[:, latent : 2 * latent], state16)
    slab_base(table_ref[...], target, first_ref[:, 2 * latent :], bias, onehot_ref, new_ref, base_ref)
    message = message_in[...] + wide_mm(second, sums_ref[...])
    joined_ref[...] = jnp.concatenate([slab_in[...], message.astype(BF)], axis=0)
    message = message + bias[:, 1:2] * count_ref[0:1]
    message_ref[...] = message
    node_base_ref[...] = node_base(state16, message, node_first_ref, bias)


def edge_gradient(wanted, extra_ref, slope_ref, onehot_ref, edges_ref, low_ref):
    slab = wanted.shape[1]
    wide = onehot_ref.shape[0] - slab
    table = jnp.concatenate(halves(wanted), axis=1)
    total = None
    for cols in chunks_of(edges_ref.shape[1]):
        hit = onehot_ref[wide:, cols]
        grad = mm(table, jnp.concatenate([hit, hit], axis=0))
        if extra_ref is not None:
            grad = grad + extra_ref[:, cols]
        pre_low = (grad * slope_ref[:, cols]).astype(BF)
        if low_ref is not None:
            low_ref[:, cols] = pre_low
        total = add_to(
            total, mm_nt(jnp.concatenate([onehot_ref[:, cols], edges_ref[:, cols]], axis=0), pre_low)
        )
    return total.T


def middle_kernel(base_ref, onehot_ref, edges_ref, beta_in, alpha_in, node_base_ref, cot_ref,
                  node_second_back, to_node, to_node_back,
                  hidden_ref, low_ref, sums_ref, node_pre_ref, node_grad_ref, wanted_ref, first_sums_ref, rims_ref,
                  slope_ref):
    slab = cot_ref.shape[1]
    wide = onehot_ref.shape[0] - slab
    cot_grad = mm(node_second_back[...], cot_ref[...].astype(BF))
    sums = activate(base_ref, alpha_in[...] + beta_in[...], onehot_ref, slab, hidden_ref, slope_ref)
    sums_ref[...] = sums
    node_pre = node_base_ref[...] + split_mm(to_node[...], sums)
    node_pre_ref[...] = node_pre
    pre_grad = cot_grad * slope_parts(node_pre)[1]
    node_grad_ref[...] = pre_grad
    wanted = split_mm(to_node_back[...], pre_grad)
    wanted_ref[...] = wanted
    first_sums = edge_gradient(wanted, None, slope_ref, onehot_ref, edges_ref, low_ref)
    rims_ref[...] = first_sums[:, slab:wide].astype(BF)
    first_sums_ref[...] = first_sums


def carry_kernel(rim, low_ref, hidden_zero_ref, slab_ref, sums_ref, sums_zero_ref, message_in,
                 node_pre_ref, node_grad_ref, first_sums_ref, count_ref, cot_ref,
                 second_ref, first_back, node_first_back, node_second_back, to_hidden,
                 extra_ref, total_ref, joined_ref, back_ref, back_node_ref):
    latent, slab = slab_ref.shape
    wide = first_sums_ref.shape[1] - slab - latent
    sums = first_sums_ref[...]
    cot = cot_ref[...]
    pre_grad = node_grad_ref[...]
    node_back = mm(node_first_back[...], pre_grad.astype(BF))
    gm = node_back[latent:].astype(BF)
    source = sums[:, :slab].astype(BF)
    target = sums[:, wide : wide + slab].astype(BF)
    back = cot + node_back[:latent] + mm(first_back[:latent], source) + mm(first_back[latent : 2 * latent], target)
    back_ref[...] = back
    back_node_ref[...] = wide_mm(node_second_back[...], back)
    self_back = first_back[2 * latent :]
    cross = None
    for cols in chunks_of(low_ref.shape[1]):
        low = low_ref[:, cols]
        extra_ref[:, cols] = pair_mm(to_hidden[...], low)
        cross = add_to(cross, mm_nt(low, hidden_zero_ref[:, cols]))
    slab16 = slab_ref[...]
    message = message_in[...] + wide_mm(second_ref[...], sums_ref[...])
    joined = jnp.concatenate([slab16, message.astype(BF)], axis=0)
    joined_ref[...] = joined
    pre_sum = sums[:, slab + 2 * rim : slab + 2 * rim + 1]
    edge_two = (
        mm_nt(gm, sums_ref[...].astype(BF))
        + mm_nt(gm, sums_zero_ref[...].astype(BF))
        + mm(self_back, cross.astype(BF))
    )
    gm_sum = 2.0 * jnp.sum(gm.astype(F32) * count_ref[0:1], axis=1, keepdims=True) + wide_mm(
        self_back, jnp.broadcast_to(pre_sum, (latent, LANES))
    )[:, :1]
    node_one, node_two, node_pre_sum, cot_sum = node_sums(
        cot, pre_grad, joined, slope_parts(node_pre_ref[...])[0].astype(BF)
    )
    edge_one = jnp.concatenate(
        [mm_nt(source, slab16), mm_nt(target, slab16), sums[:, wide + slab :]], axis=1
    )
    used = edge_one.shape[1] + edge_two.shape[1] + node_one.shape[1] + node_two.shape[1]
    pad = jnp.zeros((latent, total_ref.shape[1] - used - 4), F32)
    total_ref[...] = jnp.concatenate(
        [edge_one, edge_two, node_one, node_two, pre_sum, gm_sum, node_pre_sum, cot_sum, pad], axis=1
    )


def output_kernel(count_ref, edges_ref, hidden_ref, joined_ref, node_pre_ref, second_ref, node_second_ref, bias_ref,
                  edge_out, node_out, new_ref):
    bias = bias_ref[...]
    latent = edges_ref.shape[0]
    second = second_ref[...]
    for cols in chunks_of(edges_ref.shape[1]):
        new_ref[:, cols] = (
            edges_ref[:, cols].astype(F32) + mm(second, hidden_ref[:, cols]) + bias[:, 1:2]
        ).astype(BF)
    slots = edge_out.shape[1]
    begin = lax.axis_index("layer") * slots
    for cols in chunks_of(slots):
        position = lax.broadcasted_iota(jnp.int32, (latent, CHUNK), 1) + cols.start
        mine = new_ref[:, pl.ds(pl.multiple_of(begin + cols.start, CHUNK), CHUNK)].astype(F32)
        edge_out[:, cols] = jnp.where(position < count_ref[0, 0], mine, 0.0).astype(BF)
    node_hidden = slope_parts(node_pre_ref[...])[0].astype(BF)
    state = joined_ref[:latent].astype(F32) + mm(node_second_ref[...], node_hidden) + bias[:, 3:4]
    node_out[...] = own_rows(state.T, node_out.shape[0]).astype(BF)


def last_kernel(rim, back_in, back_node, beta_in, alpha_in, alpha_pick, beta_pick, joined_ref, node_pre_ref,
                node_hidden_ref, wanted_in, sums_ref, count_ref, extra_ref, slope_ref, onehot_ref, edges_ref,
                slab_ref, rims_ref, slab_one_ref, total_in, first_back, node_first_back, to_node_back, to_table_back,
                total_ref, back_ref):
    latent, slab = slab_ref.shape
    wide = onehot_ref.shape[0] - slab
    placed = mm_nt(alpha_in[...], alpha_pick[...]) + mm_nt(beta_in[...], beta_pick[...])
    pre_grad = (back_node[...] + split_mm(to_table_back[...], placed)) * slope_parts(node_pre_ref[...])[1]
    wanted = wanted_in[...] + split_mm(to_node_back[...], pre_grad)
    sums = edge_gradient(wanted, extra_ref, slope_ref, onehot_ref, edges_ref, None)
    source = sums[:, :wide].astype(BF)
    target = sums[:, wide : wide + slab].astype(BF)
    ext_grad = mm(first_back[:latent], source)
    node_back = mm(node_first_back[...], pre_grad.astype(BF))
    gm = node_back[latent:].astype(BF)
    grad = back_in[...] + wide_mm(first_back[:latent], placed)
    back_ref[...] = (
        grad + node_back[:latent] + ext_grad[:, :slab] + mm(first_back[latent : 2 * latent], target)
    )
    alpha, beta = rim_gradients(ext_grad, slab, rim)
    node_one, node_two, node_pre_sum, grad_sum = node_sums(grad, pre_grad, joined_ref[...], node_hidden_ref[...])
    slab16 = slab_ref[...]
    ext16 = jnp.concatenate([slab16, rims_ref[...]], axis=1)
    edge_one = jnp.concatenate(
        [
            mm_nt(source, ext16) + mm_nt(placed.astype(BF), slab_one_ref[...]),
            mm_nt(target, slab16),
            sums[:, wide + slab :],
        ],
        axis=1,
    )
    edge_two = mm_nt(gm, sums_ref[...].astype(BF))
    pre_sum = sums[:, slab + 2 * rim : slab + 2 * rim + 1]
    gm_sum = jnp.sum(gm.astype(F32) * count_ref[0:1], axis=1, keepdims=True)
    used = edge_one.shape[1] + edge_two.shape[1] + node_one.shape[1] + node_two.shape[1]
    pad = jnp.zeros((latent, total_ref.shape[1] - used - 4 - 2 * rim), F32)
    total_ref[...] = (
        total_in[...]
        + jnp.concatenate(
            [edge_one, edge_two, node_one, node_two, pre_sum, gm_sum, node_pre_sum, grad_sum, alpha, beta, pad],
            axis=1,
        )
    ).astype(BF)


def add_kernel(used, rim, bit, mine_ref, other_ref, out_ref):
    mine = mine_ref[...].astype(F32)
    other = other_ref[...].astype(F32)
    lane = lax.broadcasted_iota(jnp.int32, mine.shape, 1)
    held = other[:, used + rim : used + 2 * rim]
    if bit == 1:
        arrived = jnp.zeros_like(held)
        passing = held
    else:
        place = lax.axis_index("phi")
        home = (lax.rem(place // bit, 2) == 1) == (lax.rem(place, 2) == 0)
        arrived = mine[:, used : used + rim] + jnp.where(home, held, 0.0)
        passing = jnp.where(home, 0.0, held)
    pad = jnp.zeros((mine.shape[0], mine.shape[1] - used - 2 * rim), F32)
    out_ref[...] = jnp.concatenate(
        [(mine + other)[:, :used], arrived, passing, pad], axis=1
    ).astype(BF)


def finish_kernel(used, rim, mine_ref, other_ref, back_ref, alpha_in, upper_ref, lower_ref,
                  node_grad, edge_one, edge_two, node_one, node_two, bias_out):
    mine = mine_ref[...].astype(F32)
    other = other_ref[...].astype(F32)
    total = mine + other
    cut = 0
    for ref in (edge_one, edge_two, node_one, node_two):
        ref[...] = total[:, cut : cut + ref.shape[1]]
        cut += ref.shape[1]
    block = used - 4 - (used - 4) % LANES
    turned = total[:, block : block + LANES].T
    bias_out[...] = turned[used - 4 - block : used - block]
    alpha = alpha_in[...].astype(F32)[:, used : used + rim]
    beta = mine[:, used : used + rim] + other[:, used + rim : used + 2 * rim]
    grad = back_ref[...] + placed_rims(alpha, beta, upper_ref, lower_ref)
    node_grad[...] = own_rows(grad.T, node_grad.shape[0])


def call(kernel, outs, *args, scratch=(), smem=0, hbm=(), cost=1.0):
    args = [
        pltpu.with_memory_space_constraint(arg, HBM) if place in hbm else arg for place, arg in enumerate(args)
    ]
    held = [(arg.shape, arg.dtype) for arg in args] + list(outs)
    held += [(ref.shape, ref.dtype) for ref in scratch if jnp.issubdtype(ref.dtype, jnp.number)]
    room = sum(math.prod(shape) * jnp.dtype(kind).itemsize for shape, kind in held)
    spaces = [pltpu.SMEM if place < smem else HBM if place in hbm else VM for place in range(len(args))]
    specs = [pl.BlockSpec(memory_space=space) for space in spaces]
    return pl.pallas_call(
        kernel,
        out_shape=[jax.ShapeDtypeStruct(shape, kind) for shape, kind in outs],
        in_specs=specs,
        out_specs=[pl.BlockSpec(memory_space=VM) for _ in outs],
        scratch_shapes=list(scratch),
        compiler_params=pltpu.CompilerParams(vmem_limit_bytes=room + 10 * 1024 * 1024),
        cost_estimate=pl.CostEstimate(
            flops=int(cost * 1e9), bytes_accessed=int(cost * 3.6e6), transcendentals=0
        ),
    )(*args)


def swap(value, axis, pairing):
    count = lax.axis_size(axis)
    return lax.ppermute(value, axis, [(source, pairing(source) % count) for source in range(count)])


def by_alpha(value):
    return swap(value, "phi", lambda index: index ^ 1)


def by_beta(value):
    return swap(value, "phi", lambda index: index - 1 if index % 2 == 0 else index + 1)


def layer_parts(value):
    groups = lax.axis_size("layer")
    return [value] + [
        swap(value, "layer", lambda index, turn=turn: index + turn) for turn in range(1, groups)
    ]


def body(node_feats, edge_feats, edge_source, edge_target, edge_counts, rim_upper, rim_lower,
         edge_first, edge_second, node_first, node_second, biases, node_cot):
    groups = lax.axis_size("layer")
    ring = lax.axis_size("phi")
    latent, width = node_feats.shape
    hidden = edge_second.shape[1]
    slots = edge_feats.shape[1]
    slab = width * groups
    rim = rim_upper.shape[1]
    wide = (slab + 2 * rim) // LANES * LANES + LANES
    total_slots = slots * groups
    rows = slots // LANES
    room = wide - slab
    rim_shape = ((latent, room), BF)
    per_slot = lambda kind: ((latent, total_slots), kind)
    per_hit = lambda kind, depth=1: ((depth * latent, slab), kind)

    packed, upper, lower = call(
        prep_kernel,
        [((3 * rows + width, LANES), BF), ((1, rim), jnp.int32), ((1, rim), jnp.int32)],
        edge_counts, edge_source.reshape(rows, LANES), edge_target.reshape(rows, LANES),
        node_feats.T, node_cot.T, rim_upper, rim_lower,
        scratch=[VM((rows, LANES), jnp.int32), VM((rows, LANES), jnp.int32),
                 VM((width, latent), BF), VM((width, latent), F32), pltpu.SemaphoreType.DMA((6,))],
        smem=1, hbm=range(1, 7),
    )
    packs = layer_parts(packed)
    upper, lower, alpha_pick, beta_pick = call(
        pick_kernel,
        [((slab, rim), BF), ((slab, rim), BF), ((slab, room), BF), ((slab, room), BF)],
        packed, upper, lower, cost=0.1,
    )
    later, _ = lax.optimization_barrier((edge_feats, alpha_pick))
    parts = [edge_feats] + layer_parts(later)[1:]
    slab_zero, cot, alpha, beta = call(
        functools.partial(slab_kernel, groups, rows),
        [per_hit(BF), per_hit(F32), rim_shape, rim_shape], *packs, alpha_pick, beta_pick, cost=20.0,
    )
    beta = by_beta(beta)
    alpha = by_alpha(alpha)
    (onehot, first_back, second_back, node_first_back, node_second_back, bias,
     to_node, to_node_back, to_table, to_table_back, to_hidden, alpha_place, beta_place) = call(
        functools.partial(onehot_kernel, groups, rows, rim),
        [((wide + slab, total_slots), BF), (edge_first.shape[::-1], BF), (edge_second.shape[::-1], BF),
         (node_first.shape[::-1], BF), (node_second.shape[::-1], BF), (biases.shape[::-1], F32)]
        + [((hidden, 3 * hidden), BF)] * 5 + [((2 * slab, 2 * room), BF)] * 2,
        *packs, edge_first, edge_second, node_first, node_second, biases, alpha_pick, beta_pick, cost=2.0,
    )
    edges_zero, base, message, count, node_base_zero, table = call(
        functools.partial(start_kernel, groups),
        [per_slot(BF), per_slot(F32), per_hit(F32), ((8, slab), F32), per_hit(F32), per_hit(F32)],
        *parts, onehot, slab_zero, edge_first, node_first, bias, cost=1.0,
    )
    (hidden_zero, slope, rims_zero, sums_zero, node_pre_zero, node_hidden_zero, slab_one, table,
     alpha, beta) = call(
        forward_kernel,
        [per_slot(BF), per_slot(F32), rim_shape, per_hit(F32), per_hit(F32), per_hit(BF), per_hit(BF), per_hit(F32),
         ((latent, 2 * room), BF), ((latent, 2 * room), BF)],
        base, onehot, slab_zero, beta, alpha, node_base_zero, table, edge_first, node_second, bias, to_node, to_table,
        alpha_place, beta_place, cost=2.0,
    )
    beta = by_beta(beta)
    alpha = by_alpha(alpha)
    edges_one, base, message, joined_zero, node_base_one = call(
        between_kernel, [per_slot(BF), per_slot(F32), per_hit(F32), per_hit(BF, 2), per_hit(F32)],
        edges_zero, hidden_zero, onehot, slab_zero, slab_one, table, sums_zero, message, count,
        edge_first, edge_second, node_first, bias, cost=2.0,
    )
    total_width = edge_first.shape[1] + hidden + node_first.shape[1] + node_second.shape[1] + 4
    lanes = -(-(total_width + 2 * rim) // LANES) * LANES
    hidden_one, low, sums_one, node_pre_one, node_grad_one, wanted, first_sums, rims = call(
        middle_kernel,
        [per_slot(BF), per_slot(BF), per_hit(F32), per_hit(F32), per_hit(F32), per_hit(F32),
         ((hidden, wide + slab + latent), F32), rim_shape],
        base, onehot, edges_one, beta, alpha, node_base_one, cot, node_second_back, to_node, to_node_back,
        scratch=[VM((hidden, total_slots), F32)], cost=3.0,
    )
    beta = by_beta(rims)
    alpha = by_alpha(rims)
    extra, total, joined_one, back, back_node = call(
        functools.partial(carry_kernel, rim),
        [per_slot(F32), ((latent, lanes), F32), per_hit(BF, 2), per_hit(F32), per_hit(F32)],
        low, hidden_zero, slab_one, sums_one, sums_zero, message, node_pre_one, node_grad_one, first_sums, count, cot,
        edge_second, first_back, node_first_back, node_second_back, to_hidden, cost=2.0,
    )
    edge_out, node_out = call(
        output_kernel, [((latent, slots), BF), ((width, latent), BF)],
        edge_counts, edges_one, hidden_one, joined_one, node_pre_one, edge_second, node_second, bias,
        scratch=[VM((latent, total_slots), BF)], smem=1, cost=2.0,
    )
    total, back = call(
        functools.partial(last_kernel, rim), [((latent, lanes), BF), per_hit(F32)],
        back, back_node, beta, alpha, alpha_pick, beta_pick, joined_zero, node_pre_zero, node_hidden_zero, wanted,
        sums_zero, count, extra, slope, onehot, edges_zero, slab_zero, rims_zero, slab_one, total,
        first_back, node_first_back, to_node_back, to_table_back, cost=2.0,
    )
    other = by_alpha(total)
    alpha_last = other
    bit = 1
    while 2 * bit < ring:
        total = call(
            functools.partial(add_kernel, total_width, rim, bit), [((latent, lanes), BF)], total, other, cost=0.1,
        )[0]
        bit *= 2
        other = swap(total, "phi", lambda index, bit=bit: index ^ bit)
    node_grad, edge_one, edge_two, node_one, node_two, bias_out = call(
        functools.partial(finish_kernel, total_width, rim),
        [((width, latent), F32), (edge_first.shape, F32), (edge_second.shape, F32),
         (node_first.shape, F32), (node_second.shape, F32), (biases.shape, F32)],
        total, other, back, alpha_last, upper, lower,
    )
    return node_out.T, edge_out, node_grad.T, edge_one, edge_two, node_one, node_two, bias_out


def solution(mesh):
    split = P(None, ("phi", "layer"))
    return jax.shard_map(
        body,
        mesh=mesh,
        in_specs=(split, split, P(("phi", "layer")), P(("phi", "layer")), P("phi", "layer"),
                  P("phi", None), P("phi", None), P(), P(), P(), P(), P(), split),
        out_specs=(split, split, split, P(), P(), P(), P(), P()),
        check_vma=False,
    )
```

```python
import functools
import math

import jax
import jax.numpy as jnp
from jax import lax
from jax.experimental import pallas as pl
from jax.experimental.pallas import tpu as pltpu
from jax.sharding import PartitionSpec as P

BF = jnp.bfloat16
F32 = jnp.float32
CHUNK = 256
LANES = 128
HBM = pltpu.HBM
VM = pltpu.VMEM


def mm(left, right):
    return jnp.dot(left, right, preferred_element_type=F32)


def mm_nt(left, right):
    return lax.dot_general(left, right, (((1,), (1,)), ((), ())), preferred_element_type=F32)


def flip(weight):
    return weight.astype(F32).T.astype(BF)


def halves(value):
    high = value.astype(BF)
    return high, (value - high.astype(F32)).astype(BF)


def wide_mm(weight, value):
    high, low = halves(value)
    return mm(jnp.concatenate([weight, weight], axis=1), jnp.concatenate([high, low], axis=0))


def sigmoid(value):
    return 0.5 + 0.5 * jnp.tanh(0.5 * value)


def add_to(total, value):
    return value if total is None else total + value


def chunks_of(count):
    return [slice(first, first + CHUNK) for first in range(0, count, CHUNK)]


def is_even():
    return lax.rem(lax.axis_index("phi"), 2) == 0


def pick(parts, natural):
    groups = len(parts)
    turn = lax.rem(lax.axis_index("layer") - natural + groups, groups)
    value = parts[0]
    for rank in range(1, groups):
        value = jnp.where(turn == rank, parts[rank], value)
    return value


def own_rows(slab_rows, width):
    layer = lax.axis_index("layer")
    value = slab_rows[:width]
    for rank in range(1, slab_rows.shape[0] // width):
        value = jnp.where(layer == rank, slab_rows[rank * width : (rank + 1) * width], value)
    return value


def split(value):
    high, low = halves(value)
    return jnp.concatenate([high, high, low], axis=1)


def split_mm(table, value):
    high, low = halves(value)
    return mm(table, jnp.concatenate([high, low, high], axis=0))


def pair_mm(table, value):
    return mm(table[:, value.shape[0] :], jnp.concatenate([value, value], axis=0))


def placed_rims(alpha, beta, upper_ref, lower_ref):
    even = is_even()
    from_upper = jnp.where(even, alpha, beta).astype(BF)
    from_lower = jnp.where(even, beta, alpha).astype(BF)
    return mm_nt(from_upper, upper_ref[...]) + mm_nt(from_lower, lower_ref[...])


def rim_gradients(ext_grad, slab, rim):
    even = is_even()
    below = ext_grad[:, slab : slab + rim]
    above = ext_grad[:, slab + rim : slab + 2 * rim]
    return jnp.where(even, above, below), jnp.where(even, below, above)


def slope_parts(pre):
    logistic = sigmoid(pre)
    value = pre * logistic
    return value, logistic + value * (1.0 - logistic)


def activate(base_ref, table, onehot_ref, slab, hidden_ref, slope_ref):
    wide = onehot_ref.shape[0] - slab
    total = None
    for cols in chunks_of(base_ref.shape[1]):
        rims = onehot_ref[slab:wide, cols]
        pre = base_ref[:, cols] + mm(table, jnp.concatenate([rims, rims], axis=0))
        value, slope = slope_parts(pre)
        hidden = value.astype(BF)
        hidden_ref[:, cols] = hidden
        slope_ref[:, cols] = slope
        total = add_to(total, mm_nt(hidden, onehot_ref[wide:, cols]))
    return total


def slab_base(source, target, own, bias, onehot_ref, edges_ref, base_ref):
    slab = source.shape[1]
    wide = onehot_ref.shape[0] - slab
    table = jnp.concatenate([*halves(source), *halves(target), own], axis=1)
    for cols in chunks_of(base_ref.shape[1]):
        near = onehot_ref[:slab, cols]
        hit = onehot_ref[wide:, cols]
        stack = jnp.concatenate([near, near, hit, hit, edges_ref[:, cols]], axis=0)
        base_ref[:, cols] = mm(table, stack) + bias[:, 0:1]


def node_base(state16, message, first_ref, bias):
    latent = state16.shape[0]
    return (
        mm(first_ref[:, :latent], state16)
        + wide_mm(first_ref[:, latent:], message)
        + bias[:, 2:3]
    )


def node_sums(grad, pre_grad, joined, hidden):
    return (
        mm_nt(pre_grad.astype(BF), joined),
        mm_nt(grad.astype(BF), hidden),
        jnp.sum(pre_grad, axis=1, keepdims=True),
        jnp.sum(grad, axis=1, keepdims=True),
    )


def prep_kernel(count_ref, source_hbm, target_hbm, feats_hbm, cot_hbm, upper_hbm, lower_hbm,
                out_ref, upper_ref, lower_ref, source, target, feats, cot, sems):
    pairs = ((source_hbm, source), (target_hbm, target), (feats_hbm, feats), (cot_hbm, cot),
             (upper_hbm, upper_ref), (lower_hbm, lower_ref))
    copies = [pltpu.make_async_copy(a, b, sems.at[place]) for place, (a, b) in enumerate(pairs)]
    for copy in copies:
        copy.start()
    for copy in copies:
        copy.wait()
    rows = source.shape[0]
    position = lax.broadcasted_iota(jnp.int32, (rows, LANES), 0) * LANES + lax.broadcasted_iota(
        jnp.int32, (rows, LANES), 1
    )
    valid = position < count_ref[0, 0]
    index = source[...]
    out_ref[:rows] = jnp.where(valid, index // LANES, -1).astype(F32).astype(BF)
    out_ref[rows : 2 * rows] = (index % LANES).astype(F32).astype(BF)
    out_ref[2 * rows : 3 * rows] = jnp.where(valid, target[...], -1).astype(F32).astype(BF)
    out_ref[3 * rows :] = jnp.concatenate([feats[...].astype(F32), cot[...]], axis=1).astype(BF)


def pick_kernel(packed_ref, upper, lower, upper_ref, lower_ref, alpha_pick, beta_pick):
    hits = lax.broadcasted_iota(jnp.int32, upper_ref.shape, 0)
    upper_ref[...] = (hits == upper[...]).astype(F32).astype(BF)
    lower_ref[...] = (hits == lower[...]).astype(F32).astype(BF)
    slab, room = alpha_pick.shape
    rim = upper.shape[1]
    first = jnp.concatenate([upper[...], jnp.full((1, room - rim), -1, jnp.int32)], axis=1)
    second = jnp.concatenate(
        [jnp.full((1, rim), -1, jnp.int32), lower[...], jnp.full((1, room - 2 * rim), -1, jnp.int32)], axis=1
    )
    even = is_even()
    hits = lax.broadcasted_iota(jnp.int32, (slab, room), 0)
    alpha_pick[...] = (hits == jnp.where(even, first, second)).astype(F32).astype(BF)
    beta_pick[...] = (hits == jnp.where(even, second, first)).astype(F32).astype(BF)


def slab_kernel(groups, rows, *refs):
    packs = [ref[3 * rows :].astype(F32) for ref in refs[:groups]]
    alpha_pick, beta_pick, slab_ref, cot_ref, alpha_ref, beta_ref = refs[groups:]
    latent = slab_ref.shape[0]
    both = jnp.concatenate([pick(packs, rank) for rank in range(groups)], axis=0).T
    slab16 = both[:latent].astype(BF)
    slab_ref[...] = slab16
    cot_ref[...] = both[latent:]
    alpha_ref[...] = mm(slab16, alpha_pick[...]).astype(BF)
    beta_ref[...] = mm(slab16, beta_pick[...]).astype(BF)


def onehot_kernel(groups, rows, rim, *refs):
    packs = [ref[: 3 * rows].astype(F32) for ref in refs[:groups]]
    (slab_ref, first_ref, second_ref, node_first_ref, node_second_ref, bias_ref, alpha_pick, beta_pick,
     onehot_ref, base_ref, count_ref, table_ref, first_back, second_back, node_first_back, node_second_back, bias_out,
     to_node, to_node_back, to_table, to_table_back, to_hidden, alpha_place, beta_place) = refs[groups:]
    latent = first_ref.shape[0]
    slab, room = alpha_pick.shape
    wide = slab + room
    source_rows = lax.broadcasted_iota(jnp.int32, (wide, LANES), 0).astype(F32)
    target_rows = lax.broadcasted_iota(jnp.int32, (slab, LANES), 0).astype(F32)
    ones_row = source_rows == float(slab + 2 * rim)
    for rank in range(groups):
        pack = pick(packs, rank)
        source = jnp.where(pack[:rows] < 0.0, -1.0, pack[:rows] * LANES + pack[rows : 2 * rows])
        target = pack[2 * rows :]
        for row in range(rows):
            cols = slice((rank * rows + row) * LANES, (rank * rows + row + 1) * LANES)
            match = (source_rows == source[row : row + 1]) | ones_row
            onehot_ref[:wide, cols] = jnp.where(match, 1.0, 0.0).astype(BF)
            onehot_ref[wide:, cols] = jnp.where(target_rows == target[row : row + 1], 1.0, 0.0).astype(BF)
    bias = bias_ref[...].T
    bias_out[...] = bias
    slab16 = slab_ref[...]
    source = mm(first_ref[:, :latent], slab16)
    target = mm(first_ref[:, latent : 2 * latent], slab16)
    shift = wide_mm(first_ref[:, :latent], jnp.broadcast_to(bias[:, 3:4], (latent, LANES)))
    table_ref[...] = source + shift[:, :1]
    table = jnp.concatenate([*halves(source), *halves(target)], axis=1)
    count = None
    for cols in chunks_of(base_ref.shape[1]):
        near = onehot_ref[:slab, cols]
        hit = onehot_ref[wide:, cols]
        base_ref[:, cols] = mm(table, jnp.concatenate([near, near, hit, hit], axis=0)) + bias[:, 0:1]
        count = add_to(count, mm_nt(jnp.ones((16, CHUNK), BF), hit))
    count_ref[...] = count[:8]
    first_back[...] = flip(first_ref[...])
    second_back[...] = flip(second_ref[...])
    node_first_back[...] = flip(node_first_ref[...])
    node_second_back[...] = flip(node_second_ref[...])
    forward = mm(node_first_ref[:, latent:], second_ref[...])
    to_node[...] = split(forward)
    to_node_back[...] = split(forward.T)
    table = mm(first_ref[:, :latent], node_second_ref[...])
    to_table[...] = split(table)
    to_table_back[...] = split(table.T)
    to_hidden[...] = split(mm(first_ref[:, 2 * latent :], second_ref[...]).T)
    for choose, place in ((alpha_pick, alpha_place), (beta_pick, beta_place)):
        block = choose[...].astype(F32)
        none = jnp.zeros_like(block)
        place[...] = jnp.concatenate(
            [jnp.concatenate([block, none], axis=1), jnp.concatenate([none, block], axis=1)], axis=0
        ).astype(BF)


def start_kernel(groups, *refs):
    parts = refs[:groups]
    (base_in, onehot_ref, slab_ref, count_ref, first_ref, node_first_ref, bias_ref,
     edges_ref, base_ref, message_ref, node_base_ref) = refs[groups:]
    latent, slab = slab_ref.shape
    wide = onehot_ref.shape[0] - slab
    slots = parts[0].shape[1]
    own = first_ref[:, 2 * latent :]
    message = None
    for rank in range(groups):
        for cols in chunks_of(slots):
            here = slice(rank * slots + cols.start, rank * slots + cols.stop)
            edges = pick([part[:, cols] for part in parts], rank)
            edges_ref[:, here] = edges
            base_ref[:, here] = base_in[:, here] + mm(own, edges)
            message = add_to(message, mm_nt(edges, onehot_ref[wide:, here]))
    bias = bias_ref[...]
    message = message + bias[:, 1:2] * count_ref[0:1]
    message_ref[...] = message
    node_base_ref[...] = node_base(slab_ref[...], message, node_first_ref, bias)


def forward_kernel(base_ref, onehot_ref, slab_ref, beta_in, alpha_in, node_base_ref, table_in,
                   first_ref, node_second_ref, bias_ref, to_node, to_table, alpha_place, beta_place,
                   hidden_ref, slope_ref, rims_ref, sums_ref, node_pre_ref, node_hidden_ref, state_ref, table_ref,
                   alpha_ref, beta_ref):
    latent, slab = slab_ref.shape
    rims16 = alpha_in[...] + beta_in[...]
    rims_ref[...] = rims16
    table = jnp.concatenate(halves(mm(first_ref[:, :latent], rims16)), axis=1)
    sums = activate(base_ref, table, onehot_ref, slab, hidden_ref, slope_ref)
    sums_ref[...] = sums
    node_pre = node_base_ref[...] + split_mm(to_node[...], sums)
    node_pre_ref[...] = node_pre
    node_hidden = slope_parts(node_pre)[0].astype(BF)
    node_hidden_ref[...] = node_hidden
    table = table_in[...] + pair_mm(to_table[...], node_hidden)
    table_ref[...] = table
    both = jnp.concatenate(halves(table), axis=1)
    alpha_ref[...] = mm(both, alpha_place[...]).astype(BF)
    beta_ref[...] = mm(both, beta_place[...]).astype(BF)
    state = slab_ref[...].astype(F32) + mm(node_second_ref[...], node_hidden) + bias_ref[:, 3:4]
    state_ref[...] = state.astype(BF)


def between_kernel(edges_ref, hidden_ref, onehot_ref, slab_in, state_ref, table_ref, sums_ref, message_in, count_ref,
                   first_ref, second_ref, node_first_ref, bias_ref,
                   new_ref, base_ref, message_ref, joined_ref, node_base_ref):
    latent = edges_ref.shape[0]
    bias = bias_ref[...]
    second = second_ref[...]
    for cols in chunks_of(edges_ref.shape[1]):
        new_ref[:, cols] = (
            edges_ref[:, cols].astype(F32) + mm(second, hidden_ref[:, cols]) + bias[:, 1:2]
        ).astype(BF)
    state16 = state_ref[...]
    target = mm(first_ref[:, latent : 2 * latent], state16)
    slab_base(table_ref[...], target, first_ref[:, 2 * latent :], bias, onehot_ref, new_ref, base_ref)
    message = message_in[...] + wide_mm(second, sums_ref[...])
    joined_ref[...] = jnp.concatenate([slab_in[...], message.astype(BF)], axis=0)
    message = message + bias[:, 1:2] * count_ref[0:1]
    message_ref[...] = message
    node_base_ref[...] = node_base(state16, message, node_first_ref, bias)


def edge_gradient(wanted, extra_ref, slope_ref, onehot_ref, edges_ref, low_ref):
    slab = wanted.shape[1]
    wide = onehot_ref.shape[0] - slab
    table = jnp.concatenate(halves(wanted), axis=1)
    total = None
    for cols in chunks_of(edges_ref.shape[1]):
        hit = onehot_ref[wide:, cols]
        grad = mm(table, jnp.concatenate([hit, hit], axis=0))
        if extra_ref is not None:
            grad = grad + extra_ref[:, cols]
        pre_low = (grad * slope_ref[:, cols]).astype(BF)
        if low_ref is not None:
            low_ref[:, cols] = pre_low
        total = add_to(
            total, mm_nt(pre_low, jnp.concatenate([onehot_ref[:, cols], edges_ref[:, cols]], axis=0))
        )
    return total


def middle_kernel(base_ref, onehot_ref, edges_ref, beta_in, alpha_in, node_base_ref, cot_ref,
                  node_second_back, to_node, to_node_back,
                  hidden_ref, low_ref, sums_ref, node_pre_ref, node_grad_ref, wanted_ref, first_sums_ref, rims_ref,
                  slope_ref):
    slab = cot_ref.shape[1]
    wide = onehot_ref.shape[0] - slab
    cot_grad = mm(node_second_back[...], cot_ref[...].astype(BF))
    sums = activate(base_ref, alpha_in[...] + beta_in[...], onehot_ref, slab, hidden_ref, slope_ref)
    sums_ref[...] = sums
    node_pre = node_base_ref[...] + split_mm(to_node[...], sums)
    node_pre_ref[...] = node_pre
    pre_grad = cot_grad * slope_parts(node_pre)[1]
    node_grad_ref[...] = pre_grad
    wanted = split_mm(to_node_back[...], pre_grad)
    wanted_ref[...] = wanted
    first_sums = edge_gradient(wanted, None, slope_ref, onehot_ref, edges_ref, low_ref)
    rims_ref[...] = first_sums[:, slab:wide].astype(BF)
    first_sums_ref[...] = first_sums


def carry_kernel(rim, low_ref, hidden_zero_ref, slab_ref, sums_ref, sums_zero_ref, message_in,
                 node_pre_ref, node_grad_ref, first_sums_ref, count_ref, cot_ref,
                 second_ref, first_back, node_first_back, node_second_back, to_hidden,
                 extra_ref, total_ref, joined_ref, back_ref, back_node_ref):
    latent, slab = slab_ref.shape
    wide = first_sums_ref.shape[1] - slab - latent
    sums = first_sums_ref[...]
    cot = cot_ref[...]
    pre_grad = node_grad_ref[...]
    node_back = mm(node_first_back[...], pre_grad.astype(BF))
    gm = node_back[latent:].astype(BF)
    source = sums[:, :slab].astype(BF)
    target = sums[:, wide : wide + slab].astype(BF)
    back = cot + node_back[:latent] + mm(first_back[:latent], source) + mm(first_back[latent : 2 * latent], target)
    back_ref[...] = back
    back_node_ref[...] = wide_mm(node_second_back[...], back)
    self_back = first_back[2 * latent :]
    cross = None
    for cols in chunks_of(low_ref.shape[1]):
        low = low_ref[:, cols]
        extra_ref[:, cols] = pair_mm(to_hidden[...], low)
        cross = add_to(cross, mm_nt(low, hidden_zero_ref[:, cols]))
    slab16 = slab_ref[...]
    message = message_in[...] + wide_mm(second_ref[...], sums_ref[...])
    joined = jnp.concatenate([slab16, message.astype(BF)], axis=0)
    joined_ref[...] = joined
    pre_sum = sums[:, slab + 2 * rim : slab + 2 * rim + 1]
    edge_two = (
        mm_nt(gm, sums_ref[...].astype(BF))
        + mm_nt(gm, sums_zero_ref[...].astype(BF))
        + mm(self_back, cross.astype(BF))
    )
    gm_sum = 2.0 * jnp.sum(gm.astype(F32) * count_ref[0:1], axis=1, keepdims=True) + wide_mm(
        self_back, jnp.broadcast_to(pre_sum, (latent, LANES))
    )[:, :1]
    node_one, node_two, node_pre_sum, cot_sum = node_sums(
        cot, pre_grad, joined, slope_parts(node_pre_ref[...])[0].astype(BF)
    )
    edge_one = jnp.concatenate(
        [mm_nt(source, slab16), mm_nt(target, slab16), sums[:, wide + slab :]], axis=1
    )
    used = edge_one.shape[1] + edge_two.shape[1] + node_one.shape[1] + node_two.shape[1]
    pad = jnp.zeros((latent, total_ref.shape[1] - used - 4), F32)
    total_ref[...] = jnp.concatenate(
        [edge_one, edge_two, node_one, node_two, pre_sum, gm_sum, node_pre_sum, cot_sum, pad], axis=1
    )


def output_kernel(count_ref, edges_ref, hidden_ref, joined_ref, node_pre_ref, second_ref, node_second_ref, bias_ref,
                  edge_out, node_out, new_ref):
    bias = bias_ref[...]
    latent = edges_ref.shape[0]
    second = second_ref[...]
    for cols in chunks_of(edges_ref.shape[1]):
        new_ref[:, cols] = (
            edges_ref[:, cols].astype(F32) + mm(second, hidden_ref[:, cols]) + bias[:, 1:2]
        ).astype(BF)
    slots = edge_out.shape[1]
    begin = lax.axis_index("layer") * slots
    for cols in chunks_of(slots):
        position = lax.broadcasted_iota(jnp.int32, (latent, CHUNK), 1) + cols.start
        mine = new_ref[:, pl.ds(pl.multiple_of(begin + cols.start, CHUNK), CHUNK)].astype(F32)
        edge_out[:, cols] = jnp.where(position < count_ref[0, 0], mine, 0.0).astype(BF)
    node_hidden = slope_parts(node_pre_ref[...])[0].astype(BF)
    state = joined_ref[:latent].astype(F32) + mm(node_second_ref[...], node_hidden) + bias[:, 3:4]
    node_out[...] = own_rows(state.T, node_out.shape[0]).astype(BF)


def last_kernel(rim, back_in, back_node, beta_in, alpha_in, alpha_pick, beta_pick, joined_ref, node_pre_ref,
                node_hidden_ref, wanted_in, sums_ref, count_ref, extra_ref, slope_ref, onehot_ref, edges_ref,
                slab_ref, rims_ref, slab_one_ref, total_in, first_back, node_first_back, to_node_back, to_table_back,
                total_ref, back_ref):
    latent, slab = slab_ref.shape
    wide = onehot_ref.shape[0] - slab
    placed = mm_nt(alpha_in[...], alpha_pick[...]) + mm_nt(beta_in[...], beta_pick[...])
    pre_grad = (back_node[...] + split_mm(to_table_back[...], placed)) * slope_parts(node_pre_ref[...])[1]
    wanted = wanted_in[...] + split_mm(to_node_back[...], pre_grad)
    sums = edge_gradient(wanted, extra_ref, slope_ref, onehot_ref, edges_ref, None)
    source = sums[:, :wide].astype(BF)
    target = sums[:, wide : wide + slab].astype(BF)
    ext_grad = mm(first_back[:latent], source)
    node_back = mm(node_first_back[...], pre_grad.astype(BF))
    gm = node_back[latent:].astype(BF)
    grad = back_in[...] + wide_mm(first_back[:latent], placed)
    back_ref[...] = (
        grad + node_back[:latent] + ext_grad[:, :slab] + mm(first_back[latent : 2 * latent], target)
    )
    alpha, beta = rim_gradients(ext_grad, slab, rim)
    node_one, node_two, node_pre_sum, grad_sum = node_sums(grad, pre_grad, joined_ref[...], node_hidden_ref[...])
    slab16 = slab_ref[...]
    ext16 = jnp.concatenate([slab16, rims_ref[...]], axis=1)
    edge_one = jnp.concatenate(
        [
            mm_nt(source, ext16) + mm_nt(placed.astype(BF), slab_one_ref[...]),
            mm_nt(target, slab16),
            sums[:, wide + slab :],
        ],
        axis=1,
    )
    edge_two = mm_nt(gm, sums_ref[...].astype(BF))
    pre_sum = sums[:, slab + 2 * rim : slab + 2 * rim + 1]
    gm_sum = jnp.sum(gm.astype(F32) * count_ref[0:1], axis=1, keepdims=True)
    used = edge_one.shape[1] + edge_two.shape[1] + node_one.shape[1] + node_two.shape[1]
    pad = jnp.zeros((latent, total_ref.shape[1] - used - 4 - 2 * rim), F32)
    total_ref[...] = (
        total_in[...]
        + jnp.concatenate(
            [edge_one, edge_two, node_one, node_two, pre_sum, gm_sum, node_pre_sum, grad_sum, alpha, beta, pad],
            axis=1,
        )
    ).astype(BF)


def add_kernel(used, rim, bit, mine_ref, other_ref, out_ref):
    mine = mine_ref[...].astype(F32)
    other = other_ref[...].astype(F32)
    lane = lax.broadcasted_iota(jnp.int32, mine.shape, 1)
    held = other[:, used + rim : used + 2 * rim]
    if bit == 1:
        arrived = jnp.zeros_like(held)
        passing = held
    else:
        place = lax.axis_index("phi")
        home = (lax.rem(place // bit, 2) == 1) == (lax.rem(place, 2) == 0)
        arrived = mine[:, used : used + rim] + jnp.where(home, held, 0.0)
        passing = jnp.where(home, 0.0, held)
    pad = jnp.zeros((mine.shape[0], mine.shape[1] - used - 2 * rim), F32)
    out_ref[...] = jnp.concatenate(
        [(mine + other)[:, :used], arrived, passing, pad], axis=1
    ).astype(BF)


def finish_kernel(used, rim, mine_ref, other_ref, back_ref, alpha_in, upper_ref, lower_ref,
                  node_grad, edge_one, edge_two, node_one, node_two, bias_out):
    mine = mine_ref[...].astype(F32)
    other = other_ref[...].astype(F32)
    total = mine + other
    cut = 0
    for ref in (edge_one, edge_two, node_one, node_two):
        ref[...] = total[:, cut : cut + ref.shape[1]]
        cut += ref.shape[1]
    block = used - 4 - (used - 4) % LANES
    turned = total[:, block : block + LANES].T
    bias_out[...] = turned[used - 4 - block : used - block]
    alpha = alpha_in[...].astype(F32)[:, used : used + rim]
    beta = mine[:, used : used + rim] + other[:, used + rim : used + 2 * rim]
    grad = back_ref[...] + placed_rims(alpha, beta, upper_ref, lower_ref)
    node_grad[...] = own_rows(grad.T, node_grad.shape[0])


def call(kernel, outs, *args, scratch=(), smem=0, hbm=(), cost=1.0):
    args = [
        pltpu.with_memory_space_constraint(arg, HBM) if place in hbm else arg for place, arg in enumerate(args)
    ]
    held = [(arg.shape, arg.dtype) for arg in args] + list(outs)
    held += [(ref.shape, ref.dtype) for ref in scratch if jnp.issubdtype(ref.dtype, jnp.number)]
    room = sum(math.prod(shape) * jnp.dtype(kind).itemsize for shape, kind in held)
    spaces = [pltpu.SMEM if place < smem else HBM if place in hbm else VM for place in range(len(args))]
    specs = [pl.BlockSpec(memory_space=space) for space in spaces]
    return pl.pallas_call(
        kernel,
        out_shape=[jax.ShapeDtypeStruct(shape, kind) for shape, kind in outs],
        in_specs=specs,
        out_specs=[pl.BlockSpec(memory_space=VM) for _ in outs],
        scratch_shapes=list(scratch),
        compiler_params=pltpu.CompilerParams(vmem_limit_bytes=room + 10 * 1024 * 1024),
        cost_estimate=pl.CostEstimate(
            flops=int(cost * 1e9), bytes_accessed=int(cost * 3.6e6), transcendentals=0
        ),
    )(*args)


def swap(value, axis, pairing):
    count = lax.axis_size(axis)
    return lax.ppermute(value, axis, [(source, pairing(source) % count) for source in range(count)])


def by_alpha(value):
    return swap(value, "phi", lambda index: index ^ 1)


def by_beta(value):
    return swap(value, "phi", lambda index: index - 1 if index % 2 == 0 else index + 1)


def layer_parts(value):
    groups = lax.axis_size("layer")
    return [value] + [
        swap(value, "layer", lambda index, turn=turn: index + turn) for turn in range(1, groups)
    ]


def body(node_feats, edge_feats, edge_source, edge_target, edge_counts, rim_upper, rim_lower,
         edge_first, edge_second, node_first, node_second, biases, node_cot):
    groups = lax.axis_size("layer")
    ring = lax.axis_size("phi")
    latent, width = node_feats.shape
    hidden = edge_second.shape[1]
    slots = edge_feats.shape[1]
    slab = width * groups
    rim = rim_upper.shape[1]
    wide = (slab + 2 * rim) // LANES * LANES + LANES
    total_slots = slots * groups
    rows = slots // LANES
    room = wide - slab
    rim_shape = ((latent, room), BF)
    per_slot = lambda kind: ((latent, total_slots), kind)
    per_hit = lambda kind, depth=1: ((depth * latent, slab), kind)

    packed, upper, lower = call(
        prep_kernel,
        [((3 * rows + width, LANES), BF), ((1, rim), jnp.int32), ((1, rim), jnp.int32)],
        edge_counts, edge_source.reshape(rows, LANES), edge_target.reshape(rows, LANES),
        node_feats.T, node_cot.T, rim_upper, rim_lower,
        scratch=[VM((rows, LANES), jnp.int32), VM((rows, LANES), jnp.int32),
                 VM((width, latent), BF), VM((width, latent), F32), pltpu.SemaphoreType.DMA((6,))],
        smem=1, hbm=range(1, 7),
    )
    packs = layer_parts(packed)
    upper, lower, alpha_pick, beta_pick = call(
        pick_kernel,
        [((slab, rim), BF), ((slab, rim), BF), ((slab, room), BF), ((slab, room), BF)],
        packed, upper, lower, cost=0.1,
    )
    later, _ = lax.optimization_barrier((edge_feats, alpha_pick))
    parts = [edge_feats] + layer_parts(later)[1:]
    slab_zero, cot, alpha, beta = call(
        functools.partial(slab_kernel, groups, rows),
        [per_hit(BF), per_hit(F32), rim_shape, rim_shape], *packs, alpha_pick, beta_pick, cost=20.0,
    )
    beta = by_beta(beta)
    alpha = by_alpha(alpha)
    (onehot, base, count, table, first_back, second_back, node_first_back, node_second_back, bias,
     to_node, to_node_back, to_table, to_table_back, to_hidden, alpha_place, beta_place) = call(
        functools.partial(onehot_kernel, groups, rows, rim),
        [((wide + slab, total_slots), BF), per_slot(F32), ((8, slab), F32), per_hit(F32),
         (edge_first.shape[::-1], BF), (edge_second.shape[::-1], BF),
         (node_first.shape[::-1], BF), (node_second.shape[::-1], BF), (biases.shape[::-1], F32)]
        + [((hidden, 3 * hidden), BF)] * 5 + [((2 * slab, 2 * room), BF)] * 2,
        *packs, slab_zero, edge_first, edge_second, node_first, node_second, biases, alpha_pick, beta_pick, cost=2.0,
    )
    edges_zero, base, message, node_base_zero = call(
        functools.partial(start_kernel, groups),
        [per_slot(BF), per_slot(F32), per_hit(F32), per_hit(F32)],
        *parts, base, onehot, slab_zero, count, edge_first, node_first, bias, cost=1.0,
    )
    (hidden_zero, slope, rims_zero, sums_zero, node_pre_zero, node_hidden_zero, slab_one, table,
     alpha, beta) = call(
        forward_kernel,
        [per_slot(BF), per_slot(F32), rim_shape, per_hit(F32), per_hit(F32), per_hit(BF), per_hit(BF), per_hit(F32),
         ((latent, 2 * room), BF), ((latent, 2 * room), BF)],
        base, onehot, slab_zero, beta, alpha, node_base_zero, table, edge_first, node_second, bias, to_node, to_table,
        alpha_place, beta_place, cost=2.0,
    )
    beta = by_beta(beta)
    alpha = by_alpha(alpha)
    edges_one, base, message, joined_zero, node_base_one = call(
        between_kernel, [per_slot(BF), per_slot(F32), per_hit(F32), per_hit(BF, 2), per_hit(F32)],
        edges_zero, hidden_zero, onehot, slab_zero, slab_one, table, sums_zero, message, count,
        edge_first, edge_second, node_first, bias, cost=2.0,
    )
    total_width = edge_first.shape[1] + hidden + node_first.shape[1] + node_second.shape[1] + 4
    lanes = -(-(total_width + 2 * rim) // LANES) * LANES
    hidden_one, low, sums_one, node_pre_one, node_grad_one, wanted, first_sums, rims = call(
        middle_kernel,
        [per_slot(BF), per_slot(BF), per_hit(F32), per_hit(F32), per_hit(F32), per_hit(F32),
         ((hidden, wide + slab + latent), F32), rim_shape],
        base, onehot, edges_one, beta, alpha, node_base_one, cot, node_second_back, to_node, to_node_back,
        scratch=[VM((hidden, total_slots), F32)], cost=3.0,
    )
    beta = by_beta(rims)
    alpha = by_alpha(rims)
    extra, total, joined_one, back, back_node = call(
        functools.partial(carry_kernel, rim),
        [per_slot(F32), ((latent, lanes), F32), per_hit(BF, 2), per_hit(F32), per_hit(F32)],
        low, hidden_zero, slab_one, sums_one, sums_zero, message, node_pre_one, node_grad_one, first_sums, count, cot,
        edge_second, first_back, node_first_back, node_second_back, to_hidden, cost=2.0,
    )
    edge_out, node_out = call(
        output_kernel, [((latent, slots), BF), ((width, latent), BF)],
        edge_counts, edges_one, hidden_one, joined_one, node_pre_one, edge_second, node_second, bias,
        scratch=[VM((latent, total_slots), BF)], smem=1, cost=2.0,
    )
    total, back = call(
        functools.partial(last_kernel, rim), [((latent, lanes), BF), per_hit(F32)],
        back, back_node, beta, alpha, alpha_pick, beta_pick, joined_zero, node_pre_zero, node_hidden_zero, wanted,
        sums_zero, count, extra, slope, onehot, edges_zero, slab_zero, rims_zero, slab_one, total,
        first_back, node_first_back, to_node_back, to_table_back, cost=2.0,
    )
    other = by_alpha(total)
    alpha_last = other
    bit = 1
    while 2 * bit < ring:
        total = call(
            functools.partial(add_kernel, total_width, rim, bit), [((latent, lanes), BF)], total, other, cost=0.1,
        )[0]
        bit *= 2
        other = swap(total, "phi", lambda index, bit=bit: index ^ bit)
    node_grad, edge_one, edge_two, node_one, node_two, bias_out = call(
        functools.partial(finish_kernel, total_width, rim),
        [((width, latent), F32), (edge_first.shape, F32), (edge_second.shape, F32),
         (node_first.shape, F32), (node_second.shape, F32), (biases.shape, F32)],
        total, other, back, alpha_last, upper, lower,
    )
    return node_out.T, edge_out, node_grad.T, edge_one, edge_two, node_one, node_two, bias_out


def solution(mesh):
    split = P(None, ("phi", "layer"))
    return jax.shard_map(
        body,
        mesh=mesh,
        in_specs=(split, split, P(("phi", "layer")), P(("phi", "layer")), P("phi", "layer"),
                  P("phi", None), P("phi", None), P(), P(), P(), P(), P(), split),
        out_specs=(split, split, split, P(), P(), P(), P(), P()),
        check_vma=False,
    )
```

```python
import functools
import math

import jax
import jax.numpy as jnp
from jax import lax
from jax.experimental import pallas as pl
from jax.experimental.pallas import tpu as pltpu
from jax.sharding import PartitionSpec as P

BF = jnp.bfloat16
F32 = jnp.float32
CHUNK = 512
LANES = 128
HBM = pltpu.HBM
VM = pltpu.VMEM


def mm(left, right):
    return jnp.dot(left, right, preferred_element_type=F32)


def mm_nt(left, right):
    return lax.dot_general(left, right, (((1,), (1,)), ((), ())), preferred_element_type=F32)


def flip(weight):
    return weight.astype(F32).T.astype(BF)


def halves(value):
    high = value.astype(BF)
    return high, (value - high.astype(F32)).astype(BF)


def wide_mm(weight, value):
    high, low = halves(value)
    return mm(jnp.concatenate([weight, weight], axis=1), jnp.concatenate([high, low], axis=0))


def sigmoid(value):
    return 0.5 + 0.5 * jnp.tanh(0.5 * value)


def add_to(total, value):
    return value if total is None else total + value


def chunks_of(count):
    return [slice(first, first + CHUNK) for first in range(0, count, CHUNK)]


def is_even():
    return lax.rem(lax.axis_index("phi"), 2) == 0


def pick(parts, natural):
    groups = len(parts)
    turn = lax.rem(lax.axis_index("layer") - natural + groups, groups)
    value = parts[0]
    for rank in range(1, groups):
        value = jnp.where(turn == rank, parts[rank], value)
    return value


def own_rows(slab_rows, width):
    layer = lax.axis_index("layer")
    value = slab_rows[:width]
    for rank in range(1, slab_rows.shape[0] // width):
        value = jnp.where(layer == rank, slab_rows[rank * width : (rank + 1) * width], value)
    return value


def split(value):
    high, low = halves(value)
    return jnp.concatenate([high, high, low], axis=1)


def split_mm(table, value):
    high, low = halves(value)
    return mm(table, jnp.concatenate([high, low, high], axis=0))


def pair_mm(table, value):
    return mm(table[:, value.shape[0] :], jnp.concatenate([value, value], axis=0))


def placed_rims(alpha, beta, upper_ref, lower_ref):
    even = is_even()
    from_upper = jnp.where(even, alpha, beta).astype(BF)
    from_lower = jnp.where(even, beta, alpha).astype(BF)
    return mm_nt(from_upper, upper_ref[...]) + mm_nt(from_lower, lower_ref[...])


def rim_gradients(ext_grad, slab, rim):
    even = is_even()
    below = ext_grad[:, slab : slab + rim]
    above = ext_grad[:, slab + rim : slab + 2 * rim]
    return jnp.where(even, above, below), jnp.where(even, below, above)


def slope_parts(pre):
    logistic = sigmoid(pre)
    value = pre * logistic
    return value, logistic + value * (1.0 - logistic)


def activate(base_ref, table, onehot_ref, slab, hidden_ref, slope_ref):
    wide = onehot_ref.shape[0] - slab
    for cols in chunks_of(base_ref.shape[1]):
        rims = onehot_ref[slab:wide, cols]
        pre = base_ref[:, cols] + mm(table, jnp.concatenate([rims, rims], axis=0))
        value, slope = slope_parts(pre)
        hidden = value.astype(BF)
        hidden_ref[:, cols] = hidden
        slope_ref[:, cols] = slope
    return mm_nt(hidden_ref[...], onehot_ref[wide:])


def slab_base(source, target, own, bias, onehot_ref, edges_ref, base_ref):
    slab = source.shape[1]
    wide = onehot_ref.shape[0] - slab
    table = jnp.concatenate([*halves(source), *halves(target), own], axis=1)
    for cols in chunks_of(base_ref.shape[1]):
        near = onehot_ref[:slab, cols]
        hit = onehot_ref[wide:, cols]
        stack = jnp.concatenate([near, near, hit, hit, edges_ref[:, cols]], axis=0)
        base_ref[:, cols] = mm(table, stack) + bias[:, 0:1]


def node_base(state16, message, first_ref, bias):
    latent = state16.shape[0]
    return (
        mm(first_ref[:, :latent], state16)
        + wide_mm(first_ref[:, latent:], message)
        + bias[:, 2:3]
    )


def node_sums(grad, pre_grad, joined, hidden):
    return (
        mm_nt(pre_grad.astype(BF), joined),
        mm_nt(grad.astype(BF), hidden),
        jnp.sum(pre_grad, axis=1, keepdims=True),
        jnp.sum(grad, axis=1, keepdims=True),
    )


def prep_kernel(count_ref, source_hbm, target_hbm, feats_hbm, cot_hbm, upper_hbm, lower_hbm,
                out_ref, upper_ref, lower_ref, source, target, feats, cot, sems):
    pairs = ((source_hbm, source), (target_hbm, target), (feats_hbm, feats), (cot_hbm, cot),
             (upper_hbm, upper_ref), (lower_hbm, lower_ref))
    copies = [pltpu.make_async_copy(a, b, sems.at[place]) for place, (a, b) in enumerate(pairs)]
    for copy in copies:
        copy.start()
    for copy in copies:
        copy.wait()
    rows = source.shape[0]
    position = lax.broadcasted_iota(jnp.int32, (rows, LANES), 0) * LANES + lax.broadcasted_iota(
        jnp.int32, (rows, LANES), 1
    )
    valid = position < count_ref[0, 0]
    index = source[...]
    out_ref[:rows] = jnp.where(valid, index // LANES, -1).astype(F32).astype(BF)
    out_ref[rows : 2 * rows] = (index % LANES).astype(F32).astype(BF)
    out_ref[2 * rows : 3 * rows] = jnp.where(valid, target[...], -1).astype(F32).astype(BF)
    out_ref[3 * rows :] = jnp.concatenate([feats[...].astype(F32), cot[...]], axis=1).astype(BF)


def pick_kernel(packed_ref, upper, lower, upper_ref, lower_ref, alpha_pick, beta_pick):
    hits = lax.broadcasted_iota(jnp.int32, upper_ref.shape, 0)
    upper_ref[...] = (hits == upper[...]).astype(F32).astype(BF)
    lower_ref[...] = (hits == lower[...]).astype(F32).astype(BF)
    slab, room = alpha_pick.shape
    rim = upper.shape[1]
    first = jnp.concatenate([upper[...], jnp.full((1, room - rim), -1, jnp.int32)], axis=1)
    second = jnp.concatenate(
        [jnp.full((1, rim), -1, jnp.int32), lower[...], jnp.full((1, room - 2 * rim), -1, jnp.int32)], axis=1
    )
    even = is_even()
    hits = lax.broadcasted_iota(jnp.int32, (slab, room), 0)
    alpha_pick[...] = (hits == jnp.where(even, first, second)).astype(F32).astype(BF)
    beta_pick[...] = (hits == jnp.where(even, second, first)).astype(F32).astype(BF)


def slab_kernel(groups, rows, *refs):
    packs = [ref[3 * rows :].astype(F32) for ref in refs[:groups]]
    alpha_pick, beta_pick, slab_ref, cot_ref, alpha_ref, beta_ref = refs[groups:]
    latent = slab_ref.shape[0]
    both = jnp.concatenate([pick(packs, rank) for rank in range(groups)], axis=0).T
    slab16 = both[:latent].astype(BF)
    slab_ref[...] = slab16
    cot_ref[...] = both[latent:]
    alpha_ref[...] = mm(slab16, alpha_pick[...]).astype(BF)
    beta_ref[...] = mm(slab16, beta_pick[...]).astype(BF)


def onehot_kernel(groups, rows, rim, *refs):
    packs = [ref[: 3 * rows].astype(F32) for ref in refs[:groups]]
    (slab_ref, first_ref, second_ref, node_first_ref, node_second_ref, bias_ref, alpha_pick, beta_pick,
     onehot_ref, base_ref, count_ref, table_ref, first_back, second_back, node_first_back, node_second_back, bias_out,
     to_node, to_node_back, to_table, to_table_back, to_hidden, alpha_place, beta_place) = refs[groups:]
    latent = first_ref.shape[0]
    slab, room = alpha_pick.shape
    wide = slab + room
    source_rows = lax.broadcasted_iota(jnp.int32, (wide, LANES), 0).astype(F32)
    target_rows = lax.broadcasted_iota(jnp.int32, (slab, LANES), 0).astype(F32)
    ones_row = source_rows == float(slab + 2 * rim)
    for rank in range(groups):
        pack = pick(packs, rank)
        source = jnp.where(pack[:rows] < 0.0, -1.0, pack[:rows] * LANES + pack[rows : 2 * rows])
        target = pack[2 * rows :]
        for row in range(rows):
            cols = slice((rank * rows + row) * LANES, (rank * rows + row + 1) * LANES)
            match = (source_rows == source[row : row + 1]) | ones_row
            onehot_ref[:wide, cols] = jnp.where(match, 1.0, 0.0).astype(BF)
            onehot_ref[wide:, cols] = jnp.where(target_rows == target[row : row + 1], 1.0, 0.0).astype(BF)
    bias = bias_ref[...].T
    bias_out[...] = bias
    slab16 = slab_ref[...]
    source = mm(first_ref[:, :latent], slab16)
    target = mm(first_ref[:, latent : 2 * latent], slab16)
    shift = wide_mm(first_ref[:, :latent], jnp.broadcast_to(bias[:, 3:4], (latent, LANES)))
    table_ref[...] = source + shift[:, :1]
    table = jnp.concatenate([*halves(source), *halves(target)], axis=1)
    count = None
    for cols in chunks_of(base_ref.shape[1]):
        near = onehot_ref[:slab, cols]
        hit = onehot_ref[wide:, cols]
        base_ref[:, cols] = mm(table, jnp.concatenate([near, near, hit, hit], axis=0)) + bias[:, 0:1]
        count = add_to(count, mm_nt(jnp.ones((16, CHUNK), BF), hit))
    count_ref[...] = count[:8]
    first_back[...] = flip(first_ref[...])
    second_back[...] = flip(second_ref[...])
    node_first_back[...] = flip(node_first_ref[...])
    node_second_back[...] = flip(node_second_ref[...])
    forward = mm(node_first_ref[:, latent:], second_ref[...])
    to_node[...] = split(forward)
    to_node_back[...] = split(forward.T)
    table = mm(first_ref[:, :latent], node_second_ref[...])
    to_table[...] = split(table)
    to_table_back[...] = split(table.T)
    to_hidden[...] = split(mm(first_ref[:, 2 * latent :], second_ref[...]).T)
    for choose, place in ((alpha_pick, alpha_place), (beta_pick, beta_place)):
        block = choose[...].astype(F32)
        none = jnp.zeros_like(block)
        place[...] = jnp.concatenate(
            [jnp.concatenate([block, none], axis=1), jnp.concatenate([none, block], axis=1)], axis=0
        ).astype(BF)


def start_kernel(groups, *refs):
    parts = refs[:groups]
    (base_in, onehot_ref, slab_ref, count_ref, first_ref, node_first_ref, bias_ref,
     edges_ref, base_ref, message_ref, node_base_ref) = refs[groups:]
    latent, slab = slab_ref.shape
    wide = onehot_ref.shape[0] - slab
    slots = parts[0].shape[1]
    own = first_ref[:, 2 * latent :]
    message = None
    for rank in range(groups):
        for cols in chunks_of(slots):
            here = slice(rank * slots + cols.start, rank * slots + cols.stop)
            edges = pick([part[:, cols] for part in parts], rank)
            edges_ref[:, here] = edges
            base_ref[:, here] = base_in[:, here] + mm(own, edges)
            message = add_to(message, mm_nt(edges, onehot_ref[wide:, here]))
    bias = bias_ref[...]
    message = message + bias[:, 1:2] * count_ref[0:1]
    message_ref[...] = message
    node_base_ref[...] = node_base(slab_ref[...], message, node_first_ref, bias)


def forward_kernel(base_ref, onehot_ref, slab_ref, beta_in, alpha_in, node_base_ref, table_in,
                   first_ref, node_second_ref, bias_ref, to_node, to_table, alpha_place, beta_place,
                   hidden_ref, slope_ref, rims_ref, sums_ref, node_pre_ref, node_hidden_ref, state_ref, table_ref,
                   alpha_ref, beta_ref):
    latent, slab = slab_ref.shape
    rims16 = alpha_in[...] + beta_in[...]
    rims_ref[...] = rims16
    table = jnp.concatenate(halves(mm(first_ref[:, :latent], rims16)), axis=1)
    sums = activate(base_ref, table, onehot_ref, slab, hidden_ref, slope_ref)
    sums_ref[...] = sums
    node_pre = node_base_ref[...] + split_mm(to_node[...], sums)
    node_pre_ref[...] = node_pre
    node_hidden = slope_parts(node_pre)[0].astype(BF)
    node_hidden_ref[...] = node_hidden
    table = table_in[...] + pair_mm(to_table[...], node_hidden)
    table_ref[...] = table
    both = jnp.concatenate(halves(table), axis=1)
    alpha_ref[...] = mm(both, alpha_place[...]).astype(BF)
    beta_ref[...] = mm(both, beta_place[...]).astype(BF)
    state = slab_ref[...].astype(F32) + mm(node_second_ref[...], node_hidden) + bias_ref[:, 3:4]
    state_ref[...] = state.astype(BF)


def between_kernel(edges_ref, hidden_ref, onehot_ref, slab_in, state_ref, table_ref, sums_ref, message_in, count_ref,
                   first_ref, second_ref, node_first_ref, bias_ref,
                   new_ref, base_ref, message_ref, joined_ref, node_base_ref):
    latent = edges_ref.shape[0]
    bias = bias_ref[...]
    second = second_ref[...]
    for cols in chunks_of(edges_ref.shape[1]):
        new_ref[:, cols] = (
            edges_ref[:, cols].astype(F32) + mm(second, hidden_ref[:, cols]) + bias[:, 1:2]
        ).astype(BF)
    state16 = state_ref[...]
    target = mm(first_ref[:, latent : 2 * latent], state16)
    slab_base(table_ref[...], target, first_ref[:, 2 * latent :], bias, onehot_ref, new_ref, base_ref)
    message = message_in[...] + wide_mm(second, sums_ref[...])
    joined_ref[...] = jnp.concatenate([slab_in[...], message.astype(BF)], axis=0)
    message = message + bias[:, 1:2] * count_ref[0:1]
    message_ref[...] = message
    node_base_ref[...] = node_base(state16, message, node_first_ref, bias)


def edge_gradient(wanted, extra_ref, slope_ref, onehot_ref, edges_ref, low_ref):
    slab = wanted.shape[1]
    wide = onehot_ref.shape[0] - slab
    table = jnp.concatenate(halves(wanted), axis=1)
    for cols in chunks_of(edges_ref.shape[1]):
        hit = onehot_ref[wide:, cols]
        grad = mm(table, jnp.concatenate([hit, hit], axis=0))
        if extra_ref is not None:
            grad = grad + extra_ref[:, cols]
        low_ref[:, cols] = (grad * slope_ref[:, cols]).astype(BF)
    return mm_nt(low_ref[...], jnp.concatenate([onehot_ref[...], edges_ref[...]], axis=0))


def middle_kernel(base_ref, onehot_ref, edges_ref, beta_in, alpha_in, node_base_ref, cot_ref,
                  node_second_back, to_node, to_node_back,
                  hidden_ref, low_ref, sums_ref, node_pre_ref, node_grad_ref, wanted_ref, first_sums_ref, rims_ref,
                  slope_ref):
    slab = cot_ref.shape[1]
    wide = onehot_ref.shape[0] - slab
    cot_grad = mm(node_second_back[...], cot_ref[...].astype(BF))
    sums = activate(base_ref, alpha_in[...] + beta_in[...], onehot_ref, slab, hidden_ref, slope_ref)
    sums_ref[...] = sums
    node_pre = node_base_ref[...] + split_mm(to_node[...], sums)
    node_pre_ref[...] = node_pre
    pre_grad = cot_grad * slope_parts(node_pre)[1]
    node_grad_ref[...] = pre_grad
    wanted = split_mm(to_node_back[...], pre_grad)
    wanted_ref[...] = wanted
    first_sums = edge_gradient(wanted, None, slope_ref, onehot_ref, edges_ref, low_ref)
    rims_ref[...] = first_sums[:, slab:wide].astype(BF)
    first_sums_ref[...] = first_sums


def carry_kernel(rim, low_ref, hidden_zero_ref, slab_ref, sums_ref, sums_zero_ref, message_in,
                 node_pre_ref, node_grad_ref, first_sums_ref, count_ref, cot_ref,
                 second_ref, first_back, node_first_back, node_second_back, to_hidden,
                 extra_ref, total_ref, joined_ref, back_ref, back_node_ref):
    latent, slab = slab_ref.shape
    wide = first_sums_ref.shape[1] - slab - latent
    sums = first_sums_ref[...]
    cot = cot_ref[...]
    pre_grad = node_grad_ref[...]
    node_back = mm(node_first_back[...], pre_grad.astype(BF))
    gm = node_back[latent:].astype(BF)
    source = sums[:, :slab].astype(BF)
    target = sums[:, wide : wide + slab].astype(BF)
    back = cot + node_back[:latent] + mm(first_back[:latent], source) + mm(first_back[latent : 2 * latent], target)
    back_ref[...] = back
    back_node_ref[...] = wide_mm(node_second_back[...], back)
    self_back = first_back[2 * latent :]
    cross = None
    for cols in chunks_of(low_ref.shape[1]):
        low = low_ref[:, cols]
        extra_ref[:, cols] = pair_mm(to_hidden[...], low)
        cross = add_to(cross, mm_nt(low, hidden_zero_ref[:, cols]))
    slab16 = slab_ref[...]
    message = message_in[...] + wide_mm(second_ref[...], sums_ref[...])
    joined = jnp.concatenate([slab16, message.astype(BF)], axis=0)
    joined_ref[...] = joined
    pre_sum = sums[:, slab + 2 * rim : slab + 2 * rim + 1]
    edge_two = (
        mm_nt(gm, sums_ref[...].astype(BF))
        + mm_nt(gm, sums_zero_ref[...].astype(BF))
        + mm(self_back, cross.astype(BF))
    )
    gm_sum = 2.0 * jnp.sum(gm.astype(F32) * count_ref[0:1], axis=1, keepdims=True) + wide_mm(
        self_back, jnp.broadcast_to(pre_sum, (latent, LANES))
    )[:, :1]
    node_one, node_two, node_pre_sum, cot_sum = node_sums(
        cot, pre_grad, joined, slope_parts(node_pre_ref[...])[0].astype(BF)
    )
    edge_one = jnp.concatenate(
        [mm_nt(source, slab16), mm_nt(target, slab16), sums[:, wide + slab :]], axis=1
    )
    total_ref[...] = jnp.concatenate(
        [edge_one, edge_two, node_one, node_two, pre_sum, gm_sum, node_pre_sum, cot_sum], axis=1
    )


def output_kernel(count_ref, edges_ref, hidden_ref, joined_ref, node_pre_ref, second_ref, node_second_ref, bias_ref,
                  edge_out, node_out, done_ref, new_ref):
    bias = bias_ref[...]
    latent = edges_ref.shape[0]
    second = second_ref[...]
    for cols in chunks_of(edges_ref.shape[1]):
        new_ref[:, cols] = (
            edges_ref[:, cols].astype(F32) + mm(second, hidden_ref[:, cols]) + bias[:, 1:2]
        ).astype(BF)
    slots = edge_out.shape[1]
    begin = lax.axis_index("layer") * slots
    for cols in chunks_of(slots):
        position = lax.broadcasted_iota(jnp.int32, (latent, CHUNK), 1) + cols.start
        mine = new_ref[:, pl.ds(pl.multiple_of(begin + cols.start, CHUNK), CHUNK)].astype(F32)
        edge_out[:, cols] = jnp.where(position < count_ref[0, 0], mine, 0.0).astype(BF)
    node_hidden = slope_parts(node_pre_ref[...])[0].astype(BF)
    state = joined_ref[:latent].astype(F32) + mm(node_second_ref[...], node_hidden) + bias[:, 3:4]
    node_out[...] = own_rows(state.T, node_out.shape[0]).astype(BF)
    done_ref[...] = jnp.zeros_like(done_ref)


def last_kernel(rim, back_in, back_node, beta_in, alpha_in, alpha_pick, beta_pick, joined_ref, node_pre_ref,
                node_hidden_ref, wanted_in, sums_ref, count_ref, extra_ref, slope_ref, onehot_ref, edges_ref,
                slab_ref, rims_ref, slab_one_ref, total_in, first_back, node_first_back, to_node_back, to_table_back,
                total_ref, back_ref, low_ref):
    latent, slab = slab_ref.shape
    wide = onehot_ref.shape[0] - slab
    placed = mm_nt(alpha_in[...], alpha_pick[...]) + mm_nt(beta_in[...], beta_pick[...])
    pre_grad = (back_node[...] + split_mm(to_table_back[...], placed)) * slope_parts(node_pre_ref[...])[1]
    wanted = wanted_in[...] + split_mm(to_node_back[...], pre_grad)
    sums = edge_gradient(wanted, extra_ref, slope_ref, onehot_ref, edges_ref, low_ref)
    source = sums[:, :wide].astype(BF)
    target = sums[:, wide : wide + slab].astype(BF)
    ext_grad = mm(first_back[:latent], source)
    node_back = mm(node_first_back[...], pre_grad.astype(BF))
    gm = node_back[latent:].astype(BF)
    grad = back_in[...] + wide_mm(first_back[:latent], placed)
    back_ref[...] = (
        grad + node_back[:latent] + ext_grad[:, :slab] + mm(first_back[latent : 2 * latent], target)
    )
    alpha, beta = rim_gradients(ext_grad, slab, rim)
    node_one, node_two, node_pre_sum, grad_sum = node_sums(grad, pre_grad, joined_ref[...], node_hidden_ref[...])
    slab16 = slab_ref[...]
    ext16 = jnp.concatenate([slab16, rims_ref[...]], axis=1)
    edge_one = jnp.concatenate(
        [
            mm_nt(source, ext16) + mm_nt(placed.astype(BF), slab_one_ref[...]),
            mm_nt(target, slab16),
            sums[:, wide + slab :],
        ],
        axis=1,
    )
    edge_two = mm_nt(gm, sums_ref[...].astype(BF))
    pre_sum = sums[:, slab + 2 * rim : slab + 2 * rim + 1]
    gm_sum = jnp.sum(gm.astype(F32) * count_ref[0:1], axis=1, keepdims=True)
    total = total_in[...] + jnp.concatenate(
        [edge_one, edge_two, node_one, node_two, pre_sum, gm_sum, node_pre_sum, grad_sum], axis=1
    )
    total_ref[...] = padded([total, alpha, beta], total_ref.shape[1]).astype(BF)


def padded(pieces, width):
    spare = width - sum(piece.shape[1] for piece in pieces)
    if spare:
        pieces = pieces + [jnp.zeros((pieces[0].shape[0], spare), F32)]
    return jnp.concatenate(pieces, axis=1)


def even_chip():
    return lax.rem(lax.axis_index("phi") // 2, 2) == 0


def open_kernel(used, rim, mine_ref, other_ref, out_ref):
    mine = mine_ref[...].astype(F32)
    other = other_ref[...].astype(F32)
    up = mine[:, used + rim : used + 2 * rim]
    down = other[:, used + rim : used + 2 * rim]
    near = jnp.where(even_chip(), up, down)
    far = jnp.where(even_chip(), down, up)
    out_ref[...] = padded([mine[:, :used] + other[:, :used], near, far], out_ref.shape[1]).astype(BF)


def pass_kernel(used, rim, mine_ref, other_ref, out_ref, near_ref):
    mine = mine_ref[...].astype(F32)
    other = other_ref[...].astype(F32)
    near_ref[...] = other[:, used : used + rim]
    out_ref[...] = padded(
        [mine[:, :used] + other[:, :used], other[:, used + rim : used + 2 * rim]], out_ref.shape[1]
    ).astype(BF)


def add_kernel(used, rim, bit, mine_ref, other_ref, out_ref, far_ref):
    mine = mine_ref[...].astype(F32)
    other = other_ref[...].astype(F32)
    place = lax.axis_index("phi")
    home = (lax.rem(place // bit, 2) == 1) == even_chip()
    lane = lax.broadcasted_iota(jnp.int32, other.shape, 1)
    far_ref[...] = jnp.where(home, other[:, used : used + rim], 0.0)
    out_ref[...] = jnp.where(lane < used, mine + other, jnp.where(home, 0.0, other)).astype(BF)


def close_kernel(used, rim, mine_ref, other_ref, near_ref, done_ref, *refs):
    mine = mine_ref[...].astype(F32)
    other = other_ref[...].astype(F32)
    far = other[:, used : used + rim]
    for ref in refs[:-2]:
        far = far + ref[...]
    out_ref, down_ref = refs[-2:]
    near = near_ref[...]
    down_ref[...] = jnp.where(even_chip(), near, far)
    up = jnp.where(even_chip(), far, near)
    out_ref[...] = padded([mine[:, :used] + other[:, :used], up], out_ref.shape[1]).astype(BF)


def finish_kernel(used, rim, mine_ref, sent_ref, down_ref, first_ref, back_ref, upper_ref, lower_ref,
                  node_grad, edge_one, edge_two, node_one, node_two, bias_out):
    even = is_even()
    sent = sent_ref[...].astype(F32)
    total = jnp.where(even, sent, mine_ref[...].astype(F32))
    cut = 0
    for ref in (edge_one, edge_two, node_one, node_two):
        ref[...] = total[:, cut : cut + ref.shape[1]]
        cut += ref.shape[1]
    block = used - 4 - (used - 4) % LANES
    turned = total[:, block : block + LANES].T
    bias_out[...] = turned[used - 4 - block : used - block]
    alpha = first_ref[...].astype(F32)[:, used : used + rim]
    beta = jnp.where(even, sent[:, used : used + rim], down_ref[...])
    grad = back_ref[...] + placed_rims(alpha, beta, upper_ref, lower_ref)
    node_grad[...] = own_rows(grad.T, node_grad.shape[0])


def call(kernel, outs, *args, scratch=(), smem=0, hbm=(), cost=1.0):
    args = [
        pltpu.with_memory_space_constraint(arg, HBM) if place in hbm else arg for place, arg in enumerate(args)
    ]
    held = [(arg.shape, arg.dtype) for arg in args] + list(outs)
    held += [(ref.shape, ref.dtype) for ref in scratch if jnp.issubdtype(ref.dtype, jnp.number)]
    room = sum(math.prod(shape) * jnp.dtype(kind).itemsize for shape, kind in held)
    spaces = [pltpu.SMEM if place < smem else HBM if place in hbm else VM for place in range(len(args))]
    specs = [pl.BlockSpec(memory_space=space) for space in spaces]
    return pl.pallas_call(
        kernel,
        out_shape=[jax.ShapeDtypeStruct(shape, kind) for shape, kind in outs],
        in_specs=specs,
        out_specs=[pl.BlockSpec(memory_space=VM) for _ in outs],
        scratch_shapes=list(scratch),
        compiler_params=pltpu.CompilerParams(vmem_limit_bytes=room + 10 * 1024 * 1024),
        cost_estimate=pl.CostEstimate(
            flops=int(cost * 1e9), bytes_accessed=int(cost * 3.6e6), transcendentals=0
        ),
    )(*args)


def swap(value, axis, pairing):
    count = lax.axis_size(axis)
    return lax.ppermute(value, axis, [(source, pairing(source) % count) for source in range(count)])


def by_alpha(value):
    return swap(value, "phi", lambda index: index ^ 1)


def by_beta(value):
    return swap(value, "phi", lambda index: index - 1 if index % 2 == 0 else index + 1)


def by_chips(value, bit):
    return swap(value, "phi", lambda index: index ^ bit if index % 2 else index)


def layer_parts(value):
    groups = lax.axis_size("layer")
    return [value] + [
        swap(value, "layer", lambda index, turn=turn: index + turn) for turn in range(1, groups)
    ]


def body(node_feats, edge_feats, edge_source, edge_target, edge_counts, rim_upper, rim_lower,
         edge_first, edge_second, node_first, node_second, biases, node_cot):
    groups = lax.axis_size("layer")
    ring = lax.axis_size("phi")
    latent, width = node_feats.shape
    hidden = edge_second.shape[1]
    slots = edge_feats.shape[1]
    slab = width * groups
    rim = rim_upper.shape[1]
    wide = (slab + 2 * rim) // LANES * LANES + LANES
    total_slots = slots * groups
    rows = slots // LANES
    room = wide - slab
    rim_shape = ((latent, room), BF)
    per_slot = lambda kind: ((latent, total_slots), kind)
    per_hit = lambda kind, depth=1: ((depth * latent, slab), kind)

    packed, upper, lower = call(
        prep_kernel,
        [((3 * rows + width, LANES), BF), ((1, rim), jnp.int32), ((1, rim), jnp.int32)],
        edge_counts, edge_source.reshape(rows, LANES), edge_target.reshape(rows, LANES),
        node_feats.T, node_cot.T, rim_upper, rim_lower,
        scratch=[VM((rows, LANES), jnp.int32), VM((rows, LANES), jnp.int32),
                 VM((width, latent), BF), VM((width, latent), F32), pltpu.SemaphoreType.DMA((6,))],
        smem=1, hbm=range(1, 7),
    )
    packs = layer_parts(packed)
    upper, lower, alpha_pick, beta_pick = call(
        pick_kernel,
        [((slab, rim), BF), ((slab, rim), BF), ((slab, room), BF), ((slab, room), BF)],
        packed, upper, lower, cost=0.1,
    )
    later, _ = lax.optimization_barrier((edge_feats, alpha_pick))
    parts = [edge_feats] + layer_parts(later)[1:]
    slab_zero, cot, alpha, beta = call(
        functools.partial(slab_kernel, groups, rows),
        [per_hit(BF), per_hit(F32), rim_shape, rim_shape], *packs, alpha_pick, beta_pick, cost=20.0,
    )
    beta = by_beta(beta)
    alpha = by_alpha(alpha)
    (onehot, base, count, table, first_back, second_back, node_first_back, node_second_back, bias,
     to_node, to_node_back, to_table, to_table_back, to_hidden, alpha_place, beta_place) = call(
        functools.partial(onehot_kernel, groups, rows, rim),
        [((wide + slab, total_slots), BF), per_slot(F32), ((8, slab), F32), per_hit(F32),
         (edge_first.shape[::-1], BF), (edge_second.shape[::-1], BF),
         (node_first.shape[::-1], BF), (node_second.shape[::-1], BF), (biases.shape[::-1], F32)]
        + [((hidden, 3 * hidden), BF)] * 5 + [((2 * slab, 2 * room), BF)] * 2,
        *packs, slab_zero, edge_first, edge_second, node_first, node_second, biases, alpha_pick, beta_pick, cost=2.0,
    )
    edges_zero, base, message, node_base_zero = call(
        functools.partial(start_kernel, groups),
        [per_slot(BF), per_slot(F32), per_hit(F32), per_hit(F32)],
        *parts, base, onehot, slab_zero, count, edge_first, node_first, bias, cost=1.0,
    )
    (hidden_zero, slope, rims_zero, sums_zero, node_pre_zero, node_hidden_zero, slab_one, table,
     alpha, beta) = call(
        forward_kernel,
        [per_slot(BF), per_slot(F32), rim_shape, per_hit(F32), per_hit(F32), per_hit(BF), per_hit(BF), per_hit(F32),
         ((latent, 2 * room), BF), ((latent, 2 * room), BF)],
        base, onehot, slab_zero, beta, alpha, node_base_zero, table, edge_first, node_second, bias, to_node, to_table,
        alpha_place, beta_place, cost=2.0,
    )
    beta = by_beta(beta)
    alpha = by_alpha(alpha)
    edges_one, base, message, joined_zero, node_base_one = call(
        between_kernel, [per_slot(BF), per_slot(F32), per_hit(F32), per_hit(BF, 2), per_hit(F32)],
        edges_zero, hidden_zero, onehot, slab_zero, slab_one, table, sums_zero, message, count,
        edge_first, edge_second, node_first, bias, cost=2.0,
    )
    total_width = edge_first.shape[1] + hidden + node_first.shape[1] + node_second.shape[1] + 4
    hidden_one, low, sums_one, node_pre_one, node_grad_one, wanted, first_sums, rims = call(
        middle_kernel,
        [per_slot(BF), per_slot(BF), per_hit(F32), per_hit(F32), per_hit(F32), per_hit(F32),
         ((hidden, wide + slab + latent), F32), rim_shape],
        base, onehot, edges_one, beta, alpha, node_base_one, cot, node_second_back, to_node, to_node_back,
        scratch=[VM((hidden, total_slots), F32)], cost=3.0,
    )
    beta = by_beta(rims)
    alpha = by_alpha(rims)
    extra, total, joined_one, back, back_node = call(
        functools.partial(carry_kernel, rim),
        [per_slot(F32), ((latent, total_width), F32), per_hit(BF, 2), per_hit(F32), per_hit(F32)],
        low, hidden_zero, slab_one, sums_one, sums_zero, message, node_pre_one, node_grad_one, first_sums, count, cot,
        edge_second, first_back, node_first_back, node_second_back, to_hidden, cost=2.0,
    )
    edge_out, node_out, done = call(
        output_kernel, [((latent, slots), BF), ((width, latent), BF), ((8, LANES), F32)],
        edge_counts, edges_one, hidden_one, joined_one, node_pre_one, edge_second, node_second, bias,
        scratch=[VM((latent, total_slots), BF)], smem=1, cost=2.0,
    )
    lanes = -(-(total_width + 2 * rim) // LANES) * LANES
    total, back = call(
        functools.partial(last_kernel, rim), [((latent, lanes), BF), per_hit(F32)],
        back, back_node, beta, alpha, alpha_pick, beta_pick, joined_zero, node_pre_zero, node_hidden_zero, wanted,
        sums_zero, count, extra, slope, onehot, edges_zero, slab_zero, rims_zero, slab_one, total,
        first_back, node_first_back, to_node_back, to_table_back,
        scratch=[VM((hidden, total_slots), BF)], cost=2.0,
    )
    payload = ((latent, lanes), BF)
    rim_block = ((latent, rim), F32)
    first = by_alpha(total)
    mine = call(functools.partial(open_kernel, total_width, rim), [payload], total, first, cost=0.1)[0]
    other = by_chips(mine, 2)
    mine, near = call(
        functools.partial(pass_kernel, total_width, rim), [payload, rim_block], mine, other, cost=0.1,
    )
    far = []
    bit = 4
    while 2 * bit < ring:
        other = by_chips(mine, bit)
        mine, block = call(
            functools.partial(add_kernel, total_width, rim, bit), [payload, rim_block], mine, other, cost=0.1,
        )
        far.append(block)
        bit *= 2
    other = by_chips(mine, bit)
    mine, down = call(
        functools.partial(close_kernel, total_width, rim), [payload, rim_block], mine, other, near, done, *far, cost=0.1,
    )
    sent = by_alpha(mine)
    node_grad, edge_one, edge_two, node_one, node_two, bias_out = call(
        functools.partial(finish_kernel, total_width, rim),
        [((width, latent), F32), (edge_first.shape, F32), (edge_second.shape, F32),
         (node_first.shape, F32), (node_second.shape, F32), (biases.shape, F32)],
        mine, sent, down, first, back, upper, lower,
    )
    return node_out.T, edge_out, node_grad.T, edge_one, edge_two, node_one, node_two, bias_out


def solution(mesh):
    split = P(None, ("phi", "layer"))
    return jax.shard_map(
        body,
        mesh=mesh,
        in_specs=(split, split, P(("phi", "layer")), P(("phi", "layer")), P("phi", "layer"),
                  P("phi", None), P("phi", None), P(), P(), P(), P(), P(), split),
        out_specs=(split, split, split, P(), P(), P(), P(), P()),
        check_vma=False,
    )
```

```python
import functools
import math

import jax
import jax.numpy as jnp
from jax import lax
from jax.experimental import pallas as pl
from jax.experimental.pallas import tpu as pltpu
from jax.sharding import PartitionSpec as P

BF = jnp.bfloat16
F32 = jnp.float32
CHUNK = 512
LANES = 128
HBM = pltpu.HBM
VM = pltpu.VMEM


def mm(left, right):
    return jnp.dot(left, right, preferred_element_type=F32)


def mm_nt(left, right):
    return lax.dot_general(left, right, (((1,), (1,)), ((), ())), preferred_element_type=F32)


def flip(weight):
    return weight.astype(F32).T.astype(BF)


def halves(value):
    high = value.astype(BF)
    return high, (value - high.astype(F32)).astype(BF)


def wide_mm(weight, value):
    high, low = halves(value)
    return mm(jnp.concatenate([weight, weight], axis=1), jnp.concatenate([high, low], axis=0))


def sigmoid(value):
    return 0.5 + 0.5 * jnp.tanh(0.5 * value)


def add_to(total, value):
    return value if total is None else total + value


def chunks_of(count):
    return [slice(first, first + CHUNK) for first in range(0, count, CHUNK)]


def is_even():
    return lax.rem(lax.axis_index("phi"), 2) == 0


def pick(parts, natural):
    groups = len(parts)
    turn = lax.rem(lax.axis_index("layer") - natural + groups, groups)
    value = parts[0]
    for rank in range(1, groups):
        value = jnp.where(turn == rank, parts[rank], value)
    return value


def own_rows(slab_rows, width):
    layer = lax.axis_index("layer")
    value = slab_rows[:width]
    for rank in range(1, slab_rows.shape[0] // width):
        value = jnp.where(layer == rank, slab_rows[rank * width : (rank + 1) * width], value)
    return value


def split(value):
    high, low = halves(value)
    return jnp.concatenate([high, high, low], axis=1)


def split_mm(table, value):
    high, low = halves(value)
    return mm(table, jnp.concatenate([high, low, high], axis=0))


def pair_mm(table, value):
    return mm(table[:, value.shape[0] :], jnp.concatenate([value, value], axis=0))


def placed_rims(alpha, beta, upper_ref, lower_ref):
    even = is_even()
    from_upper = jnp.where(even, alpha, beta).astype(BF)
    from_lower = jnp.where(even, beta, alpha).astype(BF)
    return mm_nt(from_upper, upper_ref[...]) + mm_nt(from_lower, lower_ref[...])


def rim_gradients(ext_grad, slab, rim):
    even = is_even()
    below = ext_grad[:, slab : slab + rim]
    above = ext_grad[:, slab + rim : slab + 2 * rim]
    return jnp.where(even, above, below), jnp.where(even, below, above)


def slope_parts(pre):
    logistic = sigmoid(pre)
    value = pre * logistic
    return value, logistic + value * (1.0 - logistic)


def activate(base_ref, table, onehot_ref, slab, hidden_ref, slope_ref):
    wide = onehot_ref.shape[0] - slab
    for cols in chunks_of(base_ref.shape[1]):
        rims = onehot_ref[slab:wide, cols]
        pre = base_ref[:, cols] + mm(table, jnp.concatenate([rims, rims], axis=0))
        value, slope = slope_parts(pre)
        hidden = value.astype(BF)
        hidden_ref[:, cols] = hidden
        slope_ref[:, cols] = slope
    return mm_nt(hidden_ref[...], onehot_ref[wide:])


def slab_base(source, target, own, bias, onehot_ref, edges_ref, base_ref):
    slab = source.shape[1]
    wide = onehot_ref.shape[0] - slab
    table = jnp.concatenate([*halves(source), *halves(target), own], axis=1)
    for cols in chunks_of(base_ref.shape[1]):
        near = onehot_ref[:slab, cols]
        hit = onehot_ref[wide:, cols]
        stack = jnp.concatenate([near, near, hit, hit, edges_ref[:, cols]], axis=0)
        base_ref[:, cols] = mm(table, stack) + bias[:, 0:1]


def node_base(state16, message, first_ref, bias):
    latent = state16.shape[0]
    return (
        mm(first_ref[:, :latent], state16)
        + wide_mm(first_ref[:, latent:], message)
        + bias[:, 2:3]
    )


def node_sums(grad, pre_grad, joined, hidden):
    return (
        mm_nt(pre_grad.astype(BF), joined),
        mm_nt(grad.astype(BF), hidden),
        jnp.sum(pre_grad, axis=1, keepdims=True),
        jnp.sum(grad, axis=1, keepdims=True),
    )


def prep_kernel(count_ref, source_hbm, target_hbm, feats_hbm, cot_hbm, upper_hbm, lower_hbm,
                out_ref, upper_ref, lower_ref, source, target, feats, cot, sems):
    pairs = ((source_hbm, source), (target_hbm, target), (feats_hbm, feats), (cot_hbm, cot),
             (upper_hbm, upper_ref), (lower_hbm, lower_ref))
    copies = [pltpu.make_async_copy(a, b, sems.at[place]) for place, (a, b) in enumerate(pairs)]
    for copy in copies:
        copy.start()
    for copy in copies:
        copy.wait()
    rows = source.shape[0]
    position = lax.broadcasted_iota(jnp.int32, (rows, LANES), 0) * LANES + lax.broadcasted_iota(
        jnp.int32, (rows, LANES), 1
    )
    valid = position < count_ref[0, 0]
    index = source[...]
    out_ref[:rows] = jnp.where(valid, index // LANES, -1).astype(F32).astype(BF)
    out_ref[rows : 2 * rows] = (index % LANES).astype(F32).astype(BF)
    out_ref[2 * rows : 3 * rows] = jnp.where(valid, target[...], -1).astype(F32).astype(BF)
    out_ref[3 * rows :] = jnp.concatenate([feats[...].astype(F32), cot[...]], axis=1).astype(BF)


def pick_kernel(packed_ref, upper, lower, upper_ref, lower_ref, alpha_pick, beta_pick):
    hits = lax.broadcasted_iota(jnp.int32, upper_ref.shape, 0)
    upper_ref[...] = (hits == upper[...]).astype(F32).astype(BF)
    lower_ref[...] = (hits == lower[...]).astype(F32).astype(BF)
    slab, room = alpha_pick.shape
    rim = upper.shape[1]
    first = jnp.concatenate([upper[...], jnp.full((1, room - rim), -1, jnp.int32)], axis=1)
    second = jnp.concatenate(
        [jnp.full((1, rim), -1, jnp.int32), lower[...], jnp.full((1, room - 2 * rim), -1, jnp.int32)], axis=1
    )
    even = is_even()
    hits = lax.broadcasted_iota(jnp.int32, (slab, room), 0)
    alpha_pick[...] = (hits == jnp.where(even, first, second)).astype(F32).astype(BF)
    beta_pick[...] = (hits == jnp.where(even, second, first)).astype(F32).astype(BF)


def slab_kernel(groups, rows, *refs):
    packs = [ref[3 * rows :].astype(F32) for ref in refs[:groups]]
    alpha_pick, beta_pick, slab_ref, cot_ref, alpha_ref, beta_ref = refs[groups:]
    latent = slab_ref.shape[0]
    both = jnp.concatenate([pick(packs, rank) for rank in range(groups)], axis=0).T
    slab16 = both[:latent].astype(BF)
    slab_ref[...] = slab16
    cot_ref[...] = both[latent:]
    alpha_ref[...] = mm(slab16, alpha_pick[...]).astype(BF)
    beta_ref[...] = mm(slab16, beta_pick[...]).astype(BF)


def onehot_kernel(groups, rows, rim, *refs):
    packs = [ref[: 3 * rows].astype(F32) for ref in refs[:groups]]
    (slab_ref, first_ref, second_ref, node_first_ref, node_second_ref, bias_ref, alpha_pick, beta_pick,
     onehot_ref, base_ref, count_ref, table_ref, first_back, second_back, node_first_back, node_second_back, bias_out,
     to_node, to_node_back, to_table, to_table_back, to_hidden, alpha_place, beta_place) = refs[groups:]
    latent = first_ref.shape[0]
    slab, room = alpha_pick.shape
    wide = slab + room
    source_rows = lax.broadcasted_iota(jnp.int32, (wide, LANES), 0).astype(F32)
    target_rows = lax.broadcasted_iota(jnp.int32, (slab, LANES), 0).astype(F32)
    ones_row = source_rows == float(slab + 2 * rim)
    for rank in range(groups):
        pack = pick(packs, rank)
        source = jnp.where(pack[:rows] < 0.0, -1.0, pack[:rows] * LANES + pack[rows : 2 * rows])
        target = pack[2 * rows :]
        for row in range(rows):
            cols = slice((rank * rows + row) * LANES, (rank * rows + row + 1) * LANES)
            match = (source_rows == source[row : row + 1]) | ones_row
            onehot_ref[:wide, cols] = jnp.where(match, 1.0, 0.0).astype(BF)
            onehot_ref[wide:, cols] = jnp.where(target_rows == target[row : row + 1], 1.0, 0.0).astype(BF)
    bias = bias_ref[...].T
    bias_out[...] = bias
    slab16 = slab_ref[...]
    source = mm(first_ref[:, :latent], slab16)
    target = mm(first_ref[:, latent : 2 * latent], slab16)
    shift = wide_mm(first_ref[:, :latent], jnp.broadcast_to(bias[:, 3:4], (latent, LANES)))
    table_ref[...] = source + shift[:, :1]
    table = jnp.concatenate([*halves(source), *halves(target)], axis=1)
    count = None
    for cols in chunks_of(base_ref.shape[1]):
        near = onehot_ref[:slab, cols]
        hit = onehot_ref[wide:, cols]
        base_ref[:, cols] = mm(table, jnp.concatenate([near, near, hit, hit], axis=0)) + bias[:, 0:1]
        count = add_to(count, mm_nt(jnp.ones((16, CHUNK), BF), hit))
    count_ref[...] = count[:8]
    first_back[...] = flip(first_ref[...])
    second_back[...] = flip(second_ref[...])
    node_first_back[...] = flip(node_first_ref[...])
    node_second_back[...] = flip(node_second_ref[...])
    forward = mm(node_first_ref[:, latent:], second_ref[...])
    to_node[...] = split(forward)
    to_node_back[...] = split(forward.T)
    table = mm(first_ref[:, :latent], node_second_ref[...])
    to_table[...] = split(table)
    to_table_back[...] = split(table.T)
    to_hidden[...] = split(mm(first_ref[:, 2 * latent :], second_ref[...]).T)
    for choose, place in ((alpha_pick, alpha_place), (beta_pick, beta_place)):
        block = choose[...].astype(F32)
        none = jnp.zeros_like(block)
        place[...] = jnp.concatenate(
            [jnp.concatenate([block, none], axis=1), jnp.concatenate([none, block], axis=1)], axis=0
        ).astype(BF)


def start_kernel(groups, *refs):
    parts = refs[:groups]
    (base_in, onehot_ref, slab_ref, count_ref, first_ref, node_first_ref, bias_ref,
     edges_ref, base_ref, message_ref, node_base_ref) = refs[groups:]
    latent, slab = slab_ref.shape
    wide = onehot_ref.shape[0] - slab
    slots = parts[0].shape[1]
    own = first_ref[:, 2 * latent :]
    message = None
    for rank in range(groups):
        for cols in chunks_of(slots):
            here = slice(rank * slots + cols.start, rank * slots + cols.stop)
            edges = pick([part[:, cols] for part in parts], rank)
            edges_ref[:, here] = edges
            base_ref[:, here] = base_in[:, here] + mm(own, edges)
            message = add_to(message, mm_nt(edges, onehot_ref[wide:, here]))
    bias = bias_ref[...]
    message = message + bias[:, 1:2] * count_ref[0:1]
    message_ref[...] = message
    node_base_ref[...] = node_base(slab_ref[...], message, node_first_ref, bias)


def forward_kernel(base_ref, onehot_ref, slab_ref, beta_in, alpha_in, node_base_ref, table_in,
                   first_ref, node_second_ref, bias_ref, to_node, to_table, alpha_place, beta_place,
                   hidden_ref, slope_ref, rims_ref, sums_ref, node_pre_ref, node_hidden_ref, state_ref, table_ref,
                   alpha_ref, beta_ref):
    latent, slab = slab_ref.shape
    rims16 = alpha_in[...] + beta_in[...]
    rims_ref[...] = rims16
    table = jnp.concatenate(halves(mm(first_ref[:, :latent], rims16)), axis=1)
    sums = activate(base_ref, table, onehot_ref, slab, hidden_ref, slope_ref)
    sums_ref[...] = sums
    node_pre = node_base_ref[...] + split_mm(to_node[...], sums)
    node_pre_ref[...] = node_pre
    node_hidden = slope_parts(node_pre)[0].astype(BF)
    node_hidden_ref[...] = node_hidden
    table = table_in[...] + pair_mm(to_table[...], node_hidden)
    table_ref[...] = table
    both = jnp.concatenate(halves(table), axis=1)
    alpha_ref[...] = mm(both, alpha_place[...]).astype(BF)
    beta_ref[...] = mm(both, beta_place[...]).astype(BF)
    state = slab_ref[...].astype(F32) + mm(node_second_ref[...], node_hidden) + bias_ref[:, 3:4]
    state_ref[...] = state.astype(BF)


def between_kernel(edges_ref, hidden_ref, onehot_ref, slab_in, state_ref, table_ref, sums_ref, message_in, count_ref,
                   first_ref, second_ref, node_first_ref, bias_ref,
                   new_ref, base_ref, message_ref, joined_ref, node_base_ref):
    latent = edges_ref.shape[0]
    bias = bias_ref[...]
    second = second_ref[...]
    for cols in chunks_of(edges_ref.shape[1]):
        new_ref[:, cols] = (
            edges_ref[:, cols].astype(F32) + mm(second, hidden_ref[:, cols]) + bias[:, 1:2]
        ).astype(BF)
    state16 = state_ref[...]
    target = mm(first_ref[:, latent : 2 * latent], state16)
    slab_base(table_ref[...], target, first_ref[:, 2 * latent :], bias, onehot_ref, new_ref, base_ref)
    message = message_in[...] + wide_mm(second, sums_ref[...])
    joined_ref[...] = jnp.concatenate([slab_in[...], message.astype(BF)], axis=0)
    message = message + bias[:, 1:2] * count_ref[0:1]
    message_ref[...] = message
    node_base_ref[...] = node_base(state16, message, node_first_ref, bias)


def edge_gradient(wanted, extra_ref, slope_ref, onehot_ref, edges_ref, low_ref):
    slab = wanted.shape[1]
    wide = onehot_ref.shape[0] - slab
    table = jnp.concatenate(halves(wanted), axis=1)
    for cols in chunks_of(edges_ref.shape[1]):
        hit = onehot_ref[wide:, cols]
        grad = mm(table, jnp.concatenate([hit, hit], axis=0))
        if extra_ref is not None:
            grad = grad + extra_ref[:, cols]
        low_ref[:, cols] = (grad * slope_ref[:, cols]).astype(BF)
    return mm_nt(low_ref[...], jnp.concatenate([onehot_ref[...], edges_ref[...]], axis=0))


def middle_kernel(base_ref, onehot_ref, edges_ref, beta_in, alpha_in, node_base_ref, cot_ref,
                  node_second_back, to_node, to_node_back,
                  hidden_ref, low_ref, sums_ref, node_pre_ref, node_grad_ref, wanted_ref, first_sums_ref, rims_ref,
                  slope_ref):
    slab = cot_ref.shape[1]
    wide = onehot_ref.shape[0] - slab
    cot_grad = mm(node_second_back[...], cot_ref[...].astype(BF))
    sums = activate(base_ref, alpha_in[...] + beta_in[...], onehot_ref, slab, hidden_ref, slope_ref)
    sums_ref[...] = sums
    node_pre = node_base_ref[...] + split_mm(to_node[...], sums)
    node_pre_ref[...] = node_pre
    pre_grad = cot_grad * slope_parts(node_pre)[1]
    node_grad_ref[...] = pre_grad
    wanted = split_mm(to_node_back[...], pre_grad)
    wanted_ref[...] = wanted
    first_sums = edge_gradient(wanted, None, slope_ref, onehot_ref, edges_ref, low_ref)
    rims_ref[...] = first_sums[:, slab:wide].astype(BF)
    first_sums_ref[...] = first_sums


def carry_kernel(rim, low_ref, hidden_zero_ref, slab_ref, sums_ref, sums_zero_ref, message_in,
                 node_pre_ref, node_grad_ref, first_sums_ref, count_ref, cot_ref,
                 second_ref, first_back, node_first_back, node_second_back, to_hidden,
                 extra_ref, total_ref, joined_ref, back_ref, back_node_ref):
    latent, slab = slab_ref.shape
    wide = first_sums_ref.shape[1] - slab - latent
    sums = first_sums_ref[...]
    cot = cot_ref[...]
    pre_grad = node_grad_ref[...]
    node_back = mm(node_first_back[...], pre_grad.astype(BF))
    gm = node_back[latent:].astype(BF)
    source = sums[:, :slab].astype(BF)
    target = sums[:, wide : wide + slab].astype(BF)
    back = cot + node_back[:latent] + mm(first_back[:latent], source) + mm(first_back[latent : 2 * latent], target)
    back_ref[...] = back
    back_node_ref[...] = wide_mm(node_second_back[...], back)
    self_back = first_back[2 * latent :]
    cross = None
    for cols in chunks_of(low_ref.shape[1]):
        low = low_ref[:, cols]
        extra_ref[:, cols] = pair_mm(to_hidden[...], low)
        cross = add_to(cross, mm_nt(low, hidden_zero_ref[:, cols]))
    slab16 = slab_ref[...]
    message = message_in[...] + wide_mm(second_ref[...], sums_ref[...])
    joined = jnp.concatenate([slab16, message.astype(BF)], axis=0)
    joined_ref[...] = joined
    pre_sum = sums[:, slab + 2 * rim : slab + 2 * rim + 1]
    edge_two = (
        mm_nt(gm, sums_ref[...].astype(BF))
        + mm_nt(gm, sums_zero_ref[...].astype(BF))
        + mm(self_back, cross.astype(BF))
    )
    gm_sum = 2.0 * jnp.sum(gm.astype(F32) * count_ref[0:1], axis=1, keepdims=True) + wide_mm(
        self_back, jnp.broadcast_to(pre_sum, (latent, LANES))
    )[:, :1]
    node_one, node_two, node_pre_sum, cot_sum = node_sums(
        cot, pre_grad, joined, slope_parts(node_pre_ref[...])[0].astype(BF)
    )
    edge_one = jnp.concatenate(
        [mm_nt(source, slab16), mm_nt(target, slab16), sums[:, wide + slab :]], axis=1
    )
    total_ref[...] = jnp.concatenate(
        [edge_one, edge_two, node_one, node_two, pre_sum, gm_sum, node_pre_sum, cot_sum], axis=1
    )


def output_kernel(count_ref, edges_ref, hidden_ref, joined_ref, node_pre_ref, second_ref, node_second_ref, bias_ref,
                  edge_out, node_out, new_ref):
    bias = bias_ref[...]
    latent = edges_ref.shape[0]
    second = second_ref[...]
    for cols in chunks_of(edges_ref.shape[1]):
        new_ref[:, cols] = (
            edges_ref[:, cols].astype(F32) + mm(second, hidden_ref[:, cols]) + bias[:, 1:2]
        ).astype(BF)
    slots = edge_out.shape[1]
    begin = lax.axis_index("layer") * slots
    for cols in chunks_of(slots):
        position = lax.broadcasted_iota(jnp.int32, (latent, CHUNK), 1) + cols.start
        mine = new_ref[:, pl.ds(pl.multiple_of(begin + cols.start, CHUNK), CHUNK)].astype(F32)
        edge_out[:, cols] = jnp.where(position < count_ref[0, 0], mine, 0.0).astype(BF)
    node_hidden = slope_parts(node_pre_ref[...])[0].astype(BF)
    state = joined_ref[:latent].astype(F32) + mm(node_second_ref[...], node_hidden) + bias[:, 3:4]
    node_out[...] = own_rows(state.T, node_out.shape[0]).astype(BF)


def last_kernel(rim, back_in, back_node, beta_in, alpha_in, alpha_pick, beta_pick, joined_ref, node_pre_ref,
                node_hidden_ref, wanted_in, sums_ref, count_ref, extra_ref, slope_ref, onehot_ref, edges_ref,
                slab_ref, rims_ref, slab_one_ref, total_in, first_back, node_first_back, to_node_back, to_table_back,
                keep_ref, send_ref, back_ref, low_ref):
    latent, slab = slab_ref.shape
    wide = onehot_ref.shape[0] - slab
    placed = mm_nt(alpha_in[...], alpha_pick[...]) + mm_nt(beta_in[...], beta_pick[...])
    pre_grad = (back_node[...] + split_mm(to_table_back[...], placed)) * slope_parts(node_pre_ref[...])[1]
    wanted = wanted_in[...] + split_mm(to_node_back[...], pre_grad)
    sums = edge_gradient(wanted, extra_ref, slope_ref, onehot_ref, edges_ref, low_ref)
    source = sums[:, :wide].astype(BF)
    target = sums[:, wide : wide + slab].astype(BF)
    ext_grad = mm(first_back[:latent], source)
    node_back = mm(node_first_back[...], pre_grad.astype(BF))
    gm = node_back[latent:].astype(BF)
    grad = back_in[...] + wide_mm(first_back[:latent], placed)
    back_ref[...] = (
        grad + node_back[:latent] + ext_grad[:, :slab] + mm(first_back[latent : 2 * latent], target)
    )
    alpha, beta = rim_gradients(ext_grad, slab, rim)
    node_one, node_two, node_pre_sum, grad_sum = node_sums(grad, pre_grad, joined_ref[...], node_hidden_ref[...])
    slab16 = slab_ref[...]
    ext16 = jnp.concatenate([slab16, rims_ref[...]], axis=1)
    edge_one = jnp.concatenate(
        [
            mm_nt(source, ext16) + mm_nt(placed.astype(BF), slab_one_ref[...]),
            mm_nt(target, slab16),
            sums[:, wide + slab :],
        ],
        axis=1,
    )
    edge_two = mm_nt(gm, sums_ref[...].astype(BF))
    pre_sum = sums[:, slab + 2 * rim : slab + 2 * rim + 1]
    gm_sum = jnp.sum(gm.astype(F32) * count_ref[0:1], axis=1, keepdims=True)
    total = total_in[...] + jnp.concatenate(
        [edge_one, edge_two, node_one, node_two, pre_sum, gm_sum, node_pre_sum, grad_sum], axis=1
    )
    even = is_even()
    half, used = keep_ref.shape
    keep_ref[...] = jnp.where(even, total[:half], total[half:])
    pieces = [jnp.where(even, total[half:], total[:half]), alpha[:half], alpha[half:], beta[:half], beta[half:]]
    spare = send_ref.shape[1] - used - 4 * rim
    if spare:
        pieces.append(jnp.zeros((half, spare), F32))
    send_ref[...] = jnp.concatenate(pieces, axis=1).astype(BF)


def open_kernel(rim, keep_ref, other_ref, out_ref):
    half, used = keep_ref.shape
    other = other_ref[...].astype(F32)
    pieces = [keep_ref[...] + other[:, :used], other[:, used + 2 * rim : used + 4 * rim]]
    spare = out_ref.shape[1] - used - 2 * rim
    if spare:
        pieces.append(jnp.zeros((half, spare), F32))
    out_ref[...] = jnp.concatenate(pieces, axis=1).astype(BF)


def pass_kernel(used, rim, mine_ref, other_ref, out_ref, near_ref):
    other = other_ref[...].astype(F32)
    total = mine_ref[...].astype(F32)[:, :used] + other[:, :used]
    place = lax.axis_index("phi")
    home = (lax.rem(place // 2, 2) == 1) == (lax.rem(place, 2) == 0)
    held = other[:, used : used + 2 * rim]
    near_ref[...] = jnp.where(home, held, 0.0)
    pieces = [total, jnp.where(home, 0.0, held)]
    spare = out_ref.shape[1] - used - 2 * rim
    if spare:
        pieces.append(jnp.zeros((total.shape[0], spare), F32))
    block = jnp.concatenate(pieces, axis=1).astype(BF)
    half = block.shape[0]
    for first in range(0, out_ref.shape[0], half):
        out_ref[first : first + half] = block


def close_kernel(used, rim, count, all_ref, near_ref, half_ref, beta_ref):
    half = half_ref.shape[0]
    blocks = [all_ref[rank * half : (rank + 1) * half].astype(F32) for rank in range(count)]
    total = blocks[0]
    for block in blocks[1:]:
        total = total + block
    half_ref[...] = total
    place = lax.axis_index("phi")
    here = place // 4
    step = jnp.where(lax.rem(place, 2) == 0, count - 1, 1)
    source = lax.rem(here + step, count)
    held = blocks[0]
    for rank in range(1, count):
        held = jnp.where(source == rank, blocks[rank], held)
    beta_ref[...] = near_ref[...] + held[:, used : used + 2 * rim]


def rims_of(value, used, rim):
    return jnp.concatenate([value[:, used : used + rim], value[:, used + rim : used + 2 * rim]], axis=0)


def node_kernel(used, rim, first_ref, beta_ref, back_ref, upper_ref, lower_ref, node_grad):
    alpha = rims_of(first_ref[...].astype(F32), used, rim)
    beta = rims_of(beta_ref[...], 0, rim)
    grad = back_ref[...] + placed_rims(alpha, beta, upper_ref, lower_ref)
    node_grad[...] = own_rows(grad.T, node_grad.shape[0])


def finish_kernel(used, half_ref, other_ref, edge_one, edge_two, node_one, node_two, bias_out):
    even = is_even()
    mine = half_ref[...]
    other = other_ref[...]
    total = jnp.concatenate([jnp.where(even, mine, other), jnp.where(even, other, mine)], axis=0)
    cut = 0
    for ref in (edge_one, edge_two, node_one, node_two):
        ref[...] = total[:, cut : cut + ref.shape[1]]
        cut += ref.shape[1]
    block = used - 4 - (used - 4) % LANES
    turned = total[:, block : block + LANES].T
    bias_out[...] = turned[used - 4 - block : used - block]


def call(kernel, outs, *args, scratch=(), smem=0, hbm=(), cost=1.0):
    args = [
        pltpu.with_memory_space_constraint(arg, HBM) if place in hbm else arg for place, arg in enumerate(args)
    ]
    held = [(arg.shape, arg.dtype) for arg in args] + list(outs)
    held += [(ref.shape, ref.dtype) for ref in scratch if jnp.issubdtype(ref.dtype, jnp.number)]
    room = sum(math.prod(shape) * jnp.dtype(kind).itemsize for shape, kind in held)
    spaces = [pltpu.SMEM if place < smem else HBM if place in hbm else VM for place in range(len(args))]
    specs = [pl.BlockSpec(memory_space=space) for space in spaces]
    return pl.pallas_call(
        kernel,
        out_shape=[jax.ShapeDtypeStruct(shape, kind) for shape, kind in outs],
        in_specs=specs,
        out_specs=[pl.BlockSpec(memory_space=VM) for _ in outs],
        scratch_shapes=list(scratch),
        compiler_params=pltpu.CompilerParams(vmem_limit_bytes=room + 10 * 1024 * 1024),
        cost_estimate=pl.CostEstimate(
            flops=int(cost * 1e9), bytes_accessed=int(cost * 3.6e6), transcendentals=0
        ),
    )(*args)


def swap(value, axis, pairing):
    count = lax.axis_size(axis)
    return lax.ppermute(value, axis, [(source, pairing(source) % count) for source in range(count)])


def by_alpha(value):
    return swap(value, "phi", lambda index: index ^ 1)


def by_beta(value):
    return swap(value, "phi", lambda index: index - 1 if index % 2 == 0 else index + 1)


def layer_parts(value):
    groups = lax.axis_size("layer")
    return [value] + [
        swap(value, "layer", lambda index, turn=turn: index + turn) for turn in range(1, groups)
    ]


def body(node_feats, edge_feats, edge_source, edge_target, edge_counts, rim_upper, rim_lower,
         edge_first, edge_second, node_first, node_second, biases, node_cot):
    groups = lax.axis_size("layer")
    ring = lax.axis_size("phi")
    latent, width = node_feats.shape
    hidden = edge_second.shape[1]
    slots = edge_feats.shape[1]
    slab = width * groups
    rim = rim_upper.shape[1]
    wide = (slab + 2 * rim) // LANES * LANES + LANES
    total_slots = slots * groups
    rows = slots // LANES
    room = wide - slab
    rim_shape = ((latent, room), BF)
    per_slot = lambda kind: ((latent, total_slots), kind)
    per_hit = lambda kind, depth=1: ((depth * latent, slab), kind)

    packed, upper, lower = call(
        prep_kernel,
        [((3 * rows + width, LANES), BF), ((1, rim), jnp.int32), ((1, rim), jnp.int32)],
        edge_counts, edge_source.reshape(rows, LANES), edge_target.reshape(rows, LANES),
        node_feats.T, node_cot.T, rim_upper, rim_lower,
        scratch=[VM((rows, LANES), jnp.int32), VM((rows, LANES), jnp.int32),
                 VM((width, latent), BF), VM((width, latent), F32), pltpu.SemaphoreType.DMA((6,))],
        smem=1, hbm=range(1, 7),
    )
    packs = layer_parts(packed)
    upper, lower, alpha_pick, beta_pick = call(
        pick_kernel,
        [((slab, rim), BF), ((slab, rim), BF), ((slab, room), BF), ((slab, room), BF)],
        packed, upper, lower, cost=0.1,
    )
    later, _ = lax.optimization_barrier((edge_feats, alpha_pick))
    parts = [edge_feats] + layer_parts(later)[1:]
    slab_zero, cot, alpha, beta = call(
        functools.partial(slab_kernel, groups, rows),
        [per_hit(BF), per_hit(F32), rim_shape, rim_shape], *packs, alpha_pick, beta_pick, cost=20.0,
    )
    beta = by_beta(beta)
    alpha = by_alpha(alpha)
    (onehot, base, count, table, first_back, second_back, node_first_back, node_second_back, bias,
     to_node, to_node_back, to_table, to_table_back, to_hidden, alpha_place, beta_place) = call(
        functools.partial(onehot_kernel, groups, rows, rim),
        [((wide + slab, total_slots), BF), per_slot(F32), ((8, slab), F32), per_hit(F32),
         (edge_first.shape[::-1], BF), (edge_second.shape[::-1], BF),
         (node_first.shape[::-1], BF), (node_second.shape[::-1], BF), (biases.shape[::-1], F32)]
        + [((hidden, 3 * hidden), BF)] * 5 + [((2 * slab, 2 * room), BF)] * 2,
        *packs, slab_zero, edge_first, edge_second, node_first, node_second, biases, alpha_pick, beta_pick, cost=2.0,
    )
    edges_zero, base, message, node_base_zero = call(
        functools.partial(start_kernel, groups),
        [per_slot(BF), per_slot(F32), per_hit(F32), per_hit(F32)],
        *parts, base, onehot, slab_zero, count, edge_first, node_first, bias, cost=1.0,
    )
    (hidden_zero, slope, rims_zero, sums_zero, node_pre_zero, node_hidden_zero, slab_one, table,
     alpha, beta) = call(
        forward_kernel,
        [per_slot(BF), per_slot(F32), rim_shape, per_hit(F32), per_hit(F32), per_hit(BF), per_hit(BF), per_hit(F32),
         ((latent, 2 * room), BF), ((latent, 2 * room), BF)],
        base, onehot, slab_zero, beta, alpha, node_base_zero, table, edge_first, node_second, bias, to_node, to_table,
        alpha_place, beta_place, cost=2.0,
    )
    beta = by_beta(beta)
    alpha = by_alpha(alpha)
    edges_one, base, message, joined_zero, node_base_one = call(
        between_kernel, [per_slot(BF), per_slot(F32), per_hit(F32), per_hit(BF, 2), per_hit(F32)],
        edges_zero, hidden_zero, onehot, slab_zero, slab_one, table, sums_zero, message, count,
        edge_first, edge_second, node_first, bias, cost=2.0,
    )
    total_width = edge_first.shape[1] + hidden + node_first.shape[1] + node_second.shape[1] + 4
    hidden_one, low, sums_one, node_pre_one, node_grad_one, wanted, first_sums, rims = call(
        middle_kernel,
        [per_slot(BF), per_slot(BF), per_hit(F32), per_hit(F32), per_hit(F32), per_hit(F32),
         ((hidden, wide + slab + latent), F32), rim_shape],
        base, onehot, edges_one, beta, alpha, node_base_one, cot, node_second_back, to_node, to_node_back,
        scratch=[VM((hidden, total_slots), F32)], cost=3.0,
    )
    beta = by_beta(rims)
    alpha = by_alpha(rims)
    extra, total, joined_one, back, back_node = call(
        functools.partial(carry_kernel, rim),
        [per_slot(F32), ((latent, total_width), F32), per_hit(BF, 2), per_hit(F32), per_hit(F32)],
        low, hidden_zero, slab_one, sums_one, sums_zero, message, node_pre_one, node_grad_one, first_sums, count, cot,
        edge_second, first_back, node_first_back, node_second_back, to_hidden, cost=2.0,
    )
    edge_out, node_out = call(
        output_kernel, [((latent, slots), BF), ((width, latent), BF)],
        edge_counts, edges_one, hidden_one, joined_one, node_pre_one, edge_second, node_second, bias,
        scratch=[VM((latent, total_slots), BF)], smem=1, cost=2.0,
    )
    half = hidden // 2
    up = lambda count: -(-count // LANES) * LANES
    keep, send, back = call(
        functools.partial(last_kernel, rim),
        [((half, total_width), F32), ((half, up(total_width + 4 * rim)), BF), per_hit(F32)],
        back, back_node, beta, alpha, alpha_pick, beta_pick, joined_zero, node_pre_zero, node_hidden_zero, wanted,
        sums_zero, count, extra, slope, onehot, edges_zero, slab_zero, rims_zero, slab_one, total,
        first_back, node_first_back, to_node_back, to_table_back,
        scratch=[VM((hidden, total_slots), BF)], cost=2.0,
    )
    first = by_alpha(send)
    width_now = up(total_width + 2 * rim)
    mine = call(
        functools.partial(open_kernel, rim), [((half, width_now), BF)], keep, first, cost=0.1,
    )[0]
    other = swap(mine, "phi", lambda index: index ^ 2)
    mine, near = call(
        functools.partial(pass_kernel, total_width, rim),
        [((ring // 4 * half, width_now), BF), ((half, 2 * rim), F32)], mine, other, cost=0.1,
    )
    count = ring // 4
    lines = [[place + 4 * rank for rank in range(count)] for place in range(4)]
    every = lax.all_to_all(mine, "phi", 0, 0, axis_index_groups=lines, tiled=True)
    mine, beta = call(
        functools.partial(close_kernel, total_width, rim, count),
        [((half, width_now), F32), ((half, 2 * rim), F32)], every, near, cost=0.1,
    )
    whole = by_alpha(mine)
    node_grad = call(
        functools.partial(node_kernel, total_width, rim), [((width, latent), F32)],
        first, beta, back, upper, lower, cost=1.0,
    )[0]
    edge_one, edge_two, node_one, node_two, bias_out = call(
        functools.partial(finish_kernel, total_width),
        [(edge_first.shape, F32), (edge_second.shape, F32), (node_first.shape, F32), (node_second.shape, F32),
         (biases.shape, F32)],
        mine, whole,
    )
    return node_out.T, edge_out, node_grad.T, edge_one, edge_two, node_one, node_two, bias_out


def solution(mesh):
    split = P(None, ("phi", "layer"))
    return jax.shard_map(
        body,
        mesh=mesh,
        in_specs=(split, split, P(("phi", "layer")), P(("phi", "layer")), P("phi", "layer"),
                  P("phi", None), P("phi", None), P(), P(), P(), P(), P(), split),
        out_specs=(split, split, split, P(), P(), P(), P(), P()),
        check_vma=False,
    )
```

```python
import functools
import math

import jax
import jax.numpy as jnp
from jax import lax
from jax.experimental import pallas as pl
from jax.experimental.pallas import tpu as pltpu
from jax.sharding import PartitionSpec as P

BF = jnp.bfloat16
F32 = jnp.float32
CHUNK = 512
LANES = 128
HBM = pltpu.HBM
VM = pltpu.VMEM


def mm(left, right):
    return jnp.dot(left, right, preferred_element_type=F32)


def mm_nt(left, right):
    return lax.dot_general(left, right, (((1,), (1,)), ((), ())), preferred_element_type=F32)


def flip(weight):
    return weight.astype(F32).T.astype(BF)


def halves(value):
    high = value.astype(BF)
    return high, (value - high.astype(F32)).astype(BF)


def wide_mm(weight, value):
    high, low = halves(value)
    return mm(jnp.concatenate([weight, weight], axis=1), jnp.concatenate([high, low], axis=0))


def sigmoid(value):
    return 0.5 + 0.5 * jnp.tanh(0.5 * value)


def add_to(total, value):
    return value if total is None else total + value


def chunks_of(count):
    return [slice(first, first + CHUNK) for first in range(0, count, CHUNK)]


def is_even():
    return lax.rem(lax.axis_index("phi"), 2) == 0


def pick(parts, natural):
    groups = len(parts)
    turn = lax.rem(lax.axis_index("layer") - natural + groups, groups)
    value = parts[0]
    for rank in range(1, groups):
        value = jnp.where(turn == rank, parts[rank], value)
    return value


def own_rows(slab_rows, width):
    layer = lax.axis_index("layer")
    value = slab_rows[:width]
    for rank in range(1, slab_rows.shape[0] // width):
        value = jnp.where(layer == rank, slab_rows[rank * width : (rank + 1) * width], value)
    return value


def split(value):
    high, low = halves(value)
    return jnp.concatenate([high, high, low], axis=1)


def split_mm(table, value):
    high, low = halves(value)
    return mm(table, jnp.concatenate([high, low, high], axis=0))


def pair_mm(table, value):
    return mm(table[:, value.shape[0] :], jnp.concatenate([value, value], axis=0))


def placed_rims(alpha, beta, upper_ref, lower_ref):
    even = is_even()
    from_upper = jnp.where(even, alpha, beta).astype(BF)
    from_lower = jnp.where(even, beta, alpha).astype(BF)
    return mm_nt(from_upper, upper_ref[...]) + mm_nt(from_lower, lower_ref[...])


def rim_gradients(ext_grad, slab, rim):
    even = is_even()
    below = ext_grad[:, slab : slab + rim]
    above = ext_grad[:, slab + rim : slab + 2 * rim]
    return jnp.where(even, above, below), jnp.where(even, below, above)


def slope_parts(pre):
    logistic = sigmoid(pre)
    value = pre * logistic
    return value, logistic + value * (1.0 - logistic)


def activate(base_ref, table, onehot_ref, slab, hidden_ref, slope_ref):
    wide = onehot_ref.shape[0] - slab
    for cols in chunks_of(base_ref.shape[1]):
        rims = onehot_ref[slab:wide, cols]
        pre = base_ref[:, cols].astype(F32) + mm(table, jnp.concatenate([rims, rims], axis=0))
        value, slope = slope_parts(pre)
        hidden = value.astype(BF)
        hidden_ref[:, cols] = hidden
        slope_ref[:, cols] = slope.astype(BF)
    return mm_nt(hidden_ref[...], onehot_ref[wide:])


def slab_base(source, target, own, bias, onehot_ref, edges_ref, base_ref):
    slab = source.shape[1]
    wide = onehot_ref.shape[0] - slab
    table = jnp.concatenate([*halves(source), *halves(target), own], axis=1)
    for cols in chunks_of(base_ref.shape[1]):
        near = onehot_ref[:slab, cols]
        hit = onehot_ref[wide:, cols]
        stack = jnp.concatenate([near, near, hit, hit, edges_ref[:, cols]], axis=0)
        base_ref[:, cols] = (mm(table, stack) + bias[:, 0:1]).astype(BF)


def node_base(state16, message, first_ref, bias):
    latent = state16.shape[0]
    return (
        mm(first_ref[:, :latent], state16)
        + wide_mm(first_ref[:, latent:], message)
        + bias[:, 2:3]
    )


def node_sums(grad, pre_grad, joined, hidden):
    return (
        mm_nt(pre_grad.astype(BF), joined),
        mm_nt(grad.astype(BF), hidden),
        jnp.sum(pre_grad, axis=1, keepdims=True),
        jnp.sum(grad, axis=1, keepdims=True),
    )


def prep_kernel(count_ref, source_hbm, target_hbm, feats_hbm, cot_hbm, upper_hbm, lower_hbm,
                out_ref, upper_ref, lower_ref, source, target, feats, cot, sems):
    pairs = ((source_hbm, source), (target_hbm, target), (feats_hbm, feats), (cot_hbm, cot),
             (upper_hbm, upper_ref), (lower_hbm, lower_ref))
    copies = [pltpu.make_async_copy(a, b, sems.at[place]) for place, (a, b) in enumerate(pairs)]
    for copy in copies:
        copy.start()
    for copy in copies:
        copy.wait()
    rows = source.shape[0]
    position = lax.broadcasted_iota(jnp.int32, (rows, LANES), 0) * LANES + lax.broadcasted_iota(
        jnp.int32, (rows, LANES), 1
    )
    valid = position < count_ref[0, 0]
    index = source[...]
    out_ref[:rows] = jnp.where(valid, index // LANES, -1).astype(F32).astype(BF)
    out_ref[rows : 2 * rows] = (index % LANES).astype(F32).astype(BF)
    out_ref[2 * rows : 3 * rows] = jnp.where(valid, target[...], -1).astype(F32).astype(BF)
    out_ref[3 * rows :] = jnp.concatenate([feats[...].astype(F32), cot[...]], axis=1).astype(BF)


def pick_kernel(packed_ref, upper, lower, upper_ref, lower_ref, alpha_pick, beta_pick):
    hits = lax.broadcasted_iota(jnp.int32, upper_ref.shape, 0)
    upper_ref[...] = (hits == upper[...]).astype(F32).astype(BF)
    lower_ref[...] = (hits == lower[...]).astype(F32).astype(BF)
    slab, room = alpha_pick.shape
    rim = upper.shape[1]
    first = jnp.concatenate([upper[...], jnp.full((1, room - rim), -1, jnp.int32)], axis=1)
    second = jnp.concatenate(
        [jnp.full((1, rim), -1, jnp.int32), lower[...], jnp.full((1, room - 2 * rim), -1, jnp.int32)], axis=1
    )
    even = is_even()
    hits = lax.broadcasted_iota(jnp.int32, (slab, room), 0)
    alpha_pick[...] = (hits == jnp.where(even, first, second)).astype(F32).astype(BF)
    beta_pick[...] = (hits == jnp.where(even, second, first)).astype(F32).astype(BF)


def slab_kernel(groups, rows, *refs):
    packs = [ref[3 * rows :].astype(F32) for ref in refs[:groups]]
    alpha_pick, beta_pick, slab_ref, cot_ref, alpha_ref, beta_ref = refs[groups:]
    latent = slab_ref.shape[0]
    both = jnp.concatenate([pick(packs, rank) for rank in range(groups)], axis=0).T
    slab16 = both[:latent].astype(BF)
    slab_ref[...] = slab16
    cot_ref[...] = both[latent:]
    alpha_ref[...] = mm(slab16, alpha_pick[...]).astype(BF)
    beta_ref[...] = mm(slab16, beta_pick[...]).astype(BF)


def onehot_kernel(groups, rows, rim, *refs):
    packs = [ref[: 3 * rows].astype(F32) for ref in refs[:groups]]
    (slab_ref, first_ref, second_ref, node_first_ref, node_second_ref, bias_ref, alpha_pick, beta_pick,
     onehot_ref, base_ref, count_ref, table_ref, first_back, second_back, node_first_back, node_second_back, bias_out,
     to_node, to_node_back, to_table, to_table_back, to_hidden, alpha_place, beta_place) = refs[groups:]
    latent = first_ref.shape[0]
    slab, room = alpha_pick.shape
    wide = slab + room
    source_rows = lax.broadcasted_iota(jnp.int32, (wide, LANES), 0).astype(F32)
    target_rows = lax.broadcasted_iota(jnp.int32, (slab, LANES), 0).astype(F32)
    ones_row = source_rows == float(slab + 2 * rim)
    for rank in range(groups):
        pack = pick(packs, rank)
        source = jnp.where(pack[:rows] < 0.0, -1.0, pack[:rows] * LANES + pack[rows : 2 * rows])
        target = pack[2 * rows :]
        for row in range(rows):
            cols = slice((rank * rows + row) * LANES, (rank * rows + row + 1) * LANES)
            match = (source_rows == source[row : row + 1]) | ones_row
            onehot_ref[:wide, cols] = jnp.where(match, 1.0, 0.0).astype(BF)
            onehot_ref[wide:, cols] = jnp.where(target_rows == target[row : row + 1], 1.0, 0.0).astype(BF)
    bias = bias_ref[...].T
    bias_out[...] = bias
    slab16 = slab_ref[...]
    source = mm(first_ref[:, :latent], slab16)
    target = mm(first_ref[:, latent : 2 * latent], slab16)
    shift = wide_mm(first_ref[:, :latent], jnp.broadcast_to(bias[:, 3:4], (latent, LANES)))
    table_ref[...] = source + shift[:, :1]
    table = jnp.concatenate([*halves(source), *halves(target)], axis=1)
    count = None
    for cols in chunks_of(base_ref.shape[1]):
        near = onehot_ref[:slab, cols]
        hit = onehot_ref[wide:, cols]
        base_ref[:, cols] = mm(table, jnp.concatenate([near, near, hit, hit], axis=0)) + bias[:, 0:1]
        count = add_to(count, mm_nt(jnp.ones((16, CHUNK), BF), hit))
    count_ref[...] = count[:8]
    first_back[...] = flip(first_ref[...])
    second_back[...] = flip(second_ref[...])
    node_first_back[...] = flip(node_first_ref[...])
    node_second_back[...] = flip(node_second_ref[...])
    forward = mm(node_first_ref[:, latent:], second_ref[...])
    to_node[...] = split(forward)
    to_node_back[...] = split(forward.T)
    table = mm(first_ref[:, :latent], node_second_ref[...])
    to_table[...] = split(table)
    to_table_back[...] = split(table.T)
    to_hidden[...] = split(mm(first_ref[:, 2 * latent :], second_ref[...]).T)
    for choose, place in ((alpha_pick, alpha_place), (beta_pick, beta_place)):
        block = choose[...].astype(F32)
        none = jnp.zeros_like(block)
        place[...] = jnp.concatenate(
            [jnp.concatenate([block, none], axis=1), jnp.concatenate([none, block], axis=1)], axis=0
        ).astype(BF)


def start_kernel(groups, *refs):
    parts = refs[:groups]
    (base_in, onehot_ref, slab_ref, count_ref, first_ref, node_first_ref, bias_ref,
     edges_ref, base_ref, message_ref, node_base_ref) = refs[groups:]
    latent, slab = slab_ref.shape
    wide = onehot_ref.shape[0] - slab
    slots = parts[0].shape[1]
    own = first_ref[:, 2 * latent :]
    message = None
    for rank in range(groups):
        for cols in chunks_of(slots):
            here = slice(rank * slots + cols.start, rank * slots + cols.stop)
            edges = pick([part[:, cols] for part in parts], rank)
            edges_ref[:, here] = edges
            base_ref[:, here] = (base_in[:, here] + mm(own, edges)).astype(BF)
            message = add_to(message, mm_nt(edges, onehot_ref[wide:, here]))
    bias = bias_ref[...]
    message = message + bias[:, 1:2] * count_ref[0:1]
    message_ref[...] = message
    node_base_ref[...] = node_base(slab_ref[...], message, node_first_ref, bias)


def forward_kernel(base_ref, onehot_ref, slab_ref, beta_in, alpha_in, node_base_ref, table_in,
                   first_ref, node_second_ref, bias_ref, to_node, to_table, alpha_place, beta_place,
                   hidden_ref, slope_ref, rims_ref, sums_ref, node_pre_ref, node_hidden_ref, state_ref, table_ref,
                   alpha_ref, beta_ref):
    latent, slab = slab_ref.shape
    rims16 = alpha_in[...] + beta_in[...]
    rims_ref[...] = rims16
    table = jnp.concatenate(halves(mm(first_ref[:, :latent], rims16)), axis=1)
    sums = activate(base_ref, table, onehot_ref, slab, hidden_ref, slope_ref)
    sums_ref[...] = sums
    node_pre = node_base_ref[...] + split_mm(to_node[...], sums)
    node_pre_ref[...] = node_pre
    node_hidden = slope_parts(node_pre)[0].astype(BF)
    node_hidden_ref[...] = node_hidden
    table = table_in[...] + pair_mm(to_table[...], node_hidden)
    table_ref[...] = table
    both = jnp.concatenate(halves(table), axis=1)
    alpha_ref[...] = mm(both, alpha_place[...]).astype(BF)
    beta_ref[...] = mm(both, beta_place[...]).astype(BF)
    state = slab_ref[...].astype(F32) + mm(node_second_ref[...], node_hidden) + bias_ref[:, 3:4]
    state_ref[...] = state.astype(BF)


def between_kernel(edges_ref, hidden_ref, onehot_ref, slab_in, state_ref, table_ref, sums_ref, message_in, count_ref,
                   first_ref, second_ref, node_first_ref, bias_ref,
                   new_ref, base_ref, message_ref, joined_ref, node_base_ref):
    latent = edges_ref.shape[0]
    bias = bias_ref[...]
    second = second_ref[...]
    for cols in chunks_of(edges_ref.shape[1]):
        new_ref[:, cols] = (
            edges_ref[:, cols].astype(F32) + mm(second, hidden_ref[:, cols]) + bias[:, 1:2]
        ).astype(BF)
    state16 = state_ref[...]
    target = mm(first_ref[:, latent : 2 * latent], state16)
    slab_base(table_ref[...], target, first_ref[:, 2 * latent :], bias, onehot_ref, new_ref, base_ref)
    message = message_in[...] + wide_mm(second, sums_ref[...])
    joined_ref[...] = jnp.concatenate([slab_in[...], message.astype(BF)], axis=0)
    message = message + bias[:, 1:2] * count_ref[0:1]
    message_ref[...] = message
    node_base_ref[...] = node_base(state16, message, node_first_ref, bias)


def edge_gradient(wanted, extra_ref, slope_ref, onehot_ref, edges_ref, low_ref):
    slab = wanted.shape[1]
    wide = onehot_ref.shape[0] - slab
    table = jnp.concatenate(halves(wanted), axis=1)
    for cols in chunks_of(edges_ref.shape[1]):
        hit = onehot_ref[wide:, cols]
        grad = mm(table, jnp.concatenate([hit, hit], axis=0))
        if extra_ref is not None:
            grad = grad + extra_ref[:, cols].astype(F32)
        low_ref[:, cols] = (grad * slope_ref[:, cols].astype(F32)).astype(BF)
    return mm_nt(low_ref[...], jnp.concatenate([onehot_ref[...], edges_ref[...]], axis=0))


def middle_kernel(base_ref, onehot_ref, edges_ref, beta_in, alpha_in, node_base_ref, cot_ref,
                  node_second_back, to_node, to_node_back,
                  hidden_ref, low_ref, sums_ref, node_pre_ref, node_grad_ref, wanted_ref, first_sums_ref, rims_ref,
                  slope_ref):
    slab = cot_ref.shape[1]
    wide = onehot_ref.shape[0] - slab
    cot_grad = mm(node_second_back[...], cot_ref[...].astype(BF))
    sums = activate(base_ref, alpha_in[...] + beta_in[...], onehot_ref, slab, hidden_ref, slope_ref)
    sums_ref[...] = sums
    node_pre = node_base_ref[...] + split_mm(to_node[...], sums)
    node_pre_ref[...] = node_pre
    pre_grad = cot_grad * slope_parts(node_pre)[1]
    node_grad_ref[...] = pre_grad
    wanted = split_mm(to_node_back[...], pre_grad)
    wanted_ref[...] = wanted
    first_sums = edge_gradient(wanted, None, slope_ref, onehot_ref, edges_ref, low_ref)
    rims_ref[...] = first_sums[:, slab:wide].astype(BF)
    first_sums_ref[...] = first_sums


def carry_kernel(rim, low_ref, hidden_zero_ref, slab_ref, sums_ref, sums_zero_ref, message_in,
                 node_pre_ref, node_grad_ref, first_sums_ref, count_ref, cot_ref,
                 second_ref, first_back, node_first_back, node_second_back, to_hidden,
                 extra_ref, total_ref, joined_ref, back_ref, back_node_ref):
    latent, slab = slab_ref.shape
    wide = first_sums_ref.shape[1] - slab - latent
    sums = first_sums_ref[...]
    cot = cot_ref[...]
    pre_grad = node_grad_ref[...]
    node_back = mm(node_first_back[...], pre_grad.astype(BF))
    gm = node_back[latent:].astype(BF)
    source = sums[:, :slab].astype(BF)
    target = sums[:, wide : wide + slab].astype(BF)
    back = cot + node_back[:latent] + mm(first_back[:latent], source) + mm(first_back[latent : 2 * latent], target)
    back_ref[...] = back
    back_node_ref[...] = wide_mm(node_second_back[...], back)
    self_back = first_back[2 * latent :]
    cross = None
    for cols in chunks_of(low_ref.shape[1]):
        low = low_ref[:, cols]
        extra_ref[:, cols] = pair_mm(to_hidden[...], low).astype(BF)
        cross = add_to(cross, mm_nt(low, hidden_zero_ref[:, cols]))
    slab16 = slab_ref[...]
    message = message_in[...] + wide_mm(second_ref[...], sums_ref[...])
    joined = jnp.concatenate([slab16, message.astype(BF)], axis=0)
    joined_ref[...] = joined
    pre_sum = sums[:, slab + 2 * rim : slab + 2 * rim + 1]
    edge_two = (
        mm_nt(gm, sums_ref[...].astype(BF))
        + mm_nt(gm, sums_zero_ref[...].astype(BF))
        + mm(self_back, cross.astype(BF))
    )
    gm_sum = 2.0 * jnp.sum(gm.astype(F32) * count_ref[0:1], axis=1, keepdims=True) + wide_mm(
        self_back, jnp.broadcast_to(pre_sum, (latent, LANES))
    )[:, :1]
    node_one, node_two, node_pre_sum, cot_sum = node_sums(
        cot, pre_grad, joined, slope_parts(node_pre_ref[...])[0].astype(BF)
    )
    edge_one = jnp.concatenate(
        [mm_nt(source, slab16), mm_nt(target, slab16), sums[:, wide + slab :]], axis=1
    )
    total_ref[...] = jnp.concatenate(
        [edge_one, edge_two, node_one, node_two, pre_sum, gm_sum, node_pre_sum, cot_sum], axis=1
    )


def output_kernel(count_ref, edges_ref, hidden_ref, joined_ref, node_pre_ref, second_ref, node_second_ref, bias_ref,
                  edge_out, node_out, new_ref):
    bias = bias_ref[...]
    latent = edges_ref.shape[0]
    second = second_ref[...]
    for cols in chunks_of(edges_ref.shape[1]):
        new_ref[:, cols] = (
            edges_ref[:, cols].astype(F32) + mm(second, hidden_ref[:, cols]) + bias[:, 1:2]
        ).astype(BF)
    slots = edge_out.shape[1]
    begin = lax.axis_index("layer") * slots
    for cols in chunks_of(slots):
        position = lax.broadcasted_iota(jnp.int32, (latent, CHUNK), 1) + cols.start
        mine = new_ref[:, pl.ds(pl.multiple_of(begin + cols.start, CHUNK), CHUNK)].astype(F32)
        edge_out[:, cols] = jnp.where(position < count_ref[0, 0], mine, 0.0).astype(BF)
    node_hidden = slope_parts(node_pre_ref[...])[0].astype(BF)
    state = joined_ref[:latent].astype(F32) + mm(node_second_ref[...], node_hidden) + bias[:, 3:4]
    node_out[...] = own_rows(state.T, node_out.shape[0]).astype(BF)


def last_kernel(rim, back_in, back_node, beta_in, alpha_in, alpha_pick, beta_pick, joined_ref, node_pre_ref,
                node_hidden_ref, wanted_in, sums_ref, count_ref, extra_ref, slope_ref, onehot_ref, edges_ref,
                slab_ref, rims_ref, slab_one_ref, total_in, first_back, node_first_back, to_node_back, to_table_back,
                keep_ref, send_ref, back_ref, low_ref):
    latent, slab = slab_ref.shape
    wide = onehot_ref.shape[0] - slab
    placed = mm_nt(alpha_in[...], alpha_pick[...]) + mm_nt(beta_in[...], beta_pick[...])
    pre_grad = (back_node[...] + split_mm(to_table_back[...], placed)) * slope_parts(node_pre_ref[...])[1]
    wanted = wanted_in[...] + split_mm(to_node_back[...], pre_grad)
    sums = edge_gradient(wanted, extra_ref, slope_ref, onehot_ref, edges_ref, low_ref)
    source = sums[:, :wide].astype(BF)
    target = sums[:, wide : wide + slab].astype(BF)
    ext_grad = mm(first_back[:latent], source)
    node_back = mm(node_first_back[...], pre_grad.astype(BF))
    gm = node_back[latent:].astype(BF)
    grad = back_in[...] + wide_mm(first_back[:latent], placed)
    back_ref[...] = (
        grad + node_back[:latent] + ext_grad[:, :slab] + mm(first_back[latent : 2 * latent], target)
    )
    alpha, beta = rim_gradients(ext_grad, slab, rim)
    node_one, node_two, node_pre_sum, grad_sum = node_sums(grad, pre_grad, joined_ref[...], node_hidden_ref[...])
    slab16 = slab_ref[...]
    ext16 = jnp.concatenate([slab16, rims_ref[...]], axis=1)
    edge_one = jnp.concatenate(
        [
            mm_nt(source, ext16) + mm_nt(placed.astype(BF), slab_one_ref[...]),
            mm_nt(target, slab16),
            sums[:, wide + slab :],
        ],
        axis=1,
    )
    edge_two = mm_nt(gm, sums_ref[...].astype(BF))
    pre_sum = sums[:, slab + 2 * rim : slab + 2 * rim + 1]
    gm_sum = jnp.sum(gm.astype(F32) * count_ref[0:1], axis=1, keepdims=True)
    total = total_in[...] + jnp.concatenate(
        [edge_one, edge_two, node_one, node_two, pre_sum, gm_sum, node_pre_sum, grad_sum], axis=1
    )
    even = is_even()
    half, used = keep_ref.shape
    keep_ref[...] = jnp.where(even, total[:half], total[half:])
    pieces = [jnp.where(even, total[half:], total[:half]), alpha[:half], alpha[half:], beta[:half], beta[half:]]
    spare = send_ref.shape[1] - used - 4 * rim
    if spare:
        pieces.append(jnp.zeros((half, spare), F32))
    send_ref[...] = jnp.concatenate(pieces, axis=1).astype(BF)


def open_kernel(rim, keep_ref, other_ref, out_ref):
    half, used = keep_ref.shape
    other = other_ref[...].astype(F32)
    pieces = [keep_ref[...] + other[:, :used], other[:, used + 2 * rim : used + 4 * rim]]
    spare = out_ref.shape[1] - used - 2 * rim
    if spare:
        pieces.append(jnp.zeros((half, spare), F32))
    out_ref[...] = jnp.concatenate(pieces, axis=1).astype(BF)


def add_kernel(used, rim, bit, mine_ref, other_ref, arrived_in, out_ref, arrived_ref):
    other = other_ref[...].astype(F32)
    place = lax.axis_index("phi")
    home = (lax.rem(place // bit, 2) == 1) == (lax.rem(place, 2) == 0)
    held = other[:, used : used + 2 * rim]
    arrived = jnp.where(home, held, 0.0)
    if arrived_in is not None:
        arrived = arrived + arrived_in[...]
    arrived_ref[...] = arrived
    lane = lax.broadcasted_iota(jnp.int32, other.shape, 1)
    mine = mine_ref[...].astype(F32)
    passing = jnp.where(home, 0.0, other)
    out_ref[...] = jnp.where(lane < used, mine + other, passing).astype(BF)


def first_add(kernel, mine_ref, other_ref, out_ref, arrived_ref):
    kernel(mine_ref, other_ref, None, out_ref, arrived_ref)


def close_kernel(mine_ref, other_ref, half_ref):
    half_ref[...] = (mine_ref[...].astype(F32) + other_ref[...].astype(F32)).astype(BF)


def rims_of(value, used, rim):
    return jnp.concatenate([value[:, used : used + rim], value[:, used + rim : used + 2 * rim]], axis=0)


def node_kernel(used, rim, first_ref, other_ref, arrived_ref, back_ref, upper_ref, lower_ref, node_grad):
    alpha = rims_of(first_ref[...].astype(F32), used, rim)
    beta = rims_of(other_ref[...].astype(F32), used, rim) + rims_of(arrived_ref[...], 0, rim)
    grad = back_ref[...] + placed_rims(alpha, beta, upper_ref, lower_ref)
    node_grad[...] = own_rows(grad.T, node_grad.shape[0])


def finish_kernel(used, half_ref, other_ref, edge_one, edge_two, node_one, node_two, bias_out):
    even = is_even()
    mine = half_ref[...].astype(F32)
    other = other_ref[...].astype(F32)
    total = jnp.concatenate([jnp.where(even, mine, other), jnp.where(even, other, mine)], axis=0)
    cut = 0
    for ref in (edge_one, edge_two, node_one, node_two):
        ref[...] = total[:, cut : cut + ref.shape[1]]
        cut += ref.shape[1]
    block = used - 4 - (used - 4) % LANES
    turned = total[:, block : block + LANES].T
    bias_out[...] = turned[used - 4 - block : used - block]


def call(kernel, outs, *args, scratch=(), smem=0, hbm=(), cost=1.0):
    args = [
        pltpu.with_memory_space_constraint(arg, HBM) if place in hbm else arg for place, arg in enumerate(args)
    ]
    held = [(arg.shape, arg.dtype) for arg in args] + list(outs)
    held += [(ref.shape, ref.dtype) for ref in scratch if jnp.issubdtype(ref.dtype, jnp.number)]
    room = sum(math.prod(shape) * jnp.dtype(kind).itemsize for shape, kind in held)
    spaces = [pltpu.SMEM if place < smem else HBM if place in hbm else VM for place in range(len(args))]
    specs = [pl.BlockSpec(memory_space=space) for space in spaces]
    return pl.pallas_call(
        kernel,
        out_shape=[jax.ShapeDtypeStruct(shape, kind) for shape, kind in outs],
        in_specs=specs,
        out_specs=[pl.BlockSpec(memory_space=VM) for _ in outs],
        scratch_shapes=list(scratch),
        compiler_params=pltpu.CompilerParams(vmem_limit_bytes=room + 10 * 1024 * 1024),
        cost_estimate=pl.CostEstimate(
            flops=int(cost * 1e9), bytes_accessed=int(cost * 3.6e6), transcendentals=0
        ),
    )(*args)


def swap(value, axis, pairing):
    count = lax.axis_size(axis)
    return lax.ppermute(value, axis, [(source, pairing(source) % count) for source in range(count)])


def by_alpha(value):
    return swap(value, "phi", lambda index: index ^ 1)


def by_beta(value):
    return swap(value, "phi", lambda index: index - 1 if index % 2 == 0 else index + 1)


def layer_parts(value):
    groups = lax.axis_size("layer")
    return [value] + [
        swap(value, "layer", lambda index, turn=turn: index + turn) for turn in range(1, groups)
    ]


def body(node_feats, edge_feats, edge_source, edge_target, edge_counts, rim_upper, rim_lower,
         edge_first, edge_second, node_first, node_second, biases, node_cot):
    groups = lax.axis_size("layer")
    ring = lax.axis_size("phi")
    latent, width = node_feats.shape
    hidden = edge_second.shape[1]
    slots = edge_feats.shape[1]
    slab = width * groups
    rim = rim_upper.shape[1]
    wide = (slab + 2 * rim) // LANES * LANES + LANES
    total_slots = slots * groups
    rows = slots // LANES
    room = wide - slab
    rim_shape = ((latent, room), BF)
    per_slot = lambda kind: ((latent, total_slots), kind)
    per_hit = lambda kind, depth=1: ((depth * latent, slab), kind)

    packed, upper, lower = call(
        prep_kernel,
        [((3 * rows + width, LANES), BF), ((1, rim), jnp.int32), ((1, rim), jnp.int32)],
        edge_counts, edge_source.reshape(rows, LANES), edge_target.reshape(rows, LANES),
        node_feats.T, node_cot.T, rim_upper, rim_lower,
        scratch=[VM((rows, LANES), jnp.int32), VM((rows, LANES), jnp.int32),
                 VM((width, latent), BF), VM((width, latent), F32), pltpu.SemaphoreType.DMA((6,))],
        smem=1, hbm=range(1, 7),
    )
    packs = layer_parts(packed)
    upper, lower, alpha_pick, beta_pick = call(
        pick_kernel,
        [((slab, rim), BF), ((slab, rim), BF), ((slab, room), BF), ((slab, room), BF)],
        packed, upper, lower, cost=0.1,
    )
    later, _ = lax.optimization_barrier((edge_feats, alpha_pick))
    parts = [edge_feats] + layer_parts(later)[1:]
    slab_zero, cot, alpha, beta = call(
        functools.partial(slab_kernel, groups, rows),
        [per_hit(BF), per_hit(F32), rim_shape, rim_shape], *packs, alpha_pick, beta_pick, cost=20.0,
    )
    beta = by_beta(beta)
    alpha = by_alpha(alpha)
    (onehot, base, count, table, first_back, second_back, node_first_back, node_second_back, bias,
     to_node, to_node_back, to_table, to_table_back, to_hidden, alpha_place, beta_place) = call(
        functools.partial(onehot_kernel, groups, rows, rim),
        [((wide + slab, total_slots), BF), per_slot(F32), ((8, slab), F32), per_hit(F32),
         (edge_first.shape[::-1], BF), (edge_second.shape[::-1], BF),
         (node_first.shape[::-1], BF), (node_second.shape[::-1], BF), (biases.shape[::-1], F32)]
        + [((hidden, 3 * hidden), BF)] * 5 + [((2 * slab, 2 * room), BF)] * 2,
        *packs, slab_zero, edge_first, edge_second, node_first, node_second, biases, alpha_pick, beta_pick, cost=2.0,
    )
    edges_zero, base, message, node_base_zero = call(
        functools.partial(start_kernel, groups),
        [per_slot(BF), per_slot(BF), per_hit(F32), per_hit(F32)],
        *parts, base, onehot, slab_zero, count, edge_first, node_first, bias, cost=1.0,
    )
    (hidden_zero, slope, rims_zero, sums_zero, node_pre_zero, node_hidden_zero, slab_one, table,
     alpha, beta) = call(
        forward_kernel,
        [per_slot(BF), per_slot(BF), rim_shape, per_hit(F32), per_hit(F32), per_hit(BF), per_hit(BF), per_hit(F32),
         ((latent, 2 * room), BF), ((latent, 2 * room), BF)],
        base, onehot, slab_zero, beta, alpha, node_base_zero, table, edge_first, node_second, bias, to_node, to_table,
        alpha_place, beta_place, cost=2.0,
    )
    beta = by_beta(beta)
    alpha = by_alpha(alpha)
    edges_one, base, message, joined_zero, node_base_one = call(
        between_kernel, [per_slot(BF), per_slot(BF), per_hit(F32), per_hit(BF, 2), per_hit(F32)],
        edges_zero, hidden_zero, onehot, slab_zero, slab_one, table, sums_zero, message, count,
        edge_first, edge_second, node_first, bias, cost=2.0,
    )
    total_width = edge_first.shape[1] + hidden + node_first.shape[1] + node_second.shape[1] + 4
    hidden_one, low, sums_one, node_pre_one, node_grad_one, wanted, first_sums, rims = call(
        middle_kernel,
        [per_slot(BF), per_slot(BF), per_hit(F32), per_hit(F32), per_hit(F32), per_hit(F32),
         ((hidden, wide + slab + latent), F32), rim_shape],
        base, onehot, edges_one, beta, alpha, node_base_one, cot, node_second_back, to_node, to_node_back,
        scratch=[VM((hidden, total_slots), BF)], cost=3.0,
    )
    beta = by_beta(rims)
    alpha = by_alpha(rims)
    extra, total, joined_one, back, back_node = call(
        functools.partial(carry_kernel, rim),
        [per_slot(BF), ((latent, total_width), F32), per_hit(BF, 2), per_hit(F32), per_hit(F32)],
        low, hidden_zero, slab_one, sums_one, sums_zero, message, node_pre_one, node_grad_one, first_sums, count, cot,
        edge_second, first_back, node_first_back, node_second_back, to_hidden, cost=2.0,
    )
    edge_out, node_out = call(
        output_kernel, [((latent, slots), BF), ((width, latent), BF)],
        edge_counts, edges_one, hidden_one, joined_one, node_pre_one, edge_second, node_second, bias,
        scratch=[VM((latent, total_slots), BF)], smem=1, cost=2.0,
    )
    half = hidden // 2
    up = lambda count: -(-count // LANES) * LANES
    keep, send, back = call(
        functools.partial(last_kernel, rim),
        [((half, total_width), F32), ((half, up(total_width + 4 * rim)), BF), per_hit(F32)],
        back, back_node, beta, alpha, alpha_pick, beta_pick, joined_zero, node_pre_zero, node_hidden_zero, wanted,
        sums_zero, count, extra, slope, onehot, edges_zero, slab_zero, rims_zero, slab_one, total,
        first_back, node_first_back, to_node_back, to_table_back,
        scratch=[VM((hidden, total_slots), BF)], cost=2.0,
    )
    first = by_alpha(send)
    width_now = up(total_width + 2 * rim)
    mine = call(
        functools.partial(open_kernel, rim), [((half, width_now), BF)], keep, first, cost=0.1,
    )[0]
    bit = 2
    arrived = None
    while True:
        other = swap(mine, "phi", lambda index, bit=bit: index ^ bit)
        if 2 * bit >= ring:
            break
        given = (mine, other) if arrived is None else (mine, other, arrived)
        kernel = functools.partial(add_kernel, total_width, rim, bit)
        if arrived is None:
            kernel = functools.partial(first_add, kernel)
        mine, arrived = call(kernel, [((half, width_now), BF), ((half, 2 * rim), F32)], *given, cost=0.1)
        bit *= 2
    mine = call(close_kernel, [((half, width_now), BF)], mine, other, cost=0.1)[0]
    whole = by_alpha(mine)
    node_grad = call(
        functools.partial(node_kernel, total_width, rim), [((width, latent), F32)],
        first, other, arrived, back, upper, lower, cost=1.0,
    )[0]
    edge_one, edge_two, node_one, node_two, bias_out = call(
        functools.partial(finish_kernel, total_width),
        [(edge_first.shape, F32), (edge_second.shape, F32), (node_first.shape, F32), (node_second.shape, F32),
         (biases.shape, F32)],
        mine, whole,
    )
    return node_out.T, edge_out, node_grad.T, edge_one, edge_two, node_one, node_two, bias_out


def solution(mesh):
    split = P(None, ("phi", "layer"))
    return jax.shard_map(
        body,
        mesh=mesh,
        in_specs=(split, split, P(("phi", "layer")), P(("phi", "layer")), P("phi", "layer"),
                  P("phi", None), P("phi", None), P(), P(), P(), P(), P(), split),
        out_specs=(split, split, split, P(), P(), P(), P(), P()),
        check_vma=False,
    )
```

```python
import functools
import math

import jax
import jax.numpy as jnp
from jax import lax
from jax.experimental import pallas as pl
from jax.experimental.pallas import tpu as pltpu
from jax.sharding import PartitionSpec as P

BF = jnp.bfloat16
F32 = jnp.float32
CHUNK = 512
LANES = 128
HBM = pltpu.HBM
VM = pltpu.VMEM


def mm(left, right):
    return jnp.dot(left, right, preferred_element_type=F32)


def mm_nt(left, right):
    return lax.dot_general(left, right, (((1,), (1,)), ((), ())), preferred_element_type=F32)


def flip(weight):
    return weight.astype(F32).T.astype(BF)


def halves(value):
    high = value.astype(BF)
    return high, (value - high.astype(F32)).astype(BF)


def wide_mm(weight, value):
    high, low = halves(value)
    return mm(jnp.concatenate([weight, weight], axis=1), jnp.concatenate([high, low], axis=0))


def sigmoid(value):
    return 0.5 + 0.5 * jnp.tanh(0.5 * value)


def add_to(total, value):
    return value if total is None else total + value


def chunks_of(count):
    return [slice(first, first + CHUNK) for first in range(0, count, CHUNK)]


def is_even():
    return lax.rem(lax.axis_index("phi"), 2) == 0


def lower_rows(ring):
    place = lax.axis_index("phi")
    total = place
    bit = 2
    while bit < ring:
        total = total + place // bit
        bit *= 2
    return lax.rem(total, 2) == 0


def pick(parts, natural):
    groups = len(parts)
    turn = lax.rem(lax.axis_index("layer") - natural + groups, groups)
    value = parts[0]
    for rank in range(1, groups):
        value = jnp.where(turn == rank, parts[rank], value)
    return value


def own_rows(slab_rows, width):
    layer = lax.axis_index("layer")
    value = slab_rows[:width]
    for rank in range(1, slab_rows.shape[0] // width):
        value = jnp.where(layer == rank, slab_rows[rank * width : (rank + 1) * width], value)
    return value


def split(value):
    high, low = halves(value)
    return jnp.concatenate([high, high, low], axis=1)


def split_mm(table, value):
    high, low = halves(value)
    return mm(table, jnp.concatenate([high, low, high], axis=0))


def pair_mm(table, value):
    return mm(table[:, value.shape[0] :], jnp.concatenate([value, value], axis=0))


def placed_rims(alpha, beta, upper_ref, lower_ref):
    even = is_even()
    from_upper = jnp.where(even, alpha, beta).astype(BF)
    from_lower = jnp.where(even, beta, alpha).astype(BF)
    return mm_nt(from_upper, upper_ref[...]) + mm_nt(from_lower, lower_ref[...])


def rim_gradients(ext_grad, slab, rim):
    even = is_even()
    below = ext_grad[:, slab : slab + rim]
    above = ext_grad[:, slab + rim : slab + 2 * rim]
    return jnp.where(even, above, below), jnp.where(even, below, above)


def slope_parts(pre):
    logistic = sigmoid(pre)
    value = pre * logistic
    return value, logistic + value * (1.0 - logistic)


def activate(base_ref, table, onehot_ref, slab, edges_ref, second_ref, bias, hidden_ref, slope_ref, new_ref):
    wide = onehot_ref.shape[0] - slab
    second = second_ref[...]
    latent = second.shape[0]
    same = lax.broadcasted_iota(jnp.int32, (latent, latent), 0) == lax.broadcasted_iota(
        jnp.int32, (latent, latent), 1
    )
    update = jnp.concatenate([second.astype(F32), same.astype(F32)], axis=1).astype(BF)
    for cols in chunks_of(base_ref.shape[1]):
        rims = onehot_ref[slab:wide, cols]
        slope_ref[:, cols] = base_ref[:, cols] + mm(table, jnp.concatenate([rims, rims], axis=0))
    for cols in chunks_of(base_ref.shape[1]):
        value, slope = slope_parts(slope_ref[:, cols])
        hidden_ref[:, cols] = value.astype(BF)
        slope_ref[:, cols] = slope
    for cols in chunks_of(base_ref.shape[1]):
        both = jnp.concatenate([hidden_ref[:, cols], edges_ref[:, cols]], axis=0)
        new_ref[:, cols] = (mm(update, both) + bias[:, 1:2]).astype(BF)
    return mm_nt(new_ref[...], onehot_ref[wide:])


def slab_base(source, target, own, bias, onehot_ref, edges_ref, base_ref):
    slab = source.shape[1]
    wide = onehot_ref.shape[0] - slab
    table = jnp.concatenate([*halves(source), *halves(target), own], axis=1)
    for cols in chunks_of(base_ref.shape[1]):
        near = onehot_ref[:slab, cols]
        hit = onehot_ref[wide:, cols]
        stack = jnp.concatenate([near, near, hit, hit, edges_ref[:, cols]], axis=0)
        base_ref[:, cols] = mm(table, stack) + bias[:, 0:1]


def node_sums(grad, pre_grad, joined, hidden):
    return (
        mm_nt(pre_grad.astype(BF), joined),
        mm_nt(grad.astype(BF), hidden),
        jnp.sum(pre_grad, axis=1, keepdims=True),
        jnp.sum(grad, axis=1, keepdims=True),
    )


def prep_kernel(count_ref, source_hbm, target_hbm, feats_hbm, cot_hbm, upper_hbm, lower_hbm,
                out_ref, upper_ref, lower_ref, source, target, feats, cot, sems):
    pairs = ((source_hbm, source), (target_hbm, target), (feats_hbm, feats), (cot_hbm, cot),
             (upper_hbm, upper_ref), (lower_hbm, lower_ref))
    copies = [pltpu.make_async_copy(a, b, sems.at[place]) for place, (a, b) in enumerate(pairs)]
    for copy in copies:
        copy.start()
    for copy in copies:
        copy.wait()
    rows = source.shape[0]
    position = lax.broadcasted_iota(jnp.int32, (rows, LANES), 0) * LANES + lax.broadcasted_iota(
        jnp.int32, (rows, LANES), 1
    )
    valid = position < count_ref[0, 0]
    index = source[...]
    out_ref[:rows] = jnp.where(valid, index // LANES, -1).astype(F32).astype(BF)
    out_ref[rows : 2 * rows] = (index % LANES).astype(F32).astype(BF)
    out_ref[2 * rows : 3 * rows] = jnp.where(valid, target[...], -1).astype(F32).astype(BF)
    out_ref[3 * rows :] = jnp.concatenate([feats[...].astype(F32), cot[...]], axis=1).astype(BF)


def pick_kernel(packed_ref, upper, lower, upper_ref, lower_ref, alpha_pick, beta_pick):
    hits = lax.broadcasted_iota(jnp.int32, upper_ref.shape, 0)
    upper_ref[...] = (hits == upper[...]).astype(F32).astype(BF)
    lower_ref[...] = (hits == lower[...]).astype(F32).astype(BF)
    slab, room = alpha_pick.shape
    rim = upper.shape[1]
    first = jnp.concatenate([upper[...], jnp.full((1, room - rim), -1, jnp.int32)], axis=1)
    second = jnp.concatenate(
        [jnp.full((1, rim), -1, jnp.int32), lower[...], jnp.full((1, room - 2 * rim), -1, jnp.int32)], axis=1
    )
    even = is_even()
    hits = lax.broadcasted_iota(jnp.int32, (slab, room), 0)
    alpha_pick[...] = (hits == jnp.where(even, first, second)).astype(F32).astype(BF)
    beta_pick[...] = (hits == jnp.where(even, second, first)).astype(F32).astype(BF)


def slab_kernel(groups, rows, *refs):
    packs = [ref[3 * rows :].astype(F32) for ref in refs[:groups]]
    alpha_pick, beta_pick, slab_ref, cot_ref, alpha_ref, beta_ref = refs[groups:]
    latent = slab_ref.shape[0]
    both = jnp.concatenate([pick(packs, rank) for rank in range(groups)], axis=0).T
    slab16 = both[:latent].astype(BF)
    slab_ref[...] = slab16
    cot_ref[...] = both[latent:]
    alpha_ref[...] = mm(slab16, alpha_pick[...]).astype(BF)
    beta_ref[...] = mm(slab16, beta_pick[...]).astype(BF)


def onehot_kernel(groups, rows, rim, *refs):
    packs = [ref[: 3 * rows].astype(F32) for ref in refs[:groups]]
    (slab_ref, first_ref, second_ref, node_first_ref, node_second_ref, bias_ref, alpha_pick, beta_pick,
     onehot_ref, base_ref, count_ref, first_back, second_back, node_first_back, node_second_back, bias_out,
     to_node_back, to_table_back, to_hidden, alpha_place, beta_place) = refs[groups:]
    latent = first_ref.shape[0]
    slab, room = alpha_pick.shape
    wide = slab + room
    source_rows = lax.broadcasted_iota(jnp.int32, (wide, LANES), 0).astype(F32)
    target_rows = lax.broadcasted_iota(jnp.int32, (slab, LANES), 0).astype(F32)
    ones_row = source_rows == float(slab + 2 * rim)
    for rank in range(groups):
        pack = pick(packs, rank)
        source = jnp.where(pack[:rows] < 0.0, -1.0, pack[:rows] * LANES + pack[rows : 2 * rows])
        target = pack[2 * rows :]
        for row in range(rows):
            cols = slice((rank * rows + row) * LANES, (rank * rows + row + 1) * LANES)
            match = (source_rows == source[row : row + 1]) | ones_row
            onehot_ref[:wide, cols] = jnp.where(match, 1.0, 0.0).astype(BF)
            onehot_ref[wide:, cols] = jnp.where(target_rows == target[row : row + 1], 1.0, 0.0).astype(BF)
    bias = bias_ref[...].T
    bias_out[...] = bias
    slab16 = slab_ref[...]
    source = mm(first_ref[:, :latent], slab16)
    target = mm(first_ref[:, latent : 2 * latent], slab16)
    table = jnp.concatenate([*halves(source), *halves(target)], axis=1)
    count = None
    for cols in chunks_of(base_ref.shape[1]):
        near = onehot_ref[:slab, cols]
        hit = onehot_ref[wide:, cols]
        base_ref[:, cols] = mm(table, jnp.concatenate([near, near, hit, hit], axis=0)) + bias[:, 0:1]
        count = add_to(count, mm_nt(jnp.ones((16, CHUNK), BF), hit))
    count_ref[...] = count[:8]
    first_back[...] = flip(first_ref[...])
    second_back[...] = flip(second_ref[...])
    node_first_back[...] = flip(node_first_ref[...])
    node_second_back[...] = flip(node_second_ref[...])
    forward = mm(node_first_ref[:, latent:], second_ref[...])
    to_node_back[...] = split(forward.T)
    table = mm(first_ref[:, :latent], node_second_ref[...])
    to_table_back[...] = split(table.T)
    to_hidden[...] = split(mm(first_ref[:, 2 * latent :], second_ref[...]).T)
    for choose, place in ((alpha_pick, alpha_place), (beta_pick, beta_place)):
        block = choose[...].astype(F32)
        none = jnp.zeros_like(block)
        place[...] = jnp.concatenate(
            [jnp.concatenate([block, none], axis=1), jnp.concatenate([none, block], axis=1)], axis=0
        ).astype(BF)


def start_kernel(groups, *refs):
    parts = refs[:groups]
    base_in, first_ref, edges_ref, base_ref = refs[groups:]
    latent = first_ref.shape[1] // 3
    slots = parts[0].shape[1]
    own = first_ref[:, 2 * latent :]
    for rank in range(groups):
        for cols in chunks_of(slots):
            here = slice(rank * slots + cols.start, rank * slots + cols.stop)
            edges = pick([part[:, cols] for part in parts], rank)
            edges_ref[:, here] = edges
            base_ref[:, here] = base_in[:, here] + mm(own, edges)


def node_forward(slab16, message, node_first_ref, bias):
    joined = jnp.concatenate([slab16, message.astype(BF)], axis=0)
    return joined, mm(node_first_ref[...], joined) + bias[:, 2:3]


def forward_kernel(base_ref, onehot_ref, edges_ref, slab_ref, beta_in, alpha_in,
                   first_ref, second_ref, node_first_ref, node_second_ref, bias_ref, alpha_place, beta_place,
                   hidden_ref, slope_ref, new_ref, rims_ref, joined_ref, node_pre_ref, node_hidden_ref, state_ref,
                   table_ref, alpha_ref, beta_ref):
    latent, slab = slab_ref.shape
    rims16 = alpha_in[...] + beta_in[...]
    rims_ref[...] = rims16
    bias = bias_ref[...]
    table = jnp.concatenate(halves(mm(first_ref[:, :latent], rims16)), axis=1)
    message = activate(
        base_ref, table, onehot_ref, slab, edges_ref, second_ref, bias, hidden_ref, slope_ref, new_ref
    )
    slab16 = slab_ref[...]
    joined, node_pre = node_forward(slab16, message, node_first_ref, bias)
    joined_ref[...] = joined
    node_pre_ref[...] = node_pre
    node_hidden = slope_parts(node_pre)[0].astype(BF)
    node_hidden_ref[...] = node_hidden
    state = (slab16.astype(F32) + mm(node_second_ref[...], node_hidden) + bias[:, 3:4]).astype(BF)
    state_ref[...] = state
    table = mm(first_ref[:, :latent], state)
    table_ref[...] = table
    both = jnp.concatenate(halves(table), axis=1)
    alpha_ref[...] = mm(both, alpha_place[...]).astype(BF)
    beta_ref[...] = mm(both, beta_place[...]).astype(BF)


def between_kernel(edges_ref, hidden_ref, onehot_ref, state_ref, table_ref, first_ref, bias_ref, base_ref, sums_ref):
    latent, slab = state_ref.shape
    wide = onehot_ref.shape[0] - slab
    target = mm(first_ref[:, latent : 2 * latent], state_ref[...])
    slab_base(
        table_ref[...], target, first_ref[:, 2 * latent :], bias_ref[...], onehot_ref, edges_ref, base_ref
    )
    sums_ref[...] = mm_nt(hidden_ref[...], onehot_ref[wide:])


def edge_gradient(wanted, extra_ref, slope_ref, onehot_ref, edges_ref, low_ref):
    slab = wanted.shape[1]
    wide = onehot_ref.shape[0] - slab
    table = wanted.astype(BF)
    for cols in chunks_of(edges_ref.shape[1]):
        grad = mm(table, onehot_ref[wide:, cols])
        if extra_ref is not None:
            grad = grad + extra_ref[:, cols]
        low_ref[:, cols] = (grad * slope_ref[:, cols]).astype(BF)
    return mm_nt(low_ref[...], jnp.concatenate([onehot_ref[...], edges_ref[...]], axis=0))


def middle_kernel(base_ref, onehot_ref, edges_ref, slab_ref, beta_in, alpha_in, cot_ref,
                  second_ref, node_first_ref, bias_ref, node_second_back, to_node_back,
                  hidden_ref, new_ref, low_ref, joined_ref, node_pre_ref, node_grad_ref, wanted_ref, first_sums_ref,
                  rims_ref, slope_ref):
    slab = cot_ref.shape[1]
    wide = onehot_ref.shape[0] - slab
    bias = bias_ref[...]
    cot_grad = mm(node_second_back[...], cot_ref[...].astype(BF))
    message = activate(
        base_ref, alpha_in[...] + beta_in[...], onehot_ref, slab, edges_ref, second_ref, bias, hidden_ref,
        slope_ref, new_ref,
    )
    joined, node_pre = node_forward(slab_ref[...], message, node_first_ref, bias)
    joined_ref[...] = joined
    node_pre_ref[...] = node_pre
    pre_grad = cot_grad * slope_parts(node_pre)[1]
    node_grad_ref[...] = pre_grad
    wanted = pair_mm(to_node_back[...], pre_grad.astype(BF))
    wanted_ref[...] = wanted
    first_sums = edge_gradient(wanted, None, slope_ref, onehot_ref, edges_ref, low_ref)
    rims_ref[...] = first_sums[:, slab:wide].astype(BF)
    first_sums_ref[...] = first_sums


def carry_kernel(rim, low_ref, hidden_zero_ref, hidden_ref, onehot_ref, slab_ref, sums_zero_ref, joined_ref,
                 node_pre_ref, node_grad_ref, first_sums_ref, count_ref, cot_ref,
                 first_back, node_first_back, node_second_back, to_hidden,
                 extra_ref, total_ref, back_ref, back_node_ref):
    latent, slab = slab_ref.shape
    wide = first_sums_ref.shape[1] - slab - latent
    sums = first_sums_ref[...]
    cot = cot_ref[...]
    pre_grad = node_grad_ref[...]
    node_back = mm(node_first_back[...], pre_grad.astype(BF))
    gm = node_back[latent:].astype(BF)
    source = sums[:, :slab].astype(BF)
    target = sums[:, wide : wide + slab].astype(BF)
    back = cot + node_back[:latent] + mm(first_back[:latent], source) + mm(first_back[latent : 2 * latent], target)
    back_ref[...] = back
    back_node_ref[...] = wide_mm(node_second_back[...], back)
    self_back = first_back[2 * latent :]
    cross = None
    for cols in chunks_of(low_ref.shape[1]):
        low = low_ref[:, cols]
        extra_ref[:, cols] = pair_mm(to_hidden[...], low)
        cross = add_to(cross, mm_nt(low, hidden_zero_ref[:, cols]))
    slab16 = slab_ref[...]
    joined = joined_ref[...]
    hidden_sums = mm_nt(hidden_ref[...], onehot_ref[wide:])
    pre_sum = sums[:, slab + 2 * rim : slab + 2 * rim + 1]
    edge_two = (
        mm_nt(gm, hidden_sums.astype(BF))
        + mm_nt(gm, sums_zero_ref[...].astype(BF))
        + mm(self_back, cross.astype(BF))
    )
    gm_sum = 2.0 * jnp.sum(gm.astype(F32) * count_ref[0:1], axis=1, keepdims=True) + wide_mm(
        self_back, jnp.broadcast_to(pre_sum, (latent, LANES))
    )[:, :1]
    node_one, node_two, node_pre_sum, cot_sum = node_sums(
        cot, pre_grad, joined, slope_parts(node_pre_ref[...])[0].astype(BF)
    )
    edge_one = jnp.concatenate(
        [mm_nt(source, slab16), mm_nt(target, slab16), sums[:, wide + slab :]], axis=1
    )
    total_ref[...] = jnp.concatenate(
        [edge_one, edge_two, node_one, node_two, pre_sum, gm_sum, node_pre_sum, cot_sum], axis=1
    )


def output_kernel(count_ref, new_ref, joined_ref, node_pre_ref, node_second_ref, bias_ref,
                  edge_out, node_out):
    bias = bias_ref[...]
    latent = new_ref.shape[0]
    slots = edge_out.shape[1]
    begin = lax.axis_index("layer") * slots
    for cols in chunks_of(slots):
        position = lax.broadcasted_iota(jnp.int32, (latent, CHUNK), 1) + cols.start
        mine = new_ref[:, pl.ds(pl.multiple_of(begin + cols.start, CHUNK), CHUNK)].astype(F32)
        edge_out[:, cols] = jnp.where(position < count_ref[0, 0], mine, 0.0).astype(BF)
    node_hidden = slope_parts(node_pre_ref[...])[0].astype(BF)
    state = joined_ref[:latent].astype(F32) + mm(node_second_ref[...], node_hidden) + bias[:, 3:4]
    node_out[...] = own_rows(state.T, node_out.shape[0]).astype(BF)


def last_kernel(rim, ring, back_in, back_node, beta_in, alpha_in, alpha_pick, beta_pick, joined_ref, node_pre_ref,
                node_hidden_ref, wanted_in, sums_ref, count_ref, extra_ref, slope_ref, onehot_ref, edges_ref,
                slab_ref, rims_ref, slab_one_ref, total_in, first_back, node_first_back, to_node_back, to_table_back,
                keep_ref, send_ref, back_ref, low_ref):
    latent, slab = slab_ref.shape
    wide = onehot_ref.shape[0] - slab
    placed = mm_nt(alpha_in[...], alpha_pick[...]) + mm_nt(beta_in[...], beta_pick[...])
    pre_grad = (back_node[...] + pair_mm(to_table_back[...], placed.astype(BF))) * slope_parts(node_pre_ref[...])[1]
    wanted = wanted_in[...] + pair_mm(to_node_back[...], pre_grad.astype(BF))
    sums = edge_gradient(wanted, extra_ref, slope_ref, onehot_ref, edges_ref, low_ref)
    source = sums[:, :wide].astype(BF)
    target = sums[:, wide : wide + slab].astype(BF)
    ext_grad = mm(first_back[:latent], source)
    node_back = mm(node_first_back[...], pre_grad.astype(BF))
    gm = node_back[latent:].astype(BF)
    grad = back_in[...] + wide_mm(first_back[:latent], placed)
    back_ref[...] = (
        grad + node_back[:latent] + ext_grad[:, :slab] + mm(first_back[latent : 2 * latent], target)
    )
    alpha, beta = rim_gradients(ext_grad, slab, rim)
    node_one, node_two, node_pre_sum, grad_sum = node_sums(grad, pre_grad, joined_ref[...], node_hidden_ref[...])
    slab16 = slab_ref[...]
    ext16 = jnp.concatenate([slab16, rims_ref[...]], axis=1)
    edge_one = jnp.concatenate(
        [
            mm_nt(source, ext16) + mm_nt(placed.astype(BF), slab_one_ref[...]),
            mm_nt(target, slab16),
            sums[:, wide + slab :],
        ],
        axis=1,
    )
    edge_two = mm_nt(gm, sums_ref[...].astype(BF))
    pre_sum = sums[:, slab + 2 * rim : slab + 2 * rim + 1]
    gm_sum = jnp.sum(gm.astype(F32) * count_ref[0:1], axis=1, keepdims=True)
    total = total_in[...] + jnp.concatenate(
        [edge_one, edge_two, node_one, node_two, pre_sum, gm_sum, node_pre_sum, grad_sum], axis=1
    )
    lower = lower_rows(ring)
    half, used = keep_ref.shape
    keep_ref[...] = jnp.where(lower, total[:half], total[half:])
    pieces = [jnp.where(lower, total[half:], total[:half]), alpha[:half], alpha[half:], beta[:half], beta[half:]]
    spare = send_ref.shape[1] - used - 4 * rim
    if spare:
        pieces.append(jnp.zeros((half, spare), F32))
    send_ref[...] = jnp.concatenate(pieces, axis=1).astype(BF)


def open_kernel(rim, keep_ref, other_ref, out_ref):
    half, used = keep_ref.shape
    other = other_ref[...].astype(F32)
    pieces = [keep_ref[...] + other[:, :used], other[:, used + 2 * rim : used + 4 * rim]]
    spare = out_ref.shape[1] - used - 2 * rim
    if spare:
        pieces.append(jnp.zeros((half, spare), F32))
    out_ref[...] = jnp.concatenate(pieces, axis=1).astype(BF)


def add_kernel(used, rim, bit, turn, mine_ref, other_ref, out_ref, arrived_ref):
    other = other_ref[...].astype(F32)
    place = lax.axis_index("phi")
    upward = lax.rem(place, 2) == turn % 2
    home = (lax.rem(place // bit, 2) == 1) == upward
    arrived_ref[...] = jnp.where(home, other[:, used : used + 2 * rim], 0.0)
    lane = lax.broadcasted_iota(jnp.int32, other.shape, 1)
    mine = mine_ref[...].astype(F32)
    passing = jnp.where(home, 0.0, other)
    out_ref[...] = jnp.where(lane < used, mine + other, passing).astype(BF)


def close_kernel(used, rim, turns, mine_ref, other_ref, *refs):
    mine = mine_ref[...].astype(F32)
    other = other_ref[...].astype(F32)
    arrived = [ref[...] for ref in refs[:-2]] + [other[:, used : used + 2 * rim]]
    half_ref, stay_ref = refs[-2:]
    crossed = sum(arrived[2::2], arrived[0])
    stay = sum(arrived[3::2], arrived[1])
    stay_ref[...] = stay
    pieces = [(mine + other)[:, :used], crossed]
    spare = half_ref.shape[1] - used - 2 * rim
    if spare:
        pieces.append(jnp.zeros((mine.shape[0], spare), F32))
    half_ref[...] = jnp.concatenate(pieces, axis=1)


def rims_of(value, used, rim):
    return jnp.concatenate([value[:, used : used + rim], value[:, used + rim : used + 2 * rim]], axis=0)


def finish_kernel(used, rim, ring, half_ref, other_ref, stay_ref, first_ref, back_ref, upper_ref, lower_ref,
                  node_grad, edge_one, edge_two, node_one, node_two, bias_out):
    lower = lower_rows(ring)
    mine = half_ref[...]
    other = other_ref[...]
    total = jnp.concatenate([jnp.where(lower, mine, other), jnp.where(lower, other, mine)], axis=0)
    cut = 0
    for ref in (edge_one, edge_two, node_one, node_two):
        ref[...] = total[:, cut : cut + ref.shape[1]]
        cut += ref.shape[1]
    block = used - 4 - (used - 4) % LANES
    turned = total[:, block : block + LANES].T
    bias_out[...] = turned[used - 4 - block : used - block]
    alpha = rims_of(first_ref[...].astype(F32), used, rim)
    beta = rims_of(other, used, rim) + rims_of(stay_ref[...], 0, rim)
    grad = back_ref[...] + placed_rims(alpha, beta, upper_ref, lower_ref)
    node_grad[...] = own_rows(grad.T, node_grad.shape[0])


def call(kernel, outs, *args, scratch=(), smem=0, hbm=(), cost=1.0):
    args = [
        pltpu.with_memory_space_constraint(arg, HBM) if place in hbm else arg for place, arg in enumerate(args)
    ]
    held = [(arg.shape, arg.dtype) for arg in args] + list(outs)
    held += [(ref.shape, ref.dtype) for ref in scratch if jnp.issubdtype(ref.dtype, jnp.number)]
    room = sum(math.prod(shape) * jnp.dtype(kind).itemsize for shape, kind in held)
    spaces = [pltpu.SMEM if place < smem else HBM if place in hbm else VM for place in range(len(args))]
    specs = [pl.BlockSpec(memory_space=space) for space in spaces]
    return pl.pallas_call(
        kernel,
        out_shape=[jax.ShapeDtypeStruct(shape, kind) for shape, kind in outs],
        in_specs=specs,
        out_specs=[pl.BlockSpec(memory_space=VM) for _ in outs],
        scratch_shapes=list(scratch),
        compiler_params=pltpu.CompilerParams(vmem_limit_bytes=room + 10 * 1024 * 1024),
        cost_estimate=pl.CostEstimate(
            flops=int(cost * 1e9), bytes_accessed=int(cost * 3.6e6), transcendentals=0
        ),
    )(*args)


def swap(value, axis, pairing):
    count = lax.axis_size(axis)
    return lax.ppermute(value, axis, [(source, pairing(source) % count) for source in range(count)])


def by_alpha(value):
    return swap(value, "phi", lambda index: index ^ 1)


def by_beta(value):
    return swap(value, "phi", lambda index: index - 1 if index % 2 == 0 else index + 1)


def layer_parts(value):
    groups = lax.axis_size("layer")
    return [value] + [
        swap(value, "layer", lambda index, turn=turn: index + turn) for turn in range(1, groups)
    ]


def body(node_feats, edge_feats, edge_source, edge_target, edge_counts, rim_upper, rim_lower,
         edge_first, edge_second, node_first, node_second, biases, node_cot):
    groups = lax.axis_size("layer")
    ring = lax.axis_size("phi")
    latent, width = node_feats.shape
    hidden = edge_second.shape[1]
    slots = edge_feats.shape[1]
    slab = width * groups
    rim = rim_upper.shape[1]
    wide = (slab + 2 * rim) // LANES * LANES + LANES
    total_slots = slots * groups
    rows = slots // LANES
    room = wide - slab
    rim_shape = ((latent, room), BF)
    per_slot = lambda kind: ((latent, total_slots), kind)
    per_hit = lambda kind, depth=1: ((depth * latent, slab), kind)

    packed, upper, lower = call(
        prep_kernel,
        [((3 * rows + width, LANES), BF), ((1, rim), jnp.int32), ((1, rim), jnp.int32)],
        edge_counts, edge_source.reshape(rows, LANES), edge_target.reshape(rows, LANES),
        node_feats.T, node_cot.T, rim_upper, rim_lower,
        scratch=[VM((rows, LANES), jnp.int32), VM((rows, LANES), jnp.int32),
                 VM((width, latent), BF), VM((width, latent), F32), pltpu.SemaphoreType.DMA((6,))],
        smem=1, hbm=range(1, 7),
    )
    packs = layer_parts(packed)
    upper, lower, alpha_pick, beta_pick = call(
        pick_kernel,
        [((slab, rim), BF), ((slab, rim), BF), ((slab, room), BF), ((slab, room), BF)],
        packed, upper, lower, cost=0.1,
    )
    later, _ = lax.optimization_barrier((edge_feats, alpha_pick))
    parts = [edge_feats] + layer_parts(later)[1:]
    slab_zero, cot, alpha, beta = call(
        functools.partial(slab_kernel, groups, rows),
        [per_hit(BF), per_hit(F32), rim_shape, rim_shape], *packs, alpha_pick, beta_pick, cost=20.0,
    )
    beta = by_beta(beta)
    alpha = by_alpha(alpha)
    (onehot, base, count, first_back, second_back, node_first_back, node_second_back, bias,
     to_node_back, to_table_back, to_hidden, alpha_place, beta_place) = call(
        functools.partial(onehot_kernel, groups, rows, rim),
        [((wide + slab, total_slots), BF), per_slot(F32), ((8, slab), F32),
         (edge_first.shape[::-1], BF), (edge_second.shape[::-1], BF),
         (node_first.shape[::-1], BF), (node_second.shape[::-1], BF), (biases.shape[::-1], F32)]
        + [((hidden, 3 * hidden), BF)] * 3 + [((2 * slab, 2 * room), BF)] * 2,
        *packs, slab_zero, edge_first, edge_second, node_first, node_second, biases, alpha_pick, beta_pick, cost=2.0,
    )
    edges_zero, base = call(
        functools.partial(start_kernel, groups), [per_slot(BF), per_slot(F32)], *parts, base, edge_first, cost=1.0,
    )
    (hidden_zero, slope, edges_one, rims_zero, joined_zero, node_pre_zero, node_hidden_zero, slab_one, table,
     alpha, beta) = call(
        forward_kernel,
        [per_slot(BF), per_slot(F32), per_slot(BF), rim_shape, per_hit(BF, 2), per_hit(F32), per_hit(BF), per_hit(BF),
         per_hit(F32), ((latent, 2 * room), BF), ((latent, 2 * room), BF)],
        base, onehot, edges_zero, slab_zero, beta, alpha, edge_first, edge_second, node_first, node_second, bias,
        alpha_place, beta_place, cost=2.0,
    )
    beta = by_beta(beta)
    alpha = by_alpha(alpha)
    base, sums_zero = call(
        between_kernel, [per_slot(F32), per_hit(F32)],
        edges_one, hidden_zero, onehot, slab_one, table, edge_first, bias, cost=2.0,
    )
    total_width = edge_first.shape[1] + hidden + node_first.shape[1] + node_second.shape[1] + 4
    hidden_one, edges_two, low, joined_one, node_pre_one, node_grad_one, wanted, first_sums, rims = call(
        middle_kernel,
        [per_slot(BF), per_slot(BF), per_slot(BF), per_hit(BF, 2), per_hit(F32), per_hit(F32), per_hit(F32),
         ((hidden, wide + slab + latent), F32), rim_shape],
        base, onehot, edges_one, slab_one, beta, alpha, cot, edge_second, node_first, bias, node_second_back,
        to_node_back, scratch=[VM((hidden, total_slots), F32)], cost=3.0,
    )
    beta = by_beta(rims)
    alpha = by_alpha(rims)
    extra, total, back, back_node = call(
        functools.partial(carry_kernel, rim),
        [per_slot(F32), ((latent, total_width), F32), per_hit(F32), per_hit(F32)],
        low, hidden_zero, hidden_one, onehot, slab_one, sums_zero, joined_one, node_pre_one, node_grad_one, first_sums,
        count, cot, first_back, node_first_back, node_second_back, to_hidden, cost=2.0,
    )
    edge_out, node_out = call(
        output_kernel, [((latent, slots), BF), ((width, latent), BF)],
        edge_counts, edges_two, joined_one, node_pre_one, node_second, bias, smem=1, cost=2.0,
    )
    half = hidden // 2
    up = lambda count: -(-count // LANES) * LANES
    keep, send, back = call(
        functools.partial(last_kernel, rim, ring),
        [((half, total_width), F32), ((half, up(total_width + 4 * rim)), BF), per_hit(F32)],
        back, back_node, beta, alpha, alpha_pick, beta_pick, joined_zero, node_pre_zero, node_hidden_zero, wanted,
        sums_zero, count, extra, slope, onehot, edges_zero, slab_zero, rims_zero, slab_one, total,
        first_back, node_first_back, to_node_back, to_table_back,
        scratch=[VM((hidden, total_slots), BF)], cost=2.0,
    )
    first = by_alpha(send)
    width_now = up(total_width + 2 * rim)
    mine = call(
        functools.partial(open_kernel, rim), [((half, width_now), BF)], keep, first, cost=0.1,
    )[0]
    arrived = []
    bit = 2
    turn = 1
    while True:
        other = swap(mine, "phi", lambda index, bit=bit: index ^ (bit + 1))
        if 2 * bit >= ring:
            break
        mine, block = call(
            functools.partial(add_kernel, total_width, rim, bit, turn),
            [((half, width_now), BF), ((half, 2 * rim), F32)], mine, other, cost=0.1,
        )
        arrived.append(block)
        bit *= 2
        turn += 1
    mine, stay = call(
        functools.partial(close_kernel, total_width, rim, turn),
        [((half, width_now), F32), ((half, 2 * rim), F32)], mine, other, *arrived, cost=0.1,
    )
    whole = by_alpha(mine)
    node_grad, edge_one, edge_two, node_one, node_two, bias_out = call(
        functools.partial(finish_kernel, total_width, rim, ring),
        [((width, latent), F32), (edge_first.shape, F32), (edge_second.shape, F32), (node_first.shape, F32),
         (node_second.shape, F32), (biases.shape, F32)],
        mine, whole, stay, first, back, upper, lower,
    )
    return node_out.T, edge_out, node_grad.T, edge_one, edge_two, node_one, node_two, bias_out


def solution(mesh):
    split = P(None, ("phi", "layer"))
    return jax.shard_map(
        body,
        mesh=mesh,
        in_specs=(split, split, P(("phi", "layer")), P(("phi", "layer")), P("phi", "layer"),
                  P("phi", None), P("phi", None), P(), P(), P(), P(), P(), split),
        out_specs=(split, split, split, P(), P(), P(), P(), P()),
        check_vma=False,
    )
```
